32 devices in a mesh: dp: 16 (over z, y, core), mp: 2 (over x).
Axes of the slice: x: 2, y: 2, z: 4, core: 2. Of those that a mesh axis runs over, the one named last changes fastest.
Arguments:
- latents: bfloat16 [16, 5, 16, 16, 1024], P('dp', None, 'mp'), may hold values from -6 to 6
- cotangent: bfloat16 [16, 5, 16, 16, 1024], P('dp', None, 'mp'), may hold values from -6 to 6
- frame_counts: int32 [16], P('dp'), may hold values from 2 to 5
- band_ids: int32 [16], replicated, may hold values from 0 to 31
- class_ids: int32 [16], replicated, may hold values from 0 to 100
- time_table: bfloat16 [32, 1024], replicated, may hold values from -6 to 6
- class_table: bfloat16 [101, 1024], replicated, may hold values from -6 to 6
- ada_weight: bfloat16 [2, 1024, 6144], P(None, None, ('dp', 'mp')), may hold values from -0.1875 to 0.1875, as said below
- ada_bias: bfloat16 [2, 6144], P(None, ('dp', 'mp')), may hold values from -3 to 3
- qkv_weight: bfloat16 [2, 1024, 3, 1024], P(None, 'dp', None, 'mp'), may hold values from -0.1875 to 0.1875
- out_weight: bfloat16 [2, 1024, 1024], P(None, 'mp', 'dp'), may hold values from -0.75 to 0.75
- up_weight: bfloat16 [2, 1024, 4096], P(None, 'dp', 'mp'), may hold values from -0.1875 to 0.1875
- down_weight: bfloat16 [2, 4096, 1024], P(None, 'mp', 'dp'), may hold values from -0.09375 to 0.09375
- spatial_bias: bfloat16 [16, 961], P('mp'), may hold values from -3 to 3
- joint_bias: bfloat16 [16, 2025], P('mp'), may hold values from -3 to 3
Outputs:
- mixed_output: float32 [16, 5, 16, 16, 1024], P('dp', None, 'mp')
- grad_latents: float32 [16, 5, 16, 16, 1024], P('dp', None, 'mp')
- grad_time_table: float32 [32, 1024], replicated
- grad_class_table: float32 [101, 1024], replicated
- grad_ada_weight: float32 [2, 1024, 6144], P(None, None, ('dp', 'mp'))
- grad_ada_bias: float32 [2, 6144], P(None, ('dp', 'mp'))
- grad_qkv_weight: float32 [2, 1024, 3, 1024], P(None, 'dp', None, 'mp')
- grad_out_weight: float32 [2, 1024, 1024], P(None, 'mp', 'dp')
- grad_up_weight: float32 [2, 1024, 4096], P(None, 'dp', 'mp')
- grad_down_weight: float32 [2, 4096, 1024], P(None, 'mp', 'dp')
- grad_spatial_bias: float32 [16, 961], P('mp')
- grad_joint_bias: float32 [16, 2025], P('mp')
The draws below stay inside these ranges and needn't reach their ends.
Inputs may be any that keep to these rules, and one draw needn't show every extreme that they name: `ada_weight`: entries of the modulation map, of mean zero.
All inputs are finite; a program needn't handle non-finite values.
Results may differ from the reference program's by a relative error of at most 0.034.
Values may be sent and summed in bfloat16 or wider, within the bound.
No kernel may reach another device: no remote copies, remote signals or barrier semaphores. Data moves between devices by JAX's collectives and lax.ppermute only.
A program may use at most 320 MiB of HBM per device.

```python
import jax
import jax.numpy as jnp
import numpy as np
from jax import lax

D = 1024
HEADS = 16
HEAD_DIM = 64
FF = 4096
CLASSES = 101
BANDS = 32
FRAMES = 5
SIDE = 16
WIN_S = 16
WIN_T = 8
CLIPS = 16
RS = 961
RT = 2025
N_MP = 2


def draw_ada_weight(key, part):
    key = jax.random.fold_in(key, 11)
    values = jnp.clip(jax.random.normal(key, (2, D, 6 * D), jnp.float32), -6.0, 6.0)
    column = jnp.arange(6 * D).astype(jnp.float32) / (6 * D - 1)
    column_scale = 0.25 * jnp.exp(jnp.log(4.0) * column)
    return (values * column_scale[None, None, :] * D ** (-0.5)).astype(jnp.bfloat16)


def place_ends(values, own_key, low, top_value):
    spot = [jax.random.randint(jax.random.fold_in(own_key, axis), (), 0, length) for axis, length in enumerate(values.shape)]
    longest = values.shape.index(max(values.shape))
    neighbour = spot[:longest] + [(spot[longest] + 1) % values.shape[longest]] + spot[longest + 1:]
    return values.at[tuple(spot)].set(low).at[tuple(neighbour)].set(top_value)


def steps_of(key, shape, shards, smallest, high):
    level = 1.0
    for axis_at, shards_of in shards:
        steps = jax.random.uniform(jax.random.fold_in(jax.random.fold_in(key, 6), axis_at), (shards_of,), jnp.float32, smallest / len(shards), high / len(shards))
        level = level * jnp.repeat(jnp.exp(steps), shape[axis_at] // shards_of).reshape((-1,) + (1,) * (len(shape) - 1 - axis_at))
    return level


def scatter_about(key, dims, scale, bound, split=(), held_as=jnp.bfloat16):
    values = scale * jax.random.normal(key, dims, jnp.float32)
    if split:
        values = values * steps_of(key, dims, split, -0.22, 0.18)
    return jnp.clip(values, -bound, bound).astype(held_as)


def setup_inputs(seed: int = 0) -> dict:
    arg_keys = jax.random.split(jax.random.key(seed), 16)
    latents = scatter_about(arg_keys[0], (CLIPS, FRAMES, SIDE, SIDE, D), 1.0, 6.0, ((0, 16), (2, 2)))
    cotangent = scatter_about(arg_keys[1], (CLIPS, FRAMES, SIDE, SIDE, D), 1.0, 6.0, ((0, 16), (2, 2)))
    frame_counts = place_ends(jax.random.randint(arg_keys[2], (CLIPS,), 2, FRAMES + 1), jax.random.fold_in(arg_keys[2], 1), 2, FRAMES).astype(jnp.int32)
    band_ids = place_ends(jax.random.randint(arg_keys[3], (CLIPS,), 0, BANDS), jax.random.fold_in(arg_keys[3], 1), 0, BANDS - 1).astype(jnp.int32)
    class_ids = place_ends(jax.random.randint(arg_keys[4], (CLIPS,), 0, CLASSES), jax.random.fold_in(arg_keys[4], 1), 0, CLASSES - 1).astype(jnp.int32)
    time_table = scatter_about(arg_keys[5], (BANDS, D), 1.0, 6.0)
    class_table = scatter_about(arg_keys[6], (CLASSES, D), 1.0, 6.0)
    ada_weight = draw_ada_weight(jax.random.fold_in(arg_keys[15], 71), 0)
    ada_bias = scatter_about(arg_keys[8], (2, 6 * D), 0.5, 3.0, ((1, 32),))
    qkv_weight = scatter_about(arg_keys[9], (2, D, 3, D), D ** -0.5, 0.1875, ((1, 16), (3, 2)))
    out_weight = scatter_about(arg_keys[10], (2, D, D), (D // 16) ** -0.5, 0.75, ((1, 2), (2, 16)))
    up_weight = scatter_about(arg_keys[11], (2, D, FF), D ** -0.5, 0.1875, ((1, 16), (2, 2)))
    down_weight = scatter_about(arg_keys[12], (2, FF, D), FF ** -0.5, 0.09375, ((1, 2), (2, 16)))
    spatial_bias = scatter_about(arg_keys[13], (HEADS, RS), 0.5, 3.0, ((0, 2),))
    joint_bias = scatter_about(arg_keys[14], (HEADS, RT), 0.5, 3.0, ((0, 2),))
    return {"latents": latents, "cotangent": cotangent, "frame_counts": frame_counts, "band_ids": band_ids, "class_ids": class_ids, "time_table": time_table, "class_table": class_table, "ada_weight": ada_weight, "ada_bias": ada_bias, "qkv_weight": qkv_weight, "out_weight": out_weight, "up_weight": up_weight, "down_weight": down_weight, "spatial_bias": spatial_bias, "joint_bias": joint_bias}


epsilon = 1e-06
masked_score = -1e+30
highest = lax.Precision.HIGHEST

@jax.custom_vjp
def low(v):
    return lax.optimization_barrier(v.astype(jnp.bfloat16)).astype(jnp.float32)

@jax.custom_vjp
def low_back(v):
    return v

def low_keep(v):
    return (low(v), None)

def low_pass(kept, grad):
    return (grad,)

def back_keep(v):
    return (v, None)

def back_low(kept, grad):
    return (low(grad),)
low.defvjp(low_keep, low_pass)
low_back.defvjp(back_keep, back_low)

def spatial_table():
    places = np.arange(WIN_S * WIN_S)
    row_at = places // WIN_S
    col_at = places % WIN_S
    row_rel = row_at[:, None] - row_at[None, :] + WIN_S - 1
    col_rel = col_at[:, None] - col_at[None, :] + WIN_S - 1
    return (row_rel * (2 * WIN_S - 1) + col_rel).astype(np.int32)

def joint_table():
    places = np.arange(FRAMES * WIN_T * WIN_T)
    time_at = places // (WIN_T * WIN_T)
    row_at = places // WIN_T % WIN_T
    col_at = places % WIN_T
    time_rel = time_at[:, None] - time_at[None, :] + FRAMES - 1
    row_rel = row_at[:, None] - row_at[None, :] + WIN_T - 1
    col_rel = col_at[:, None] - col_at[None, :] + WIN_T - 1
    return ((time_rel * (2 * WIN_T - 1) + row_rel) * (2 * WIN_T - 1) + col_rel).astype(np.int32)

def to_windows(values, window, is_joint):
    clip_count, frames, side_cells, channels = (values.shape[0], values.shape[1], values.shape[2], values.shape[4])
    per_side = side_cells // window
    if is_joint:
        shaped = values.reshape(clip_count, frames, per_side, window, per_side, window, channels)
        shaped = shaped.transpose(0, 2, 4, 1, 3, 5, 6)
        return shaped.reshape(clip_count * per_side * per_side, frames * window * window, channels)
    shaped = values.reshape(clip_count, frames, per_side, window, per_side, window, channels)
    shaped = shaped.transpose(0, 1, 2, 4, 3, 5, 6)
    return shaped.reshape(clip_count * frames * per_side * per_side, window * window, channels)

def from_windows(values, clip_count, frames, side_cells, window, is_joint):
    per_side = side_cells // window
    channels = values.shape[-1]
    if is_joint:
        shaped = values.reshape(clip_count, per_side, per_side, frames, window, window, channels)
        shaped = shaped.transpose(0, 3, 1, 4, 2, 5, 6)
    else:
        shaped = values.reshape(clip_count, frames, per_side, per_side, window, window, channels)
        shaped = shaped.transpose(0, 1, 2, 4, 3, 5, 6)
    return shaped.reshape(clip_count, frames, side_cells, side_cells, channels)

def normalize(values):
    center = values - lax.optimization_barrier(jnp.mean(values, axis=-1, keepdims=True))
    spread = lax.optimization_barrier(jnp.mean(center * center, axis=-1, keepdims=True))
    return center * lax.rsqrt(spread + epsilon)

def group_copies(values, groups):
    return low_back(jnp.broadcast_to(values[:, :, :, None, :], (values.shape[0], values.shape[1], values.shape[2], groups, values.shape[3])))

def layer_pair(latent, modulated, frame_valid, qkv_all, out_all, up_all, down_all, spatial_matrix, joint_matrix):
    groups = N_MP
    local_width = D // groups
    local_hidden = FF // groups
    frame_mask = frame_valid[:, None, None, None]
    key_frames = np.arange(FRAMES * WIN_T * WIN_T) // (WIN_T * WIN_T)
    key_valid = frame_valid[key_frames]
    current = latent
    for which_block in range(2):
        is_joint = which_block == 1
        window = WIN_T if is_joint else WIN_S
        bias_matrix = joint_matrix if is_joint else spatial_matrix
        shift_one = modulated[which_block, 0]
        scale_one = modulated[which_block, 1]
        gate_one = modulated[which_block, 2]
        shift_two = modulated[which_block, 3]
        scale_two = modulated[which_block, 4]
        gate_two = modulated[which_block, 5]
        moved = low(normalize(current) * (1.0 + scale_one) + shift_one)
        copies = group_copies(moved, groups)
        qkv_grouped = qkv_all[which_block].reshape(D, 3, groups, local_width)
        projected = jnp.einsum('fyxgd,dkgh->fyxkgh', copies, qkv_grouped, precision=highest)
        projected = low_back(low(projected))
        windows = to_windows(projected.reshape(1, FRAMES, SIDE, SIDE, 3 * D), window, is_joint)
        windows = windows.reshape(windows.shape[0], windows.shape[1], 3, HEADS, HEAD_DIM)
        query_part = windows[:, :, 0]
        key_part = windows[:, :, 1]
        value_part = windows[:, :, 2]
        scores = jnp.einsum('nqhe,nkhe->nhqk', query_part, key_part, precision=highest) * HEAD_DIM ** (-0.5) + bias_matrix[None]
        scores = low_back(scores)
        if is_joint:
            scores = jnp.where(key_valid[None, None, None, :] > 0, scores, masked_score)
        row_max = lax.optimization_barrier(jnp.max(scores, axis=-1, keepdims=True))
        weights = jnp.exp(scores - row_max)
        probs_low = low(weights / lax.optimization_barrier(jnp.sum(weights, axis=-1, keepdims=True)))
        mixed_rows = jnp.einsum('nhqk,nkhe->nqhe', probs_low, value_part, precision=highest)
        mixed_rows = low_back(low(mixed_rows))
        mixed_rows = from_windows(mixed_rows.reshape(mixed_rows.shape[0], mixed_rows.shape[1], D), 1, FRAMES, SIDE, window, is_joint)[0]
        mixed_groups = mixed_rows.reshape(FRAMES, SIDE, SIDE, groups, local_width)
        partial_value = jnp.einsum('fyxgk,gkd->fyxgd', mixed_groups, out_all[which_block].reshape(groups, local_width, D), precision=highest)
        branch = low_back(lax.optimization_barrier(jnp.sum(low(partial_value), axis=3)))
        current = current + frame_mask * gate_one * branch
        moved = low(normalize(current) * (1.0 + scale_two) + shift_two)
        copies = group_copies(moved, groups)
        hidden = low_back(jnp.einsum('fyxgd,dgk->fyxgk', copies, up_all[which_block].reshape(D, groups, local_hidden), precision=highest))
        activated = low(jax.nn.gelu(hidden, approximate=False))
        partial_value = jnp.einsum('fyxgk,gkd->fyxgd', activated, down_all[which_block].reshape(groups, local_hidden, D), precision=highest)
        branch = low_back(lax.optimization_barrier(jnp.sum(low(partial_value), axis=3)))
        current = current + frame_mask * gate_two * branch
    return current

def reference(latents, cotangent, frame_counts, band_ids, class_ids, time_table, class_table, ada_weight, ada_bias, qkv_weight, out_weight, up_weight, down_weight, spatial_bias, joint_bias):
    spatial_index = spatial_table()
    joint_index = joint_table()
    frame_valid = (jnp.arange(FRAMES)[None, :] < frame_counts[:, None]).astype(jnp.float32)
    band_hot = (band_ids[:, None] == jnp.arange(BANDS)[None, :]).astype(jnp.float32)
    class_hot = (class_ids[:, None] == jnp.arange(CLASSES)[None, :]).astype(jnp.float32)

    def forward(latent_all, time_rows, class_rows, ada_w, ada_b, qkv_all, out_all, up_all, down_all, spatial_rows, joint_rows):
        condition = jnp.dot(band_hot, time_rows, precision=highest) + jnp.dot(class_hot, class_rows, precision=highest)
        activity = low(jax.nn.silu(condition))
        modulation = jnp.einsum('cd,bde->bce', activity, ada_w, precision=highest) + ada_b[:, None, :]
        modulation = modulation.reshape(2, CLIPS, 6, D).transpose(1, 0, 2, 3)
        spatial_matrix = spatial_rows[:, spatial_index]
        joint_matrix = joint_rows[:, joint_index]

        def one_clip(running, clip_items):
            latent, modulated, valid_row = clip_items
            outcome = jax.checkpoint(layer_pair)(latent, modulated, valid_row, qkv_all, out_all, up_all, down_all, spatial_matrix, joint_matrix)
            return (running, outcome)
        return lax.scan(one_clip, jnp.zeros((), jnp.float32), (latent_all, modulation, frame_valid))[1]
    arguments = tuple((array_value.astype(jnp.float32) for array_value in (latents, time_table, class_table, ada_weight, ada_bias, qkv_weight, out_weight, up_weight, down_weight, spatial_bias, joint_bias)))
    result, pullback = jax.vjp(forward, *arguments)
    gradients = pullback(cotangent.astype(jnp.float32))
    return (result, gradients[0], gradients[1], gradients[2], gradients[3], gradients[4], gradients[5], gradients[6], gradients[7], gradients[8], gradients[9], gradients[10])
```

```python
import jax
import jax.numpy as jnp
import numpy as np
from jax import lax
from jax.experimental import pallas as pl
from jax.experimental.pallas import tpu as pltpu
from jax.sharding import Mesh
from jax.sharding import PartitionSpec as P

HEAD_DIM = 64
CLASSES = 101
BANDS = 32
FRAMES = 5
WIN_S = 16
WIN_T = 8


epsilon = 1e-06
masked_score = -1e30


def spatial_table():
    places = np.arange(WIN_S * WIN_S)
    row_at = places // WIN_S
    col_at = places % WIN_S
    row_rel = row_at[:, None] - row_at[None, :] + WIN_S - 1
    col_rel = col_at[:, None] - col_at[None, :] + WIN_S - 1
    return (row_rel * (2 * WIN_S - 1) + col_rel).astype(np.int32)


def joint_table():
    places = np.arange(FRAMES * WIN_T * WIN_T)
    time_at = places // (WIN_T * WIN_T)
    row_at = places // WIN_T % WIN_T
    col_at = places % WIN_T
    time_rel = time_at[:, None] - time_at[None, :] + FRAMES - 1
    row_rel = row_at[:, None] - row_at[None, :] + WIN_T - 1
    col_rel = col_at[:, None] - col_at[None, :] + WIN_T - 1
    return ((time_rel * (2 * WIN_T - 1) + row_rel) * (2 * WIN_T - 1) + col_rel).astype(np.int32)


def to_windows(values, window, is_joint):
    clip_count, frames, side_cells, channels = (
        values.shape[0],
        values.shape[1],
        values.shape[2],
        values.shape[4],
    )
    per_side = side_cells // window
    if is_joint:
        shaped = values.reshape(clip_count, frames, per_side, window, per_side, window, channels)
        shaped = shaped.transpose(0, 2, 4, 1, 3, 5, 6)
        return shaped.reshape(clip_count * per_side * per_side, frames * window * window, channels)
    shaped = values.reshape(clip_count, frames, per_side, window, per_side, window, channels)
    shaped = shaped.transpose(0, 1, 2, 4, 3, 5, 6)
    return shaped.reshape(clip_count * frames * per_side * per_side, window * window, channels)


def from_windows(values, clip_count, frames, side_cells, window, is_joint):
    per_side = side_cells // window
    channels = values.shape[-1]
    if is_joint:
        shaped = values.reshape(clip_count, per_side, per_side, frames, window, window, channels)
        shaped = shaped.transpose(0, 3, 1, 4, 2, 5, 6)
    else:
        shaped = values.reshape(clip_count, frames, per_side, per_side, window, window, channels)
        shaped = shaped.transpose(0, 1, 2, 4, 3, 5, 6)
    return shaped.reshape(clip_count, frames, side_cells, side_cells, channels)


def normalize(values):
    center = values - jnp.mean(values, axis=-1, keepdims=True)
    spread = jnp.mean(center * center, axis=-1, keepdims=True)
    inverse = lax.rsqrt(spread + epsilon)
    return (center * inverse, inverse)


def norm_back(grad_normed, normed, inverse):
    first_mean = jnp.mean(grad_normed, axis=-1, keepdims=True)
    second_mean = jnp.mean(grad_normed * normed, axis=-1, keepdims=True)
    return inverse * (grad_normed - first_mean - normed * second_mean)


def exact_gelu(values):
    return jax.nn.gelu(values, approximate=False)


def gather_rows(values):
    return lax.all_gather(values, "mp", axis=2, tiled=True)


def sum_rows(values):
    return lax.psum_scatter(
        values.astype(jnp.bfloat16), "mp", scatter_dimension=2, tiled=True
    ).astype(jnp.float32)


def gather_grads(values):
    return lax.all_gather(values, "mp", axis=2, tiled=True)


def input_sums(values):
    return lax.psum_scatter(
        values.astype(jnp.bfloat16), "mp", scatter_dimension=2, tiled=True
    ).astype(jnp.float32)


def inputs_again(moved):
    return lax.all_gather(moved, "mp", axis=2, tiled=True)


def attention_scores(query_part, key_part, bias_matrix, key_valid):
    scores = (
        jnp.einsum("nqhe,nkhe->nhqk", query_part, key_part, preferred_element_type=jnp.float32)
        * HEAD_DIM ** (-0.5)
        + bias_matrix[None]
    )
    if key_valid is not None:
        scores = jnp.where(key_valid[:, None, None, :] > 0, scores, masked_score)
    return scores


def local(
    latents,
    cotangent,
    frame_counts,
    band_ids,
    class_ids,
    time_table,
    class_table,
    ada_weight,
    ada_bias,
    qkv_weight,
    out_weight,
    up_weight,
    down_weight,
    spatial_bias,
    joint_bias,
):
    clip_count = latents.shape[0]
    frames = latents.shape[1]
    side_cells = latents.shape[3]
    model_width = latents.shape[4]
    heads_local = spatial_bias.shape[0]
    local_width = heads_local * HEAD_DIM
    dp_count = lax.axis_size("dp")
    mp_count = lax.axis_size("mp")
    col_width = ada_weight.shape[2]
    band_hot = (band_ids[:, None] == jnp.arange(BANDS)[None, :]).astype(jnp.bfloat16)
    class_hot = (class_ids[:, None] == jnp.arange(CLASSES)[None, :]).astype(jnp.bfloat16)
    condition = jnp.dot(band_hot, time_table, preferred_element_type=jnp.float32) + jnp.dot(
        class_hot, class_table, preferred_element_type=jnp.float32
    )
    activity_low = jax.nn.silu(condition).astype(jnp.bfloat16)
    ada_cols, ada_bias_cols = (
        lax.all_gather(ada_weight, "mp", axis=2, tiled=True),
        lax.all_gather(ada_bias, "mp", axis=1, tiled=True),
    )
    mod_part = jnp.einsum(
        "cd,bde->bce", activity_low, ada_cols, preferred_element_type=jnp.float32
    ) + ada_bias_cols[:, None, :].astype(jnp.float32)
    modulation = lax.all_gather(mod_part, "dp", axis=2, tiled=True)
    first_clip = lax.axis_index("dp") * clip_count
    own_mod = lax.dynamic_slice_in_dim(modulation, first_clip, clip_count, 1).reshape(
        2, clip_count, 6, model_width
    )
    frame_valid = (jnp.arange(frames)[None, :] < frame_counts[:, None]).astype(jnp.float32)
    frame_mask = frame_valid[:, :, None, None, None]
    key_frames = np.arange(frames * WIN_T * WIN_T) // (WIN_T * WIN_T)
    joint_cells = key_frames.shape[0]
    per_side = side_cells // WIN_T
    key_valid = frame_valid[:, key_frames]
    key_valid = jnp.broadcast_to(
        key_valid[:, None, :], (clip_count, per_side * per_side, joint_cells)
    ).reshape(clip_count * per_side * per_side, joint_cells)
    w_qkv, w_out, w_up, w_down = (
        lax.all_gather(qkv_weight, "dp", axis=1, tiled=True),
        lax.all_gather(out_weight, "dp", axis=2, tiled=True),
        lax.all_gather(up_weight, "dp", axis=1, tiled=True),
        lax.all_gather(down_weight, "dp", axis=2, tiled=True),
    )
    spatial_index = spatial_table()
    joint_index = joint_table()
    spatial_matrix = spatial_bias.astype(jnp.float32)[:, spatial_index]
    joint_matrix = joint_bias.astype(jnp.float32)[:, joint_index]
    current = latents.astype(jnp.float32)
    stored = []
    for which_block in range(2):
        is_joint = which_block == 1
        window = WIN_T if is_joint else WIN_S
        bias_matrix = joint_matrix if is_joint else spatial_matrix
        mask_keys = key_valid if is_joint else None
        block_mod = own_mod[which_block][:, :, None, None, None, :]
        normed_one, inverse_one = normalize(current)
        moved_one = (normed_one * (1.0 + block_mod[:, 1]) + block_mod[:, 0]).astype(jnp.bfloat16)
        gathered_one = gather_rows(moved_one)
        projected = jnp.einsum(
            "cfyxd,dkh->cfyxkh",
            gathered_one,
            w_qkv[which_block],
            preferred_element_type=jnp.float32,
        ).astype(jnp.bfloat16)
        windows = to_windows(
            projected.reshape(clip_count, frames, side_cells, side_cells, 3 * local_width),
            window,
            is_joint,
        )
        windows = windows.reshape(windows.shape[0], windows.shape[1], 3, heads_local, HEAD_DIM)
        scores = attention_scores(windows[:, :, 0], windows[:, :, 1], bias_matrix, mask_keys)
        row_max = jnp.max(scores, axis=-1, keepdims=True)
        log_total = row_max + jnp.log(jnp.sum(jnp.exp(scores - row_max), axis=-1, keepdims=True))
        probs_low = jnp.exp(scores - log_total).astype(jnp.bfloat16)
        mixed_win = jnp.einsum(
            "nhqk,nkhe->nqhe", probs_low, windows[:, :, 2], preferred_element_type=jnp.float32
        ).astype(jnp.bfloat16)
        mixed_rows = from_windows(
            mixed_win.reshape(mixed_win.shape[0], mixed_win.shape[1], local_width),
            clip_count,
            frames,
            side_cells,
            window,
            is_joint,
        )
        branch_one = sum_rows(
            jnp.einsum(
                "cfyxk,kd->cfyxd",
                mixed_rows,
                w_out[which_block],
                preferred_element_type=jnp.float32,
            )
        )
        after_attn = current + frame_mask * block_mod[:, 2] * branch_one
        normed_two, inverse_two = normalize(after_attn)
        moved_two = (normed_two * (1.0 + block_mod[:, 4]) + block_mod[:, 3]).astype(jnp.bfloat16)
        gathered_two = gather_rows(moved_two)
        hidden = jnp.einsum(
            "cfyxd,dk->cfyxk", gathered_two, w_up[which_block], preferred_element_type=jnp.float32
        )
        activated = exact_gelu(hidden).astype(jnp.bfloat16)
        branch_two = sum_rows(
            jnp.einsum(
                "cfyxk,kd->cfyxd",
                activated,
                w_down[which_block],
                preferred_element_type=jnp.float32,
            )
        )
        current = after_attn + frame_mask * block_mod[:, 5] * branch_two
        stored.append(
            (
                normed_one,
                inverse_one,
                moved_one,
                gathered_one,
                windows,
                log_total,
                mixed_rows,
                branch_one,
                normed_two,
                inverse_two,
                moved_two,
                gathered_two,
                hidden,
                activated,
                branch_two,
            )
        )
    grad_state = cotangent.astype(jnp.float32)
    mod_grads = []
    qkv_grads = []
    out_grads = []
    up_grads = []
    down_grads = []
    table_parts = []
    for which_block in (1, 0):
        is_joint = which_block == 1
        window = WIN_T if is_joint else WIN_S
        bias_matrix = joint_matrix if is_joint else spatial_matrix
        mask_keys = key_valid if is_joint else None
        block_mod = own_mod[which_block][:, :, None, None, None, :]
        (
            normed_one,
            inverse_one,
            moved_one,
            gathered_one,
            windows,
            log_total,
            mixed_rows,
            branch_one,
            normed_two,
            inverse_two,
            moved_two,
            gathered_two,
            hidden,
            activated,
            branch_two,
        ) = stored[which_block]
        grad_gate_two = jnp.sum(frame_mask * grad_state * branch_two, axis=(1, 2, 3))
        grad_rows = gather_grads((frame_mask * block_mod[:, 5] * grad_state).astype(jnp.bfloat16))
        down_grads.append(
            jnp.einsum("cfyxk,cfyxd->kd", activated, grad_rows, preferred_element_type=jnp.float32)
        )
        grad_act = jnp.einsum(
            "cfyxd,kd->cfyxk", grad_rows, w_down[which_block], preferred_element_type=jnp.float32
        )
        grad_hidden = jax.vjp(exact_gelu, hidden)[1](grad_act)[0].astype(jnp.bfloat16)
        inputs_two = inputs_again(moved_two)
        up_grads.append(
            jnp.einsum(
                "cfyxd,cfyxk->dk", inputs_two, grad_hidden, preferred_element_type=jnp.float32
            )
        )
        grad_moved = input_sums(
            jnp.einsum(
                "cfyxk,dk->cfyxd",
                grad_hidden,
                w_up[which_block],
                preferred_element_type=jnp.float32,
            )
        )
        grad_shift_two = jnp.sum(grad_moved, axis=(1, 2, 3))
        grad_scale_two = jnp.sum(grad_moved * normed_two, axis=(1, 2, 3))
        grad_state = grad_state + norm_back(
            grad_moved * (1.0 + block_mod[:, 4]), normed_two, inverse_two
        )
        grad_gate_one = jnp.sum(frame_mask * grad_state * branch_one, axis=(1, 2, 3))
        grad_rows = gather_grads((frame_mask * block_mod[:, 2] * grad_state).astype(jnp.bfloat16))
        out_grads.append(
            jnp.einsum("cfyxk,cfyxd->kd", mixed_rows, grad_rows, preferred_element_type=jnp.float32)
        )
        grad_mixed = jnp.einsum(
            "cfyxd,kd->cfyxk", grad_rows, w_out[which_block], preferred_element_type=jnp.float32
        ).astype(jnp.bfloat16)
        grad_win = to_windows(grad_mixed, window, is_joint)
        grad_win = grad_win.reshape(grad_win.shape[0], grad_win.shape[1], heads_local, HEAD_DIM)
        query_part = windows[:, :, 0]
        key_part = windows[:, :, 1]
        value_part = windows[:, :, 2]
        probs_full = jnp.exp(
            attention_scores(query_part, key_part, bias_matrix, mask_keys) - log_total
        )
        grad_value = jnp.einsum(
            "nhqk,nqhe->nkhe",
            probs_full.astype(jnp.bfloat16),
            grad_win,
            preferred_element_type=jnp.float32,
        ).astype(jnp.bfloat16)
        grad_probs = jnp.einsum(
            "nqhe,nkhe->nhqk", grad_win, value_part, preferred_element_type=jnp.float32
        )
        row_dot = jnp.sum(probs_full * grad_probs, axis=-1, keepdims=True)
        grad_scores = (probs_full * (grad_probs - row_dot)).astype(jnp.bfloat16)
        bias_sum = jnp.sum(grad_scores.astype(jnp.float32), axis=0)
        if is_joint:
            table_parts.append(
                jnp.zeros((heads_local, joint_bias.shape[1]), jnp.float32)
                .at[:, joint_index]
                .add(bias_sum)
            )
        else:
            table_parts.append(
                jnp.zeros((heads_local, spatial_bias.shape[1]), jnp.float32)
                .at[:, spatial_index]
                .add(bias_sum)
            )
        grad_query = (
            jnp.einsum("nhqk,nkhe->nqhe", grad_scores, key_part, preferred_element_type=jnp.float32)
            * HEAD_DIM ** (-0.5)
        ).astype(jnp.bfloat16)
        grad_key = (
            jnp.einsum(
                "nhqk,nqhe->nkhe", grad_scores, query_part, preferred_element_type=jnp.float32
            )
            * HEAD_DIM ** (-0.5)
        ).astype(jnp.bfloat16)
        stacked = jnp.stack([grad_query, grad_key, grad_value], axis=2).reshape(
            grad_query.shape[0], grad_query.shape[1], 3 * local_width
        )
        grad_projected = from_windows(
            stacked, clip_count, frames, side_cells, window, is_joint
        ).reshape(clip_count, frames, side_cells, side_cells, 3, local_width)
        inputs_one = inputs_again(moved_one)
        qkv_grads.append(
            jnp.einsum(
                "cfyxd,cfyxkh->dkh", inputs_one, grad_projected, preferred_element_type=jnp.float32
            )
        )
        grad_moved = input_sums(
            jnp.einsum(
                "cfyxkh,dkh->cfyxd",
                grad_projected,
                w_qkv[which_block],
                preferred_element_type=jnp.float32,
            )
        )
        grad_shift_one = jnp.sum(grad_moved, axis=(1, 2, 3))
        grad_scale_one = jnp.sum(grad_moved * normed_one, axis=(1, 2, 3))
        grad_state = grad_state + norm_back(
            grad_moved * (1.0 + block_mod[:, 1]), normed_one, inverse_one
        )
        mod_grads.append(
            jnp.stack(
                [
                    grad_shift_one,
                    grad_scale_one,
                    grad_gate_one,
                    grad_shift_two,
                    grad_scale_two,
                    grad_gate_two,
                ],
                axis=1,
            )
        )
    grad_mod = jnp.stack(mod_grads[::-1], axis=0).reshape(2, clip_count, 6 * model_width)
    ordered = (
        grad_mod.reshape(2, clip_count, dp_count, mp_count, col_width)
        .transpose(0, 1, 3, 2, 4)
        .reshape(2, clip_count, 6 * model_width)
    )
    summed_cols = lax.psum_scatter(ordered, "mp", scatter_dimension=2, tiled=True)
    grad_mod_cols = lax.all_to_all(summed_cols, "dp", split_axis=2, concat_axis=1, tiled=True)
    grad_ada_weight = jnp.einsum(
        "cd,bce->bde",
        activity_low.astype(jnp.float32),
        grad_mod_cols,
        precision=lax.Precision.HIGHEST,
    )
    grad_ada_bias = jnp.sum(grad_mod_cols, axis=1)
    grad_mod_block = lax.all_gather(grad_mod_cols, "mp", axis=2, tiled=True)
    activity_part = jnp.einsum(
        "bce,bde->cd", grad_mod_block, ada_cols.astype(jnp.float32), precision=lax.Precision.HIGHEST
    )
    grad_activity = lax.psum(activity_part, "dp")
    grad_condition = jax.vjp(jax.nn.silu, condition)[1](grad_activity)[0]
    grad_time = jnp.dot(
        band_hot.astype(jnp.float32).T, grad_condition, precision=lax.Precision.HIGHEST
    )
    grad_class = jnp.dot(
        class_hot.astype(jnp.float32).T, grad_condition, precision=lax.Precision.HIGHEST
    )
    grad_spatial, grad_joint = lax.psum((table_parts[1], table_parts[0]), "dp")
    grad_qkv, grad_out, grad_up, grad_down = (
        lax.psum_scatter(jnp.stack(qkv_grads[::-1], axis=0), "dp", scatter_dimension=1, tiled=True),
        lax.psum_scatter(jnp.stack(out_grads[::-1], axis=0), "dp", scatter_dimension=2, tiled=True),
        lax.psum_scatter(jnp.stack(up_grads[::-1], axis=0), "dp", scatter_dimension=1, tiled=True),
        lax.psum_scatter(
            jnp.stack(down_grads[::-1], axis=0), "dp", scatter_dimension=2, tiled=True
        ),
    )
    return (
        current,
        grad_state,
        grad_time,
        grad_class,
        grad_ada_weight,
        grad_ada_bias,
        grad_qkv,
        grad_out,
        grad_up,
        grad_down,
        grad_spatial,
        grad_joint,
    )


def solution_any(mesh):
    placed = (
        P("dp", None, "mp", None, None),
        P("dp", None, "mp", None, None),
        P("dp"),
        P(),
        P(),
        P(),
        P(),
        P(None, None, ("dp", "mp")),
        P(None, ("dp", "mp")),
        P(None, "dp", None, "mp"),
        P(None, "mp", "dp"),
        P(None, "dp", "mp"),
        P(None, "mp", "dp"),
        P("mp", None),
        P("mp", None),
    )
    return jax.shard_map(
        local,
        mesh=mesh,
        in_specs=placed,
        out_specs=(
            P("dp", None, "mp", None, None),
            P("dp", None, "mp", None, None),
            P(),
            P(),
            P(None, None, ("dp", "mp")),
            P(None, ("dp", "mp")),
            P(None, "dp", None, "mp"),
            P(None, "mp", "dp"),
            P(None, "dp", "mp"),
            P(None, "mp", "dp"),
            P("mp", None),
            P("mp", None),
        ),
        check_vma=False,
    )


low = jnp.bfloat16
full = jnp.float32
HALF_ROOT = 0.7071067811865476
PHI_AT_ZERO = 0.3989422804014327
MIB = 1024 * 1024


def flip(values, axis):
    return lax.ppermute(values, axis, [(0, 1), (1, 0)])


def z_trade(values, step):
    return lax.ppermute(values, "z", [(place, place ^ step) for place in range(4)])


def swap(values):
    return lax.ppermute(values, ("c", "x"), [(0, 0), (1, 2), (2, 1), (3, 3)])


def params(mib, semantics=None):
    return pltpu.CompilerParams(vmem_limit_bytes=mib * MIB, dimension_semantics=semantics)


def place_kernel(where, own, from_y, from_x, far_lo, far_hi, whole):
    k = pl.program_id(0)
    place = where[1] * 2 + where[2]
    whole[0, place] = own[0]
    whole[0, place ^ 1] = from_x[0]
    whole[0, place ^ 2] = from_y[0]

    @pl.when(k < 2)
    def _():
        whole[0, place ^ 3] = far_lo[0]

    @pl.when(k >= 2)
    def _():
        whole[0, place ^ 3] = far_hi[0]


def gather_piece(shard, where):
    rows, width = shard.shape
    near = [shard] + [z_trade(shard, k) for k in (1, 2, 3)]
    own = jnp.stack(near)
    from_y = flip(own, "y")
    from_x = flip(own, "x")
    far_lo = flip(from_y[:2], "x")
    far_hi = flip(from_x[2:], "y")
    block = (1, rows, width)
    whole = pl.pallas_call(
        place_kernel,
        grid_spec=pltpu.PrefetchScalarGridSpec(
            num_scalar_prefetch=1,
            grid=(4,),
            in_specs=[pl.BlockSpec(block, lambda k, where: (k, 0, 0))] * 3
            + [
                pl.BlockSpec(block, lambda k, where: (jnp.minimum(k, 1), 0, 0)),
                pl.BlockSpec(block, lambda k, where: (jnp.maximum(k - 2, 0), 0, 0)),
            ],
            out_specs=pl.BlockSpec(
                (1, 4, rows, width), lambda k, where: (where[0] ^ k, 0, 0, 0)
            ),
        ),
        out_shape=jax.ShapeDtypeStruct((4, 4, rows, width), shard.dtype),
        compiler_params=params(16),
        cost_estimate=pl.CostEstimate(
            flops=0, bytes_accessed=2 * 16 * rows * width * 2, transcendentals=0
        ),
        name="place_weights",
    )(where, own, from_y, from_x, far_lo, far_hi)
    return whole.reshape(16 * rows, width)


def scatter_piece(parts, where):
    own, to_x, to_y, far_lo, far_hi = parts
    z = where[0]
    got_x = flip(far_lo, "x")
    got_y = flip(far_hi, "y")
    add = lambda a, b: (a.astype(full) + b.astype(full)).astype(low)
    to_y = jnp.concatenate([add(to_y[:2], got_x), to_y[2:]])
    to_x = jnp.concatenate([to_x[:2], add(to_x[2:], got_y)])
    got_y = flip(to_y, "y")
    got_x = flip(to_x, "x")

    def total(k):
        pick = lambda a: lax.dynamic_index_in_dim(a, z ^ k, 0, keepdims=False).astype(full)
        return pick(own) + pick(got_y) + pick(got_x)

    result = total(0)
    for k in (1, 2, 3):
        result = result + z_trade(total(k).astype(low), k).astype(full)
    return swap(result.astype(low)).astype(full)


def weight_grad_kernel(where, *refs, pairs, widths):
    lhs = refs[: 2 * pairs]
    rhs = refs[2 * pairs : 3 * pairs]
    own, to_x, to_y, far_lo, far_hi, held = refs[3 * pairs :]
    z = pl.program_id(0)
    place = where[1] * 2 + where[2]
    start = 0
    for at in range(pairs):
        first = lhs[2 * at][...].T
        second = lhs[2 * at + 1][...].T
        for begin in range(0, widths[at], 512):
            cols = slice(begin, begin + 512)
            block = jnp.dot(
                first, rhs[at][0, :, cols], preferred_element_type=full
            ) + jnp.dot(second, rhs[at][1, :, cols], preferred_element_type=full)
            held[:, start + begin : start + begin + 512] = block.astype(low)
        start += widths[at]

    def part(rel):
        return held[pl.ds(pl.multiple_of((place ^ rel) * 64, 64), 64), :]

    own[0] = part(0)
    to_x[0] = part(1)
    to_y[0] = part(2)

    @pl.when(z < 2)
    def _():
        far_lo[0] = part(3)

    @pl.when(z >= 2)
    def _():
        far_hi[0] = part(3)


def weight_grad(where, *items):
    pairs = len(items)
    widths = tuple(item[2].shape[2] for item in items)
    width = sum(widths)
    rows, features = items[0][0].shape
    tile = features // 4
    quads = jax.ShapeDtypeStruct((4, 64, width), low)
    twos = jax.ShapeDtypeStruct((2, 64, width), low)
    lhs_spec = pl.BlockSpec((rows, tile), lambda z: (0, z))
    return pl.pallas_call(
        lambda *refs: weight_grad_kernel(*refs, pairs=pairs, widths=widths),
        grid=(4,),
        out_shape=[quads, quads, quads, twos, twos],
        in_specs=[pl.BlockSpec(memory_space=pltpu.SMEM)]
        + [lhs_spec] * (2 * pairs)
        + [pl.BlockSpec((2, rows, w), lambda z: (0, 0, 0)) for w in widths],
        out_specs=[pl.BlockSpec((1, 64, width), lambda z: (z, 0, 0))] * 3
        + [
            pl.BlockSpec((1, 64, width), lambda z: (jnp.minimum(z, 1), 0, 0)),
            pl.BlockSpec((1, 64, width), lambda z: (jnp.maximum(z - 2, 0), 0, 0)),
        ],
        scratch_shapes=[pltpu.VMEM((tile, width), low)],
        compiler_params=params(56),
        cost_estimate=pl.CostEstimate(
            flops=4 * rows * features * width,
            bytes_accessed=4 * rows * (width + features) + 2 * features * width,
            transcendentals=0,
        ),
        name="weight_grad",
    )(where, *[half for item in items for half in item[:2]], *[item[2] for item in items])


def gelu_and_slope(values):
    bell = jnp.exp(-0.5 * values * values)
    t = 1.0 / (1.0 + (0.3275911 * HALF_ROOT) * jnp.abs(values))
    poly = t * (
        0.254829592
        + t * (-0.284496736 + t * (1.421413741 + t * (-1.453152027 + t * 1.061405429)))
    )
    tail = 0.5 * poly * bell
    phi = jnp.where(values >= 0, 1.0 - tail, tail)
    return values * phi, phi + (PHI_AT_ZERO * values) * bell


def both_kernel(kind, *refs):
    weight = refs[2][...]
    for half in range(2):
        product = jnp.dot(refs[half][...], weight, preferred_element_type=full)
        if kind == "gelu":
            act, slope = gelu_and_slope(product)
            refs[3][half] = act.astype(low)
            refs[4][half] = slope.astype(low)
        elif kind == "slope":
            refs[4][half] = (product * refs[3][half].astype(full)).astype(low)
        else:
            refs[3][half] = product.astype(low)


def both_times(kind, own, other, weight, slope=None):
    rows, depth = own.shape
    width = weight.shape[1]
    tile = 256 if kind == "gelu" else 512
    out_spec = pl.BlockSpec((2, rows, tile), lambda j: (0, 0, j))
    out = jax.ShapeDtypeStruct((2, rows, width), low)
    extra = [] if slope is None else [slope]
    count = 2 if kind == "gelu" else 1
    return pl.pallas_call(
        lambda *refs: both_kernel(kind, *refs),
        grid=(width // tile,),
        out_shape=[out] * count,
        in_specs=[pl.BlockSpec((rows, depth), lambda j: (0, 0))] * 2
        + [pl.BlockSpec((depth, tile), lambda j: (0, j))]
        + [out_spec] * len(extra),
        out_specs=[out_spec] * count,
        compiler_params=params(40),
        cost_estimate=pl.CostEstimate(
            flops=4 * rows * depth * width,
            bytes_accessed=4 * rows * depth + 2 * depth * width + 4 * rows * width * count,
            transcendentals=0,
        ),
        name="both_" + kind,
    )(own, other, weight, *extra)


def one_kernel(values, weight, out):
    out[...] = lax.dot_general(
        values[0], weight[...], (((1,), (1,)), ((), ())), preferred_element_type=full
    ).astype(low)


def one_back(values, half, weight):
    rows, depth = values.shape[1:]
    width = weight.shape[0]
    tile = 256
    return pl.pallas_call(
        one_kernel,
        grid=(width // tile,),
        out_shape=jax.ShapeDtypeStruct((rows, width), low),
        in_specs=[
            pl.BlockSpec((1, rows, depth), lambda j: (half, 0, 0)),
            pl.BlockSpec((tile, depth), lambda j: (j, 0)),
        ],
        out_specs=pl.BlockSpec((rows, tile), lambda j: (0, j)),
        compiler_params=params(40),
        cost_estimate=pl.CostEstimate(
            flops=2 * rows * depth * width,
            bytes_accessed=2 * (rows * depth + depth * width + rows * width),
            transcendentals=0,
        ),
        name="one_back",
    )(values, weight)


def branch_sum(values, weight):
    away = flip(one_back(values, 1, weight), "c")
    return one_back(values, 0, weight).astype(full) + away.astype(full)


def attend_kernel(count, bias, joined, mixed, probs, *, heads, cells, masked):
    width = heads * HEAD_DIM
    values = joined[...].reshape(cells, 3 * width)
    lead = mixed.shape
    if masked:
        column = lax.broadcasted_iota(jnp.int32, (1, cells), 1)
        shown = column < count[0] * (WIN_T * WIN_T)
    outs = []
    for h in range(heads):
        cols = slice(h * HEAD_DIM, (h + 1) * HEAD_DIM)
        query = values[:, cols]
        key = values[:, width + h * HEAD_DIM : width + (h + 1) * HEAD_DIM]
        value = values[:, 2 * width + h * HEAD_DIM : 2 * width + (h + 1) * HEAD_DIM]
        scores = lax.dot_general(
            query, key, (((1,), (1,)), ((), ())), preferred_element_type=full
        ) * HEAD_DIM ** (-0.5) + bias[h].astype(full)
        if masked:
            scores = jnp.where(shown, scores, masked_score)
        weights = jnp.exp(scores - jnp.max(scores, axis=-1, keepdims=True))
        share = (weights * (1.0 / jnp.sum(weights, axis=-1, keepdims=True))).astype(low)
        probs[0, h] = share
        outs.append(jnp.dot(share, value, preferred_element_type=full).astype(low))
    mixed[...] = jnp.concatenate(outs, axis=1).reshape(lead)


def attend_back_kernel(joined, grad, probs, back, bias_out, total, *, heads, cells, sides):
    step = pl.program_id(0) * pl.num_programs(1) + pl.program_id(1)
    width = heads * HEAD_DIM
    values = joined[...].reshape(cells, 3 * width)
    grads = grad[...].reshape(cells, width)
    grads_t = grads.astype(full).T.astype(low)
    queries_t = values[:, :width].astype(full).T.astype(low)
    queries, keys_t, values_t = [], [], []

    @pl.when(step == 0)
    def _():
        total[...] = jnp.zeros(total.shape, full)

    for h in range(heads):
        cols = slice(h * HEAD_DIM, (h + 1) * HEAD_DIM)
        key = values[:, width + h * HEAD_DIM : width + (h + 1) * HEAD_DIM]
        value = values[:, 2 * width + h * HEAD_DIM : 2 * width + (h + 1) * HEAD_DIM]
        share = probs[0, h]
        values_t.append(jnp.dot(grads_t[cols], share, preferred_element_type=full).astype(low))
        grad_share = lax.dot_general(
            grads[:, cols], value, (((1,), (1,)), ((), ())), preferred_element_type=full
        )
        share_full = share.astype(full)
        product = share_full * grad_share
        row_dot = jnp.sum(product, axis=-1, keepdims=True)
        grad_scores = (product - share_full * row_dot).astype(low)

        total[h] += grad_scores.astype(full)
        queries.append(
            (jnp.dot(grad_scores, key, preferred_element_type=full) * HEAD_DIM ** (-0.5)).astype(
                low
            )
        )
        keys_t.append(
            (
                jnp.dot(queries_t[cols], grad_scores, preferred_element_type=full)
                * HEAD_DIM ** (-0.5)
            ).astype(low)
        )
    key_grads = jnp.concatenate(keys_t, axis=0).astype(full).T.astype(low)
    value_grads = jnp.concatenate(values_t, axis=0).astype(full).T.astype(low)
    back[...] = jnp.concatenate(queries + [key_grads, value_grads], axis=1).reshape(back.shape)

    @pl.when(step == pl.num_programs(0) * pl.num_programs(1) - 1)
    def _():
        for h in range(heads):
            for place, spots in enumerate(sides):
                part = None
                for row, col in spots:
                    block = total[h, row * 64 : row * 64 + 64, :][:, col * 64 : col * 64 + 64]
                    part = block if part is None else part + block
                bias_out[h, place] = part


def spatial_sides():
    sides = [[] for _ in range(9)]
    for row in range(4):
        for col in range(4):
            place = (row // 2 - col // 2 + 1) * 3 + (row % 2 - col % 2 + 1)
            sides[place].append((row, col))
    return sides


def joint_sides():
    sides = [[] for _ in range(2 * FRAMES - 1)]
    for row in range(FRAMES):
        for col in range(FRAMES):
            sides[row - col + FRAMES - 1].append((row, col))
    return sides


def window_specs(is_joint, frames, width):
    if is_joint:
        shape, at = (1, frames, 1, 64, width), lambda i, j: (i, 0, j, 0, 0)
    else:
        shape, at = (2, 1, 2, 64, width), lambda i, j: (0, j, 0, 0, 0)
    return pl.BlockSpec(shape, at)


def attend(count, bias, joined, is_joint):
    frames = joined.shape[1]
    heads, cells = bias.shape[0], bias.shape[1]
    width = heads * HEAD_DIM
    grid = (2, 2) if is_joint else (1, frames)
    number = grid[0] * grid[1]
    fetch = lambda i, j: (i * grid[1] + j, 0, 0, 0)
    return pl.pallas_call(
        lambda *refs: attend_kernel(*refs, heads=heads, cells=cells, masked=is_joint),
        grid=grid,
        out_shape=[
            jax.ShapeDtypeStruct(joined.shape[:4] + (width,), low),
            jax.ShapeDtypeStruct((number, heads, cells, cells), low),
        ],
        in_specs=[
            pl.BlockSpec(memory_space=pltpu.SMEM),
            pl.BlockSpec(bias.shape, lambda i, j: (0, 0, 0)),
            window_specs(is_joint, frames, 3 * width),
        ],
        out_specs=[
            window_specs(is_joint, frames, width),
            pl.BlockSpec((1, heads, cells, cells), fetch),
        ],
        compiler_params=params(48),
        cost_estimate=pl.CostEstimate(
            flops=16 * number * heads * cells * cells * HEAD_DIM,
            bytes_accessed=2 * number * heads * cells * cells,
            transcendentals=number * heads * cells * cells,
        ),
        name="attend_joint" if is_joint else "attend_spatial",
    )(count, bias, joined)


def attend_back(joined, grad, probs, is_joint):
    frames = joined.shape[1]
    number, heads, cells, _ = probs.shape
    width = heads * HEAD_DIM
    grid = (2, 2) if is_joint else (1, frames)
    fetch = lambda i, j: (i * grid[1] + j, 0, 0, 0)
    return pl.pallas_call(
        lambda *refs: attend_back_kernel(
            *refs, heads=heads, cells=cells, sides=joint_sides() if is_joint else spatial_sides()
        ),
        grid=grid,
        out_shape=[
            jax.ShapeDtypeStruct(joined.shape, low),
            jax.ShapeDtypeStruct((heads, 9, 64, 64), full),
        ],
        in_specs=[
            window_specs(is_joint, frames, 3 * width),
            window_specs(is_joint, frames, width),
            pl.BlockSpec((1, heads, cells, cells), fetch),
        ],
        out_specs=[
            window_specs(is_joint, frames, 3 * width),
            pl.BlockSpec((heads, 9, 64, 64), lambda i, j: (0, 0, 0, 0)),
        ],
        scratch_shapes=[pltpu.VMEM((heads, cells, cells), full)],
        compiler_params=params(56),
        cost_estimate=pl.CostEstimate(
            flops=32 * number * heads * cells * cells * HEAD_DIM,
            bytes_accessed=2 * number * heads * cells * cells,
            transcendentals=number * heads * cells * cells,
        ),
        name="attend_back_joint" if is_joint else "attend_back_spatial",
    )(joined, grad, probs)


def offset_hot():
    places = np.arange(WIN_T * WIN_T)
    rows = places[:, None] // WIN_T - places[None, :] // WIN_T + WIN_T - 1
    cols = places[:, None] % WIN_T - places[None, :] % WIN_T + WIN_T - 1
    spots = (rows * (2 * WIN_T - 1) + cols).reshape(-1).astype(np.int32)
    return jnp.arange((2 * WIN_T - 1) ** 2, dtype=jnp.int32)[:, None] == jnp.asarray(spots)[None]


def fast_local(
    latents,
    cotangent,
    frame_counts,
    band_ids,
    class_ids,
    time_table,
    class_table,
    ada_weight,
    ada_bias,
    qkv_weight,
    out_weight,
    up_weight,
    down_weight,
    spatial_bias,
    joint_bias,
):
    frames = latents.shape[1]
    model_width = latents.shape[4]
    heads = spatial_bias.shape[0]
    width = heads * HEAD_DIM
    col_width = ada_weight.shape[2]
    rows = frames * 128
    z, y, c, x = (lax.axis_index(name) for name in ("z", "y", "c", "x"))
    where = jnp.stack([z, y, x]).astype(jnp.int32)

    count = swap(frame_counts.astype(full)).astype(jnp.int32)

    def rearranged(values):
        shaped = values.reshape(frames, 8, 2, 8, model_width).transpose(0, 2, 1, 3, 4)
        return shaped.reshape(rows, model_width)

    qkv_rows = qkv_weight.reshape(2, -1, 3 * width)
    out_rows = out_weight.transpose(0, 2, 1)
    down_rows = down_weight.transpose(0, 2, 1)
    weights = []
    for k in range(2):
        weights.append(
            [
                gather_piece(swap(shard), where)
                for shard in (qkv_rows[k], out_rows[k], up_weight[k], down_rows[k])
            ]
        )

    band_hot = (band_ids[:, None] == jnp.arange(BANDS)[None, :]).astype(low)
    class_hot = (class_ids[:, None] == jnp.arange(CLASSES)[None, :]).astype(low)
    condition = jnp.dot(band_hot, time_table, preferred_element_type=full) + jnp.dot(
        class_hot, class_table, preferred_element_type=full
    )
    activity = jax.nn.silu(condition).astype(low)
    mod_part = jnp.einsum(
        "cd,bde->cbe", activity, ada_weight, preferred_element_type=full
    ) + ada_bias[None].astype(full)
    mine = lax.all_to_all(mod_part, ("z", "y", "x"), split_axis=0, concat_axis=0, tiled=True)
    theirs = flip(mine, "c")
    pair = jnp.where(c == 0, jnp.stack([mine, theirs]), jnp.stack([theirs, mine]))
    own_mod = (
        pair.reshape(2, 8, 2, 2, col_width)
        .transpose(3, 1, 0, 2, 4)
        .reshape(2, 6, 1, 1, model_width)
    )

    hot = offset_hot()
    wide = 2 * WIN_T - 1
    square = spatial_bias.reshape(heads, 2 * WIN_S - 1, 2 * WIN_S - 1)
    spatial_parts = jnp.stack(
        [
            square[:, 8 * a : 8 * a + wide, 8 * b : 8 * b + wide].reshape(heads, -1)
            for a in range(3)
            for b in range(3)
        ],
        axis=1,
    )
    parts = swap(jnp.concatenate([spatial_parts, joint_bias.reshape(heads, 9, -1)]))
    blocks = jnp.dot(
        parts.reshape(heads * 18, wide * wide), hot.astype(low), preferred_element_type=full
    ).astype(low)
    blocks = blocks.reshape(2, heads, 9, 64, 64)
    near = blocks[0].reshape(heads, 3, 3, 64, 64)
    near = jnp.where(c == 0, near, near[:, ::-1])
    spatial_matrix = jnp.concatenate(
        [
            jnp.concatenate(
                [
                    near[:, row // 2 - col // 2 + 1, row % 2 - col % 2 + 1]
                    for col in range(4)
                ],
                axis=2,
            )
            for row in range(4)
        ],
        axis=1,
    )
    joint_matrix = jnp.concatenate(
        [
            jnp.concatenate(
                [blocks[1][:, row - col + FRAMES - 1] for col in range(FRAMES)], axis=2
            )
            for row in range(FRAMES)
        ],
        axis=1,
    )

    mask = (jnp.arange(frames) < count[0]).astype(full)[:, None, None]
    tall = lambda values: values.reshape(frames, 128, model_width)
    flat = lambda values: values.reshape(rows, model_width)
    windowed = lambda values: values.reshape(2, frames, 2, 64, values.shape[-1])
    current = tall(rearranged(swap(latents))).astype(full)
    stored = []
    for k in range(2):
        w_qkv, w_out, w_up, w_down = weights[k]
        mod = own_mod[k]
        normed_one, inverse_one = normalize(current)
        moved_one = flat((normed_one * (1.0 + mod[1]) + mod[0]).astype(low))
        other_one = flip(moved_one, "c")
        (joined,) = both_times("plain", moved_one, other_one, w_qkv)
        joined = windowed(joined)
        mixed, probs = attend(count, joint_matrix if k else spatial_matrix, joined, k == 1)
        mixed = mixed.reshape(2, rows, width)
        branch_one = tall(branch_sum(mixed, w_out))
        after_attn = current + mask * mod[2] * branch_one
        normed_two, inverse_two = normalize(after_attn)
        moved_two = flat((normed_two * (1.0 + mod[4]) + mod[3]).astype(low))
        other_two = flip(moved_two, "c")
        act, slope = both_times("gelu", moved_two, other_two, w_up)
        branch_two = tall(branch_sum(act, w_down))
        current = after_attn + mask * mod[5] * branch_two
        stored.append(
            (
                normed_one,
                inverse_one,
                moved_one,
                other_one,
                joined,
                probs,
                mixed,
                branch_one,
                normed_two,
                inverse_two,
                moved_two,
                other_two,
                act,
                slope,
                branch_two,
            )
        )

    def restored(values):
        sent = swap(values.reshape(rows, model_width).astype(low)).astype(full)
        shaped = sent.reshape(frames, 2, 8, 8, model_width).transpose(0, 2, 1, 3, 4)
        return shaped.reshape(1, frames, 8, 16, model_width)

    output = restored(current)
    state = tall(rearranged(swap(cotangent))).astype(full)
    summed = lambda values: jnp.sum(values, axis=(0, 1))
    mod_grads = [None, None]
    grads = [None, None]
    bias_blocks = [None, None]
    for k in (1, 0):
        w_qkv, w_out, w_up, w_down = weights[k]
        mod = own_mod[k]
        (
            normed_one,
            inverse_one,
            moved_one,
            other_one,
            joined,
            probs,
            mixed,
            branch_one,
            normed_two,
            inverse_two,
            moved_two,
            other_two,
            act,
            slope,
            branch_two,
        ) = stored[k]
        gate_two = summed(mask * state * branch_two)
        grad_own = flat((mask * mod[5] * state).astype(low))
        grad_other = flip(grad_own, "c")
        (grad_hidden,) = both_times("slope", grad_own, grad_other, w_down, slope)
        down_parts = weight_grad(where, (grad_own, grad_other, act))
        grad_down = scatter_piece(down_parts, where)
        grad_moved = tall(branch_sum(grad_hidden, w_up))
        up_parts = weight_grad(where, (moved_two, other_two, grad_hidden))
        grad_up = scatter_piece(up_parts, where)
        shift_two = summed(grad_moved)
        scale_two = summed(grad_moved * normed_two)
        state = state + norm_back(grad_moved * (1.0 + mod[4]), normed_two, inverse_two)
        gate_one = summed(mask * state * branch_one)
        grad_own = flat((mask * mod[2] * state).astype(low))
        grad_other = flip(grad_own, "c")
        (grad_mixed,) = both_times("plain", grad_own, grad_other, w_out)
        back, bias_blocks[k] = attend_back(joined, windowed(grad_mixed), probs, k == 1)
        back = back.reshape(2, rows, 3 * width)
        out_parts = weight_grad(where, (grad_own, grad_other, mixed))
        grad_out = scatter_piece(out_parts, where)
        grad_moved = tall(branch_sum(back, w_qkv))
        qkv_parts = weight_grad(where, (moved_one, other_one, back))
        grad_qkv = scatter_piece(qkv_parts, where)
        shift_one = summed(grad_moved)
        scale_one = summed(grad_moved * normed_one)
        state = state + norm_back(grad_moved * (1.0 + mod[1]), normed_one, inverse_one)
        mod_grads[k] = jnp.stack([shift_one, scale_one, gate_one, shift_two, scale_two, gate_two])
        grads[k] = (grad_qkv, grad_out, grad_up, grad_down)

    grad_latents = restored(state)
    exact = lax.Precision.HIGHEST

    near = bias_blocks[0].reshape(heads, 3, 3, 64, 64)
    near = jnp.where(c == 0, near, near[:, ::-1]).reshape(heads, 9, 64, 64)
    tables = jnp.dot(
        jnp.stack([near, bias_blocks[1]]).reshape(heads * 18, 64 * 64),
        hot.astype(full).T,
        precision=exact,
    )
    for name in ("x", "y"):
        tables = tables + flip(tables, name)
    for step in (1, 2):
        tables = tables + z_trade(tables, step)
    tables = swap(tables).reshape(2, heads, 9, wide, wide)
    grad_joint = tables[1].reshape(heads, 9 * wide * wide)
    near = tables[0].reshape(heads, 3, 3, wide, wide)
    long = 2 * WIN_S - 1
    grad_spatial = 0.0
    for a in range(3):
        for b in range(3):
            grad_spatial = grad_spatial + jnp.pad(
                near[:, a, b],
                ((0, 0), (8 * a, long - wide - 8 * a), (8 * b, long - wide - 8 * b)),
            )
    grad_spatial = grad_spatial.reshape(heads, long * long)

    grad_mod = jnp.stack(mod_grads).reshape(2, 6 * model_width)
    grad_mod = grad_mod + flip(grad_mod, "c")
    ordered = grad_mod.reshape(2, 8, 2, 2, col_width).transpose(2, 1, 3, 0, 4)
    ordered = lax.dynamic_index_in_dim(ordered, c, 0, keepdims=False)
    cols = lax.all_to_all(
        ordered.reshape(16, 2, col_width),
        ("z", "y", "x"),
        split_axis=0,
        concat_axis=0,
        tiled=True,
    )
    grad_ada_weight = jnp.einsum("cd,cbe->bde", activity.astype(full), cols, precision=exact)
    grad_ada_bias = jnp.sum(cols, axis=0)
    grad_activity = jnp.einsum("cbe,bde->cd", cols, ada_weight.astype(full), precision=exact)
    for name in ("c", "x", "y"):
        grad_activity = grad_activity + flip(grad_activity, name)
    for step in (1, 2):
        grad_activity = grad_activity + z_trade(grad_activity, step)
    grad_condition = jax.vjp(jax.nn.silu, condition)[1](grad_activity)[0]
    grad_time = jnp.dot(band_hot.astype(full).T, grad_condition, precision=exact)
    grad_class = jnp.dot(class_hot.astype(full).T, grad_condition, precision=exact)

    stack = lambda at: jnp.stack([grads[0][at], grads[1][at]])
    return (
        output,
        grad_latents,
        grad_time,
        grad_class,
        grad_ada_weight,
        grad_ada_bias,
        stack(0).reshape(2, -1, 3, width),
        stack(1).transpose(0, 2, 1),
        stack(2),
        stack(3).transpose(0, 2, 1),
        grad_spatial,
        grad_joint,
    )


def solution(mesh):
    if mesh.shape["dp"] != 16 or mesh.shape["mp"] != 2:
        return solution_any(mesh)
    fine = Mesh(mesh.devices.reshape(4, 2, 2, 2), ("z", "y", "c", "x"))
    dp, mp = ("z", "y", "c"), "x"
    both = dp + (mp,)
    tokens = P(dp, None, mp, None, None)
    weight_specs = (
        P(None, None, both),
        P(None, both),
        P(None, dp, None, mp),
        P(None, mp, dp),
        P(None, dp, mp),
        P(None, mp, dp),
        P(mp, None),
        P(mp, None),
    )
    return jax.shard_map(
        fast_local,
        mesh=fine,
        in_specs=(tokens, tokens, P(dp), P(), P(), P(), P()) + weight_specs,
        out_specs=(tokens, tokens, P(), P()) + weight_specs,
        check_vma=False,
    )
```

```python
import jax
import jax.numpy as jnp
import numpy as np
from jax import lax
from jax.experimental import pallas as pl
from jax.experimental.pallas import tpu as pltpu
from jax.sharding import Mesh
from jax.sharding import PartitionSpec as P

HEAD_DIM = 64
CLASSES = 101
BANDS = 32
FRAMES = 5
WIN_S = 16
WIN_T = 8


epsilon = 1e-06
masked_score = -1e30


def spatial_table():
    places = np.arange(WIN_S * WIN_S)
    row_at = places // WIN_S
    col_at = places % WIN_S
    row_rel = row_at[:, None] - row_at[None, :] + WIN_S - 1
    col_rel = col_at[:, None] - col_at[None, :] + WIN_S - 1
    return (row_rel * (2 * WIN_S - 1) + col_rel).astype(np.int32)


def joint_table():
    places = np.arange(FRAMES * WIN_T * WIN_T)
    time_at = places // (WIN_T * WIN_T)
    row_at = places // WIN_T % WIN_T
    col_at = places % WIN_T
    time_rel = time_at[:, None] - time_at[None, :] + FRAMES - 1
    row_rel = row_at[:, None] - row_at[None, :] + WIN_T - 1
    col_rel = col_at[:, None] - col_at[None, :] + WIN_T - 1
    return ((time_rel * (2 * WIN_T - 1) + row_rel) * (2 * WIN_T - 1) + col_rel).astype(np.int32)


def to_windows(values, window, is_joint):
    clip_count, frames, side_cells, channels = (
        values.shape[0],
        values.shape[1],
        values.shape[2],
        values.shape[4],
    )
    per_side = side_cells // window
    if is_joint:
        shaped = values.reshape(clip_count, frames, per_side, window, per_side, window, channels)
        shaped = shaped.transpose(0, 2, 4, 1, 3, 5, 6)
        return shaped.reshape(clip_count * per_side * per_side, frames * window * window, channels)
    shaped = values.reshape(clip_count, frames, per_side, window, per_side, window, channels)
    shaped = shaped.transpose(0, 1, 2, 4, 3, 5, 6)
    return shaped.reshape(clip_count * frames * per_side * per_side, window * window, channels)


def from_windows(values, clip_count, frames, side_cells, window, is_joint):
    per_side = side_cells // window
    channels = values.shape[-1]
    if is_joint:
        shaped = values.reshape(clip_count, per_side, per_side, frames, window, window, channels)
        shaped = shaped.transpose(0, 3, 1, 4, 2, 5, 6)
    else:
        shaped = values.reshape(clip_count, frames, per_side, per_side, window, window, channels)
        shaped = shaped.transpose(0, 1, 2, 4, 3, 5, 6)
    return shaped.reshape(clip_count, frames, side_cells, side_cells, channels)


def normalize(values):
    center = values - jnp.mean(values, axis=-1, keepdims=True)
    spread = jnp.mean(center * center, axis=-1, keepdims=True)
    inverse = lax.rsqrt(spread + epsilon)
    return (center * inverse, inverse)


def norm_back(grad_normed, normed, inverse):
    first_mean = jnp.mean(grad_normed, axis=-1, keepdims=True)
    second_mean = jnp.mean(grad_normed * normed, axis=-1, keepdims=True)
    return inverse * (grad_normed - first_mean - normed * second_mean)


def exact_gelu(values):
    return jax.nn.gelu(values, approximate=False)


def gather_rows(values):
    return lax.all_gather(values, "mp", axis=2, tiled=True)


def sum_rows(values):
    return lax.psum_scatter(
        values.astype(jnp.bfloat16), "mp", scatter_dimension=2, tiled=True
    ).astype(jnp.float32)


def gather_grads(values):
    return lax.all_gather(values, "mp", axis=2, tiled=True)


def input_sums(values):
    return lax.psum_scatter(
        values.astype(jnp.bfloat16), "mp", scatter_dimension=2, tiled=True
    ).astype(jnp.float32)


def inputs_again(moved):
    return lax.all_gather(moved, "mp", axis=2, tiled=True)


def attention_scores(query_part, key_part, bias_matrix, key_valid):
    scores = (
        jnp.einsum("nqhe,nkhe->nhqk", query_part, key_part, preferred_element_type=jnp.float32)
        * HEAD_DIM ** (-0.5)
        + bias_matrix[None]
    )
    if key_valid is not None:
        scores = jnp.where(key_valid[:, None, None, :] > 0, scores, masked_score)
    return scores


def local(
    latents,
    cotangent,
    frame_counts,
    band_ids,
    class_ids,
    time_table,
    class_table,
    ada_weight,
    ada_bias,
    qkv_weight,
    out_weight,
    up_weight,
    down_weight,
    spatial_bias,
    joint_bias,
):
    clip_count = latents.shape[0]
    frames = latents.shape[1]
    side_cells = latents.shape[3]
    model_width = latents.shape[4]
    heads_local = spatial_bias.shape[0]
    local_width = heads_local * HEAD_DIM
    dp_count = lax.axis_size("dp")
    mp_count = lax.axis_size("mp")
    col_width = ada_weight.shape[2]
    band_hot = (band_ids[:, None] == jnp.arange(BANDS)[None, :]).astype(jnp.bfloat16)
    class_hot = (class_ids[:, None] == jnp.arange(CLASSES)[None, :]).astype(jnp.bfloat16)
    condition = jnp.dot(band_hot, time_table, preferred_element_type=jnp.float32) + jnp.dot(
        class_hot, class_table, preferred_element_type=jnp.float32
    )
    activity_low = jax.nn.silu(condition).astype(jnp.bfloat16)
    ada_cols, ada_bias_cols = (
        lax.all_gather(ada_weight, "mp", axis=2, tiled=True),
        lax.all_gather(ada_bias, "mp", axis=1, tiled=True),
    )
    mod_part = jnp.einsum(
        "cd,bde->bce", activity_low, ada_cols, preferred_element_type=jnp.float32
    ) + ada_bias_cols[:, None, :].astype(jnp.float32)
    modulation = lax.all_gather(mod_part, "dp", axis=2, tiled=True)
    first_clip = lax.axis_index("dp") * clip_count
    own_mod = lax.dynamic_slice_in_dim(modulation, first_clip, clip_count, 1).reshape(
        2, clip_count, 6, model_width
    )
    frame_valid = (jnp.arange(frames)[None, :] < frame_counts[:, None]).astype(jnp.float32)
    frame_mask = frame_valid[:, :, None, None, None]
    key_frames = np.arange(frames * WIN_T * WIN_T) // (WIN_T * WIN_T)
    joint_cells = key_frames.shape[0]
    per_side = side_cells // WIN_T
    key_valid = frame_valid[:, key_frames]
    key_valid = jnp.broadcast_to(
        key_valid[:, None, :], (clip_count, per_side * per_side, joint_cells)
    ).reshape(clip_count * per_side * per_side, joint_cells)
    w_qkv, w_out, w_up, w_down = (
        lax.all_gather(qkv_weight, "dp", axis=1, tiled=True),
        lax.all_gather(out_weight, "dp", axis=2, tiled=True),
        lax.all_gather(up_weight, "dp", axis=1, tiled=True),
        lax.all_gather(down_weight, "dp", axis=2, tiled=True),
    )
    spatial_index = spatial_table()
    joint_index = joint_table()
    spatial_matrix = spatial_bias.astype(jnp.float32)[:, spatial_index]
    joint_matrix = joint_bias.astype(jnp.float32)[:, joint_index]
    current = latents.astype(jnp.float32)
    stored = []
    for which_block in range(2):
        is_joint = which_block == 1
        window = WIN_T if is_joint else WIN_S
        bias_matrix = joint_matrix if is_joint else spatial_matrix
        mask_keys = key_valid if is_joint else None
        block_mod = own_mod[which_block][:, :, None, None, None, :]
        normed_one, inverse_one = normalize(current)
        moved_one = (normed_one * (1.0 + block_mod[:, 1]) + block_mod[:, 0]).astype(jnp.bfloat16)
        gathered_one = gather_rows(moved_one)
        projected = jnp.einsum(
            "cfyxd,dkh->cfyxkh",
            gathered_one,
            w_qkv[which_block],
            preferred_element_type=jnp.float32,
        ).astype(jnp.bfloat16)
        windows = to_windows(
            projected.reshape(clip_count, frames, side_cells, side_cells, 3 * local_width),
            window,
            is_joint,
        )
        windows = windows.reshape(windows.shape[0], windows.shape[1], 3, heads_local, HEAD_DIM)
        scores = attention_scores(windows[:, :, 0], windows[:, :, 1], bias_matrix, mask_keys)
        row_max = jnp.max(scores, axis=-1, keepdims=True)
        log_total = row_max + jnp.log(jnp.sum(jnp.exp(scores - row_max), axis=-1, keepdims=True))
        probs_low = jnp.exp(scores - log_total).astype(jnp.bfloat16)
        mixed_win = jnp.einsum(
            "nhqk,nkhe->nqhe", probs_low, windows[:, :, 2], preferred_element_type=jnp.float32
        ).astype(jnp.bfloat16)
        mixed_rows = from_windows(
            mixed_win.reshape(mixed_win.shape[0], mixed_win.shape[1], local_width),
            clip_count,
            frames,
            side_cells,
            window,
            is_joint,
        )
        branch_one = sum_rows(
            jnp.einsum(
                "cfyxk,kd->cfyxd",
                mixed_rows,
                w_out[which_block],
                preferred_element_type=jnp.float32,
            )
        )
        after_attn = current + frame_mask * block_mod[:, 2] * branch_one
        normed_two, inverse_two = normalize(after_attn)
        moved_two = (normed_two * (1.0 + block_mod[:, 4]) + block_mod[:, 3]).astype(jnp.bfloat16)
        gathered_two = gather_rows(moved_two)
        hidden = jnp.einsum(
            "cfyxd,dk->cfyxk", gathered_two, w_up[which_block], preferred_element_type=jnp.float32
        )
        activated = exact_gelu(hidden).astype(jnp.bfloat16)
        branch_two = sum_rows(
            jnp.einsum(
                "cfyxk,kd->cfyxd",
                activated,
                w_down[which_block],
                preferred_element_type=jnp.float32,
            )
        )
        current = after_attn + frame_mask * block_mod[:, 5] * branch_two
        stored.append(
            (
                normed_one,
                inverse_one,
                moved_one,
                gathered_one,
                windows,
                log_total,
                mixed_rows,
                branch_one,
                normed_two,
                inverse_two,
                moved_two,
                gathered_two,
                hidden,
                activated,
                branch_two,
            )
        )
    grad_state = cotangent.astype(jnp.float32)
    mod_grads = []
    qkv_grads = []
    out_grads = []
    up_grads = []
    down_grads = []
    table_parts = []
    for which_block in (1, 0):
        is_joint = which_block == 1
        window = WIN_T if is_joint else WIN_S
        bias_matrix = joint_matrix if is_joint else spatial_matrix
        mask_keys = key_valid if is_joint else None
        block_mod = own_mod[which_block][:, :, None, None, None, :]
        (
            normed_one,
            inverse_one,
            moved_one,
            gathered_one,
            windows,
            log_total,
            mixed_rows,
            branch_one,
            normed_two,
            inverse_two,
            moved_two,
            gathered_two,
            hidden,
            activated,
            branch_two,
        ) = stored[which_block]
        grad_gate_two = jnp.sum(frame_mask * grad_state * branch_two, axis=(1, 2, 3))
        grad_rows = gather_grads((frame_mask * block_mod[:, 5] * grad_state).astype(jnp.bfloat16))
        down_grads.append(
            jnp.einsum("cfyxk,cfyxd->kd", activated, grad_rows, preferred_element_type=jnp.float32)
        )
        grad_act = jnp.einsum(
            "cfyxd,kd->cfyxk", grad_rows, w_down[which_block], preferred_element_type=jnp.float32
        )
        grad_hidden = jax.vjp(exact_gelu, hidden)[1](grad_act)[0].astype(jnp.bfloat16)
        inputs_two = inputs_again(moved_two)
        up_grads.append(
            jnp.einsum(
                "cfyxd,cfyxk->dk", inputs_two, grad_hidden, preferred_element_type=jnp.float32
            )
        )
        grad_moved = input_sums(
            jnp.einsum(
                "cfyxk,dk->cfyxd",
                grad_hidden,
                w_up[which_block],
                preferred_element_type=jnp.float32,
            )
        )
        grad_shift_two = jnp.sum(grad_moved, axis=(1, 2, 3))
        grad_scale_two = jnp.sum(grad_moved * normed_two, axis=(1, 2, 3))
        grad_state = grad_state + norm_back(
            grad_moved * (1.0 + block_mod[:, 4]), normed_two, inverse_two
        )
        grad_gate_one = jnp.sum(frame_mask * grad_state * branch_one, axis=(1, 2, 3))
        grad_rows = gather_grads((frame_mask * block_mod[:, 2] * grad_state).astype(jnp.bfloat16))
        out_grads.append(
            jnp.einsum("cfyxk,cfyxd->kd", mixed_rows, grad_rows, preferred_element_type=jnp.float32)
        )
        grad_mixed = jnp.einsum(
            "cfyxd,kd->cfyxk", grad_rows, w_out[which_block], preferred_element_type=jnp.float32
        ).astype(jnp.bfloat16)
        grad_win = to_windows(grad_mixed, window, is_joint)
        grad_win = grad_win.reshape(grad_win.shape[0], grad_win.shape[1], heads_local, HEAD_DIM)
        query_part = windows[:, :, 0]
        key_part = windows[:, :, 1]
        value_part = windows[:, :, 2]
        probs_full = jnp.exp(
            attention_scores(query_part, key_part, bias_matrix, mask_keys) - log_total
        )
        grad_value = jnp.einsum(
            "nhqk,nqhe->nkhe",
            probs_full.astype(jnp.bfloat16),
            grad_win,
            preferred_element_type=jnp.float32,
        ).astype(jnp.bfloat16)
        grad_probs = jnp.einsum(
            "nqhe,nkhe->nhqk", grad_win, value_part, preferred_element_type=jnp.float32
        )
        row_dot = jnp.sum(probs_full * grad_probs, axis=-1, keepdims=True)
        grad_scores = (probs_full * (grad_probs - row_dot)).astype(jnp.bfloat16)
        bias_sum = jnp.sum(grad_scores.astype(jnp.float32), axis=0)
        if is_joint:
            table_parts.append(
                jnp.zeros((heads_local, joint_bias.shape[1]), jnp.float32)
                .at[:, joint_index]
                .add(bias_sum)
            )
        else:
            table_parts.append(
                jnp.zeros((heads_local, spatial_bias.shape[1]), jnp.float32)
                .at[:, spatial_index]
                .add(bias_sum)
            )
        grad_query = (
            jnp.einsum("nhqk,nkhe->nqhe", grad_scores, key_part, preferred_element_type=jnp.float32)
            * HEAD_DIM ** (-0.5)
        ).astype(jnp.bfloat16)
        grad_key = (
            jnp.einsum(
                "nhqk,nqhe->nkhe", grad_scores, query_part, preferred_element_type=jnp.float32
            )
            * HEAD_DIM ** (-0.5)
        ).astype(jnp.bfloat16)
        stacked = jnp.stack([grad_query, grad_key, grad_value], axis=2).reshape(
            grad_query.shape[0], grad_query.shape[1], 3 * local_width
        )
        grad_projected = from_windows(
            stacked, clip_count, frames, side_cells, window, is_joint
        ).reshape(clip_count, frames, side_cells, side_cells, 3, local_width)
        inputs_one = inputs_again(moved_one)
        qkv_grads.append(
            jnp.einsum(
                "cfyxd,cfyxkh->dkh", inputs_one, grad_projected, preferred_element_type=jnp.float32
            )
        )
        grad_moved = input_sums(
            jnp.einsum(
                "cfyxkh,dkh->cfyxd",
                grad_projected,
                w_qkv[which_block],
                preferred_element_type=jnp.float32,
            )
        )
        grad_shift_one = jnp.sum(grad_moved, axis=(1, 2, 3))
        grad_scale_one = jnp.sum(grad_moved * normed_one, axis=(1, 2, 3))
        grad_state = grad_state + norm_back(
            grad_moved * (1.0 + block_mod[:, 1]), normed_one, inverse_one
        )
        mod_grads.append(
            jnp.stack(
                [
                    grad_shift_one,
                    grad_scale_one,
                    grad_gate_one,
                    grad_shift_two,
                    grad_scale_two,
                    grad_gate_two,
                ],
                axis=1,
            )
        )
    grad_mod = jnp.stack(mod_grads[::-1], axis=0).reshape(2, clip_count, 6 * model_width)
    ordered = (
        grad_mod.reshape(2, clip_count, dp_count, mp_count, col_width)
        .transpose(0, 1, 3, 2, 4)
        .reshape(2, clip_count, 6 * model_width)
    )
    summed_cols = lax.psum_scatter(ordered, "mp", scatter_dimension=2, tiled=True)
    grad_mod_cols = lax.all_to_all(summed_cols, "dp", split_axis=2, concat_axis=1, tiled=True)
    grad_ada_weight = jnp.einsum(
        "cd,bce->bde",
        activity_low.astype(jnp.float32),
        grad_mod_cols,
        precision=lax.Precision.HIGHEST,
    )
    grad_ada_bias = jnp.sum(grad_mod_cols, axis=1)
    grad_mod_block = lax.all_gather(grad_mod_cols, "mp", axis=2, tiled=True)
    activity_part = jnp.einsum(
        "bce,bde->cd", grad_mod_block, ada_cols.astype(jnp.float32), precision=lax.Precision.HIGHEST
    )
    grad_activity = lax.psum(activity_part, "dp")
    grad_condition = jax.vjp(jax.nn.silu, condition)[1](grad_activity)[0]
    grad_time = jnp.dot(
        band_hot.astype(jnp.float32).T, grad_condition, precision=lax.Precision.HIGHEST
    )
    grad_class = jnp.dot(
        class_hot.astype(jnp.float32).T, grad_condition, precision=lax.Precision.HIGHEST
    )
    grad_spatial, grad_joint = lax.psum((table_parts[1], table_parts[0]), "dp")
    grad_qkv, grad_out, grad_up, grad_down = (
        lax.psum_scatter(jnp.stack(qkv_grads[::-1], axis=0), "dp", scatter_dimension=1, tiled=True),
        lax.psum_scatter(jnp.stack(out_grads[::-1], axis=0), "dp", scatter_dimension=2, tiled=True),
        lax.psum_scatter(jnp.stack(up_grads[::-1], axis=0), "dp", scatter_dimension=1, tiled=True),
        lax.psum_scatter(
            jnp.stack(down_grads[::-1], axis=0), "dp", scatter_dimension=2, tiled=True
        ),
    )
    return (
        current,
        grad_state,
        grad_time,
        grad_class,
        grad_ada_weight,
        grad_ada_bias,
        grad_qkv,
        grad_out,
        grad_up,
        grad_down,
        grad_spatial,
        grad_joint,
    )


def solution_any(mesh):
    placed = (
        P("dp", None, "mp", None, None),
        P("dp", None, "mp", None, None),
        P("dp"),
        P(),
        P(),
        P(),
        P(),
        P(None, None, ("dp", "mp")),
        P(None, ("dp", "mp")),
        P(None, "dp", None, "mp"),
        P(None, "mp", "dp"),
        P(None, "dp", "mp"),
        P(None, "mp", "dp"),
        P("mp", None),
        P("mp", None),
    )
    return jax.shard_map(
        local,
        mesh=mesh,
        in_specs=placed,
        out_specs=(
            P("dp", None, "mp", None, None),
            P("dp", None, "mp", None, None),
            P(),
            P(),
            P(None, None, ("dp", "mp")),
            P(None, ("dp", "mp")),
            P(None, "dp", None, "mp"),
            P(None, "mp", "dp"),
            P(None, "dp", "mp"),
            P(None, "mp", "dp"),
            P("mp", None),
            P("mp", None),
        ),
        check_vma=False,
    )


low = jnp.bfloat16
full = jnp.float32
HALF_ROOT = 0.7071067811865476
PHI_AT_ZERO = 0.3989422804014327
MIB = 1024 * 1024


def flip(values, axis):
    return lax.ppermute(values, axis, [(0, 1), (1, 0)])


def z_trade(values, step):
    return lax.ppermute(values, "z", [(place, place ^ step) for place in range(4)])


def swap(values):
    return lax.ppermute(values, ("c", "x"), [(0, 0), (1, 2), (2, 1), (3, 3)])


def shape_of(dims, dtype=low):
    return jax.ShapeDtypeStruct(tuple(dims), dtype)


def whole(array):
    zeros = (0,) * len(array.shape)
    return pl.BlockSpec(tuple(array.shape), lambda *at: zeros)


class Chain:
    def __init__(self, info):
        self.info = info
        self.last = []
        self.pending = []

    def wait(self, *values):
        self.pending += values

    def run(self, name, kernel, args, in_specs, outs, out_specs, grid=(1,), scratch=(), mib=48, waits=()):
        count = len(args)
        unread = self.last + self.pending + list(waits)
        self.pending = []
        held = len(unread)

        def body(*refs):
            kernel(*refs[: 1 + count], *refs[1 + count + held :])

        results = pl.pallas_call(
            body,
            grid_spec=pltpu.PrefetchScalarGridSpec(
                num_scalar_prefetch=1,
                grid=grid,
                in_specs=list(in_specs) + [pl.BlockSpec(memory_space=pl.ANY)] * held,
                out_specs=list(out_specs),
                scratch_shapes=list(scratch),
            ),
            out_shape=list(outs),
            compiler_params=pltpu.CompilerParams(vmem_limit_bytes=mib * MIB),
            cost_estimate=pl.CostEstimate(flops=1, bytes_accessed=1, transcendentals=0),
            name=name,
        )(self.info, *args, *unread)
        self.last = [results[0]]
        return results


def cut_kernel(info, packed, *outs):
    start = 0
    for out in outs:
        width = out.shape[1]
        out[...] = packed[:, start : start + width]
        start += width


PIECE = 2048
PIECE_TILE = 512


def tile_spec(count, rows=64):
    return pl.BlockSpec((count, rows, PIECE_TILE), lambda j, info: (0, 0, j))


def flat_spec(rows=64):
    return pl.BlockSpec((rows, PIECE_TILE), lambda j, info: (0, j))


class Gather:
    def __init__(self, chain, shards):
        self.chain = chain
        self.shards = shards
        self.near = {}
        self.sent = {}
        self.got = {}
        self.step_at = 0

    def over_z(self, at):
        self.near[at] = [z_trade(self.shards[at], k) for k in (1, 2, 3)]

    def step(self):
        at = self.step_at
        self.step_at += 1
        own = at < len(self.shards)
        far = at > 0
        args, specs = [], []
        if own:
            args += [self.shards[at]] + self.near[at]
            specs += [flat_spec()] * 4
        start = 0
        if far:
            got_x, got_y = self.got[at - 1]
            start = got_x.shape[0] - 4
            args += [got_x, got_y]
            specs += [tile_spec(got_x.shape[0])] * 2

        def kernel(info, *refs):
            to_x, to_y = refs[-2:]
            if own:
                for k in range(4):
                    to_x[(2 if far else 0) + k] = refs[k][...]
                    to_y[(2 if far else 0) + k] = refs[k][...]
            if far:
                from_x, from_y = refs[-4:-2]
                to_x[0:2] = from_y[start : start + 2]
                to_y[0:2] = from_x[start + 2 : start + 4]

        count = (2 if far else 0) + (4 if own else 0)
        outs = [shape_of((count, 64, PIECE))] * 2
        to_x, to_y = self.chain.run(
            "gather_step",
            kernel,
            args,
            specs,
            outs,
            [tile_spec(count)] * 2,
            grid=(PIECE // PIECE_TILE,),
        )
        self.sent[at] = to_x
        self.got[at] = (flip(to_x, "x"), flip(to_y, "y"))

    def place(self, at, widths):
        def kernel(info, own, from_x, from_y, far_lo, far_hi, *outs):
            k = pl.program_id(0)
            place = info[1] * 2 + info[2]

            def put(rel, block):
                start = 0
                for out in outs:
                    width = out.shape[3]
                    out[0, place ^ rel] = block[0, :, start : start + width]
                    start += width

            put(0, own)
            put(1, from_x)
            put(2, from_y)

            @pl.when(k < 2)
            def _():
                put(3, far_lo)

            @pl.when(k >= 2)
            def _():
                put(3, far_hi)

        got_x, got_y = self.got[at]
        start = got_x.shape[0] - 4
        block = (1, 64, PIECE)
        quad = pl.BlockSpec(block, lambda k, info: (k + start, 0, 0))
        results = self.chain.run(
            "place_weights",
            kernel,
            [self.sent[at], got_x, got_y, *self.got[at + 1]],
            [
                quad,
                quad,
                quad,
                pl.BlockSpec(block, lambda k, info: (jnp.minimum(k, 1), 0, 0)),
                pl.BlockSpec(block, lambda k, info: (jnp.maximum(k - 2, 0), 0, 0)),
            ],
            [shape_of((4, 4, 64, w)) for w in widths],
            [pl.BlockSpec((1, 4, 64, w), lambda k, info: (info[0] ^ k, 0, 0, 0)) for w in widths],
            grid=(4,),
        )
        return [a.reshape(16 * 64, a.shape[3]) for a in results]


def weight_grad_kernel(info, *refs, pairs, widths):
    lhs = refs[: 4 * pairs]
    rhs = refs[4 * pairs : 5 * pairs]
    near, to_x, to_y, far_lo, far_hi, held = refs[5 * pairs :]
    z = pl.program_id(0)
    place = info[1] * 2 + info[2]
    start = 0
    for at in range(pairs):
        halves = []
        for half in range(2):
            spot = 4 * at + 2 * half
            halves.append(jnp.concatenate([lhs[spot][...].T, lhs[spot + 1][...].T], axis=1))
        for begin in range(0, widths[at], 512):
            cols = slice(begin, begin + 512)
            block = jnp.dot(
                halves[0], rhs[at][0, :, cols], preferred_element_type=full
            ) + jnp.dot(halves[1], rhs[at][1, :, cols], preferred_element_type=full)
            held[:, start + begin : start + begin + 512] = block.astype(low)
        start += widths[at]

    def part(rel):
        return held[pl.ds(pl.multiple_of((place ^ rel) * 64, 64), 64), :]

    near[0] = part(0)
    to_x[0] = part(1)
    to_y[0] = part(2)

    @pl.when(z < 2)
    def _():
        far_lo[0] = part(3)

    @pl.when(z >= 2)
    def _():
        far_hi[0] = part(3)


class Scatter:
    def __init__(self, chain):
        self.chain = chain
        self.parts = []
        self.got = None
        self.held = None
        self.done = []
        self.step_at = 0

    def weight_grad(self, *items):
        pairs = len(items)
        widths = tuple(item[2].shape[2] for item in items)
        rows, features = items[0][0][0].shape
        tile = features // 4
        quads = shape_of((4, 64, PIECE))
        twos = shape_of((2, 64, PIECE))
        lhs_spec = pl.BlockSpec((rows, tile), lambda z, info: (0, z))
        block = (1, 64, PIECE)
        self.parts.append(
            self.chain.run(
                "weight_grad",
                lambda *refs: weight_grad_kernel(*refs, pairs=pairs, widths=widths),
                [part for item in items for pair in item[:2] for part in pair]
                + [item[2] for item in items],
                [lhs_spec] * (4 * pairs)
                + [pl.BlockSpec((2, 2 * rows, w), lambda z, info: (0, 0, 0)) for w in widths],
                [quads, quads, quads, twos, twos],
                [pl.BlockSpec(block, lambda z, info: (z, 0, 0))] * 3
                + [
                    pl.BlockSpec(block, lambda z, info: (jnp.minimum(z, 1), 0, 0)),
                    pl.BlockSpec(block, lambda z, info: (jnp.maximum(z - 2, 0), 0, 0)),
                ],
                grid=(4,),
                scratch=[pltpu.VMEM((tile, PIECE), low)],
                mib=56,
            )
        )
        if len(self.parts) == 1:
            self.got = (flip(self.parts[0][3], "x"), flip(self.parts[0][4], "y"))

    def step(self, total):
        at = self.step_at
        self.step_at += 1
        far = at + 1 < total
        mid = at < total
        near = 0 <= at - 1 < total
        last = 0 <= at - 2 < total
        args, specs = [], []

        def put(array, spec):
            args.append(array)
            specs.append(spec)
            return len(args) - 1

        names = {}
        if far:
            names["far_lo"] = put(self.parts[at + 1][3], tile_spec(2))
            names["far_hi"] = put(self.parts[at + 1][4], tile_spec(2))
        if mid:
            names["to_x"] = put(self.parts[at][1], tile_spec(4))
            names["to_y"] = put(self.parts[at][2], tile_spec(4))
        if near:
            names["near"] = put(self.parts[at - 1][0], tile_spec(4))
        if mid or near:
            count = self.got[0].shape[0]
            names["got_x"] = put(self.got[0], tile_spec(count))
            names["got_y"] = put(self.got[1], tile_spec(count))
        if last:
            for k in range(4):
                names["held%d" % k] = put(self.held[k], flat_spec())
        outs, out_specs = [], []
        sent = (2 if far else 0) + (4 if mid else 0)
        if mid:
            outs += [shape_of((sent, 64, PIECE))] * 2
            out_specs += [tile_spec(sent)] * 2
        if near:
            outs += [shape_of((64, PIECE), full)] + [shape_of((64, PIECE))] * 3
            out_specs += [flat_spec()] * 4
        if last:
            outs.append(shape_of((64, PIECE)))
            out_specs.append(flat_spec())
        number = len(args)

        def kernel(info, *refs):
            out = list(refs[number:])
            get = {name: refs[spot] for name, spot in names.items()}
            if mid:
                out_x, out_y = out[:2]
                del out[:2]
                start = 0
                if far:
                    out_x[0:2] = get["far_lo"][...]
                    out_y[0:2] = get["far_hi"][...]
                    start = 2
                for k in range(4):
                    part_x = get["to_x"][k]
                    part_y = get["to_y"][k]
                    if k < 2:
                        part_y = (part_y.astype(full) + get["got_x"][k].astype(full)).astype(low)
                    else:
                        part_x = (
                            part_x.astype(full) + get["got_y"][k - 2].astype(full)
                        ).astype(low)
                    out_x[start + k] = part_x
                    out_y[start + k] = part_y
            if near:
                start = get["got_x"].shape[0] - 4
                for k in range(4):
                    spot = info[0] ^ k
                    value = get["near"][spot].astype(full)
                    value = value + get["got_x"][start + spot].astype(full)
                    value = value + get["got_y"][start + spot].astype(full)
                    out[k][...] = value.astype(out[k].dtype)
                del out[:4]
            if last:
                value = get["held0"][...]
                for k in (1, 2, 3):
                    value = value + get["held%d" % k][...].astype(full)
                out[0][...] = value.astype(low)

        results = list(
            self.chain.run(
                "scatter_step", kernel, args, specs, outs, out_specs, grid=(PIECE // PIECE_TILE,)
            )
        )
        if mid:
            self.got = (flip(results[0], "x"), flip(results[1], "y"))
            del results[:2]
        if near:
            self.held = [results[0]] + [z_trade(results[k], k) for k in (1, 2, 3)]
            del results[:4]
        if last:
            self.done.append(results[0])


def add_all(chain, *values):
    def kernel(info, *refs):
        total = refs[0][...]
        for other in refs[1:-1]:
            total = total + other[...]
        refs[-1][...] = total

    out = shape_of(values[0].shape, full)
    (result,) = chain.run(
        "add_all", kernel, list(values), [whole(a) for a in values], [out], [whole(out)]
    )
    return result


def join_pieces(chain, pieces):
    def kernel(info, *refs):
        for at, piece in enumerate(refs[:-1]):
            refs[-1][:, at * PIECE : (at + 1) * PIECE] = piece[...]

    out = shape_of((64, PIECE * len(pieces)))
    (result,) = chain.run(
        "join_pieces", kernel, pieces, [whole(a) for a in pieces], [out], [whole(out)]
    )
    return result


def gelu_and_slope(values):
    bell = jnp.exp(-0.5 * values * values)
    t = 1.0 / (1.0 + (0.3275911 * HALF_ROOT) * jnp.abs(values))
    poly = t * (
        0.254829592
        + t * (-0.284496736 + t * (1.421413741 + t * (-1.453152027 + t * 1.061405429)))
    )
    tail = 0.5 * poly * bell
    phi = jnp.where(values >= 0, 1.0 - tail, tail)
    return values * phi, phi + (PHI_AT_ZERO * values) * bell


ROW_TILE = 320


def flip_rows(pair):
    return tuple(flip(part, "c") for part in pair)


def both_kernel(info, *refs, kind):
    weight = refs[4][...]
    for part in range(4):
        half = part // 2
        rows = slice(part % 2 * ROW_TILE, (part % 2 + 1) * ROW_TILE)
        product = jnp.dot(refs[part][...], weight, preferred_element_type=full)
        if kind == "gelu":
            act, slope = gelu_and_slope(product)
            refs[5][half, rows] = act.astype(low)
            refs[6][half, rows] = slope.astype(low)
        elif kind == "slope":
            refs[6][half, rows] = (product * refs[5][half, rows].astype(full)).astype(low)
        else:
            refs[5][half, rows] = product.astype(low)


def both_times(chain, kind, own, other, weight, slope=None, waits=()):
    depth = weight.shape[0]
    rows = 2 * ROW_TILE
    width = weight.shape[1]
    tile = 256 if kind == "gelu" else 512
    out_spec = pl.BlockSpec((2, rows, tile), lambda j, info: (0, 0, j))
    extra = [] if slope is None else [slope]
    count = 2 if kind == "gelu" else 1
    return chain.run(
        "both_" + kind,
        lambda *refs: both_kernel(*refs, kind=kind),
        [*own, *other, weight] + extra,
        [whole(part) for part in (*own, *other)]
        + [pl.BlockSpec((depth, tile), lambda j, info: (0, j))]
        + [out_spec] * len(extra),
        [shape_of((2, rows, width))] * count,
        [out_spec] * count,
        grid=(width // tile,),
        waits=waits,
    )


def times_back(values, weight):
    return lax.dot_general(
        values, weight, (((1,), (1,)), ((), ())), preferred_element_type=full
    ).astype(low)


def other_rows(chain, values, weight):
    rows, depth = values.shape[1:]
    width = weight.shape[0]
    tile = 256

    def kernel(info, rows_in, weight_in, first, second):
        result = times_back(rows_in[0], weight_in[...])
        first[...] = result[:ROW_TILE]
        second[...] = result[ROW_TILE:]

    half = pl.BlockSpec((ROW_TILE, tile), lambda j, info: (0, j))
    results = chain.run(
        "other_rows",
        kernel,
        [values, weight],
        [
            pl.BlockSpec((1, rows, depth), lambda j, info: (1, 0, 0)),
            pl.BlockSpec((tile, depth), lambda j, info: (j, 0)),
        ],
        [shape_of((ROW_TILE, width))] * 2,
        [half] * 2,
        grid=(width // tile,),
    )
    return flip_rows(results)


def put_half(pair, values):
    @pl.when(pl.program_id(0) == 0)
    def _():
        pair[0][...] = values

    @pl.when(pl.program_id(0) == 1)
    def _():
        pair[1][...] = values


def get_half(pair):
    return jnp.where(pl.program_id(0) == 0, pair[0][...].astype(full), pair[1][...].astype(full))


def shown_rows(info):
    first = pl.program_id(0) * ROW_TILE
    row = first + lax.broadcasted_iota(jnp.int32, (ROW_TILE, 1), 0)
    return (row < info[3] * 128).astype(full)


def norm_and_move(values, shift, scale):
    center = values - jnp.mean(values, axis=-1, keepdims=True)
    spread = jnp.mean(center * center, axis=-1, keepdims=True)
    inverse = lax.rsqrt(spread + epsilon)
    normed = center * inverse
    return normed.astype(low), inverse, (normed * (1.0 + scale) + shift).astype(low)


def row_specs(model_width):
    tall = pl.BlockSpec((ROW_TILE, model_width), lambda i, info: (i, 0))
    thin = pl.BlockSpec((ROW_TILE, 1), lambda i, info: (i, 0))
    return tall, thin


def first_norm(chain, current, rows_of):
    rows, model_width = current.shape
    tall, thin = row_specs(model_width)

    def kernel(info, values, given, normed, inverse, *moved):
        normed[...], inverse[...], result = norm_and_move(
            values[...].astype(full), given[0:1], given[1:2]
        )
        put_half(moved, result)

    half = shape_of((ROW_TILE, model_width))
    normed, inverse, *moved = chain.run(
        "first_norm",
        kernel,
        [current, rows_of],
        [tall, whole(rows_of)],
        [shape_of(current.shape), shape_of((rows, 1), full), half, half],
        [tall, thin, whole(half), whole(half)],
        grid=(rows // ROW_TILE,),
    )
    return normed, inverse, moved


def forward_step(chain, values, weight, away, current, rows_of, last, waits=()):
    rows, model_width = current.shape
    depth = values.shape[2]
    tall, thin = row_specs(model_width)

    def kernel(info, own, weight_in, first, second, current_in, given, after, branch_out, *rest):
        branch = times_back(own[0], weight_in[...]).astype(full) + get_half((first, second))
        total = current_in[...].astype(full) + shown_rows(info) * given[0:1] * branch
        after[...] = total.astype(after.dtype)
        branch_out[...] = branch.astype(low)
        if not last:
            normed, inverse, *moved = rest
            normed[...], inverse[...], result = norm_and_move(total, given[1:2], given[2:3])
            put_half(moved, result)

    outs = [shape_of(current.shape, low if last else full), shape_of(current.shape)]
    specs = [tall, tall]
    if not last:
        half = shape_of((ROW_TILE, model_width))
        outs += [shape_of(current.shape), shape_of((rows, 1), full), half, half]
        specs += [tall, thin, whole(half), whole(half)]
    results = chain.run(
        "forward_step",
        kernel,
        [values, weight, *away, current, rows_of],
        [
            pl.BlockSpec((1, ROW_TILE, depth), lambda i, info: (0, i, 0)),
            whole(weight),
            whole(away[0]),
            whole(away[1]),
            tall,
            whole(rows_of),
        ],
        outs,
        specs,
        grid=(rows // ROW_TILE,),
        waits=waits,
    )
    return results if last else (*results[:4], results[4:])


def add_rows(out, at, values):
    total = jnp.sum(values, axis=0, keepdims=True)

    @pl.when(pl.program_id(0) == 0)
    def _():
        out[at : at + 1] = total

    @pl.when(pl.program_id(0) > 0)
    def _():
        out[at : at + 1] += total


def first_back(chain, state, branch, gate):
    rows, model_width = state.shape
    tall, _ = row_specs(model_width)

    def kernel(info, state_in, branch_in, gate_in, first, second, sums):
        values = state_in[...].astype(full) * shown_rows(info)
        put_half((first, second), (values * gate_in[...]).astype(low))
        add_rows(sums, 0, values * branch_in[...].astype(full))

    sums = shape_of((8, model_width), full)
    half = shape_of((ROW_TILE, model_width))
    first, second, sums = chain.run(
        "first_back",
        kernel,
        [state, branch, gate],
        [tall, tall, whole(gate)],
        [half, half, sums],
        [whole(half), whole(half), whole(sums)],
        grid=(rows // ROW_TILE,),
    )
    return (first, second), sums


def backward_step(chain, values, weight, away, normed, inverse, state, rows_of, branch):
    rows, model_width = state.shape
    depth = values.shape[2]
    tall, thin = row_specs(model_width)
    last = branch is None

    def kernel(
        info, own, weight_in, first, second, normed_in, inverse_in, state_in, given, *rest
    ):
        grad = times_back(own[0], weight_in[...]).astype(full) + get_half((first, second))
        normal = normed_in[...].astype(full)
        moved = grad * (1.0 + given[0:1])
        first_mean = jnp.mean(moved, axis=-1, keepdims=True)
        second_mean = jnp.mean(moved * normal, axis=-1, keepdims=True)
        total = state_in[...].astype(full) + inverse_in[...] * (
            moved - first_mean - normal * second_mean
        )
        if last:
            state_out, sums = rest
        else:
            branch_in, state_out, sums, *sent = rest
        state_out[...] = total.astype(state_out.dtype)
        add_rows(sums, 0, grad)
        add_rows(sums, 1, grad * normal)
        if not last:
            shown = total * shown_rows(info)
            put_half(sent, (shown * given[1:2]).astype(low))
            add_rows(sums, 2, shown * branch_in[...].astype(full))

    sums = shape_of((8, model_width), full)
    outs = [shape_of(state.shape, low if last else full), sums]
    specs = [tall, whole(sums)]
    if not last:
        half = shape_of((ROW_TILE, model_width))
        outs += [half, half]
        specs += [whole(half)] * 2
    extra = [] if last else [branch]
    results = chain.run(
        "backward_step",
        kernel,
        [values, weight, *away, normed, inverse, state, rows_of] + extra,
        [
            pl.BlockSpec((1, ROW_TILE, depth), lambda i, info: (0, i, 0)),
            whole(weight),
            whole(away[0]),
            whole(away[1]),
            tall,
            thin,
            tall,
            whole(rows_of),
        ]
        + [tall] * len(extra),
        outs,
        specs,
        grid=(rows // ROW_TILE,),
    )
    return results if last else (*results[:2], results[2:])


def attend_kernel(info, blocks, joined, mixed, probs, bias, *, heads, cells, masked, sides):
    width = heads * HEAD_DIM

    @pl.when((pl.program_id(0) == 0) & (pl.program_id(1) == 0))
    def _():
        for h in range(heads):
            for place, spots in enumerate(sides):
                block = blocks[h, place]
                for row, col in spots:
                    bias[h, row * 64 : row * 64 + 64, col * 64 : col * 64 + 64] = block

    values = joined[...].reshape(cells, 3 * width)
    lead = mixed.shape
    if masked:
        column = lax.broadcasted_iota(jnp.int32, (1, cells), 1)
        shown = column < info[3] * (WIN_T * WIN_T)
    outs = []
    for h in range(heads):
        cols = slice(h * HEAD_DIM, (h + 1) * HEAD_DIM)
        query = values[:, cols]
        key = values[:, width + h * HEAD_DIM : width + (h + 1) * HEAD_DIM]
        value = values[:, 2 * width + h * HEAD_DIM : 2 * width + (h + 1) * HEAD_DIM]
        scores = lax.dot_general(
            query, key, (((1,), (1,)), ((), ())), preferred_element_type=full
        ) * HEAD_DIM ** (-0.5) + bias[h].astype(full)
        if masked:
            scores = jnp.where(shown, scores, masked_score)
        weights = jnp.exp(scores - jnp.max(scores, axis=-1, keepdims=True))
        share = (weights * (1.0 / jnp.sum(weights, axis=-1, keepdims=True))).astype(low)
        probs[0, h] = share
        outs.append(jnp.dot(share, value, preferred_element_type=full).astype(low))
    mixed[...] = jnp.concatenate(outs, axis=1).reshape(lead)


def attend_back_kernel(info, joined, grad, probs, back, bias_out, total, *, heads, cells, sides):
    step = pl.program_id(0) * pl.num_programs(1) + pl.program_id(1)
    width = heads * HEAD_DIM
    values = joined[...].reshape(cells, 3 * width)
    grads = grad[...].reshape(cells, width)
    grads_t = grads.astype(full).T.astype(low)
    queries_t = values[:, :width].astype(full).T.astype(low)
    queries, keys_t, values_t = [], [], []

    @pl.when(step == 0)
    def _():
        total[...] = jnp.zeros(total.shape, full)

    for h in range(heads):
        cols = slice(h * HEAD_DIM, (h + 1) * HEAD_DIM)
        key = values[:, width + h * HEAD_DIM : width + (h + 1) * HEAD_DIM]
        value = values[:, 2 * width + h * HEAD_DIM : 2 * width + (h + 1) * HEAD_DIM]
        share = probs[0, h]
        values_t.append(jnp.dot(grads_t[cols], share, preferred_element_type=full).astype(low))
        grad_share = lax.dot_general(
            grads[:, cols], value, (((1,), (1,)), ((), ())), preferred_element_type=full
        )
        share_full = share.astype(full)
        product = share_full * grad_share
        row_dot = jnp.sum(product, axis=-1, keepdims=True)
        grad_scores = (product - share_full * row_dot).astype(low)
        total[h] += grad_scores.astype(full)
        queries.append(
            (jnp.dot(grad_scores, key, preferred_element_type=full) * HEAD_DIM ** (-0.5)).astype(
                low
            )
        )
        keys_t.append(
            (
                jnp.dot(queries_t[cols], grad_scores, preferred_element_type=full)
                * HEAD_DIM ** (-0.5)
            ).astype(low)
        )
    key_grads = jnp.concatenate(keys_t, axis=0).astype(full).T.astype(low)
    value_grads = jnp.concatenate(values_t, axis=0).astype(full).T.astype(low)
    back[...] = jnp.concatenate(queries + [key_grads, value_grads], axis=1).reshape(back.shape)

    @pl.when(step == pl.num_programs(0) * pl.num_programs(1) - 1)
    def _():
        for h in range(heads):
            for place, spots in enumerate(sides):
                part = None
                for row, col in spots:
                    block = total[h, row * 64 : row * 64 + 64, :][:, col * 64 : col * 64 + 64]
                    part = block if part is None else part + block
                bias_out[h, place] = part


def spatial_sides():
    sides = [[] for _ in range(9)]
    for row in range(4):
        for col in range(4):
            place = (row // 2 - col // 2 + 1) * 3 + (row % 2 - col % 2 + 1)
            sides[place].append((row, col))
    return sides


def joint_sides():
    sides = [[] for _ in range(2 * FRAMES - 1)]
    for row in range(FRAMES):
        for col in range(FRAMES):
            sides[row - col + FRAMES - 1].append((row, col))
    return sides


def window_specs(is_joint, frames, width):
    if is_joint:
        shape, at = (1, frames, 1, 64, width), lambda i, j, info: (i, 0, j, 0, 0)
    else:
        shape, at = (2, 1, 2, 64, width), lambda i, j, info: (0, j, 0, 0, 0)
    return pl.BlockSpec(shape, at)


def attend(chain, blocks, joined, is_joint):
    frames = joined.shape[1]
    heads = blocks.shape[0]
    width = heads * HEAD_DIM
    grid = (2, 2) if is_joint else (1, frames)
    cells = 64 * frames if is_joint else 256
    number = grid[0] * grid[1]
    sides = joint_sides() if is_joint else spatial_sides()
    fetch = lambda i, j, info: (i * grid[1] + j, 0, 0, 0)
    return chain.run(
        "attend_joint" if is_joint else "attend_spatial",
        lambda *refs: attend_kernel(
            *refs, heads=heads, cells=cells, masked=is_joint, sides=sides
        ),
        [blocks, joined],
        [whole(blocks), window_specs(is_joint, frames, 3 * width)],
        [shape_of(joined.shape[:4] + (width,)), shape_of((number, heads, cells, cells))],
        [window_specs(is_joint, frames, width), pl.BlockSpec((1, heads, cells, cells), fetch)],
        grid=grid,
        scratch=[pltpu.VMEM((heads, cells, cells), low)],
    )


def attend_back(chain, joined, grad, probs, is_joint):
    frames = joined.shape[1]
    number, heads, cells, _ = probs.shape
    width = heads * HEAD_DIM
    grid = (2, 2) if is_joint else (1, frames)
    sides = joint_sides() if is_joint else spatial_sides()
    fetch = lambda i, j, info: (i * grid[1] + j, 0, 0, 0)
    sums = shape_of((heads, 9, 64, 64), full)
    return chain.run(
        "attend_back_joint" if is_joint else "attend_back_spatial",
        lambda *refs: attend_back_kernel(*refs, heads=heads, cells=cells, sides=sides),
        [joined, grad, probs],
        [
            window_specs(is_joint, frames, 3 * width),
            window_specs(is_joint, frames, width),
            pl.BlockSpec((1, heads, cells, cells), fetch),
        ],
        [shape_of(joined.shape), sums],
        [window_specs(is_joint, frames, 3 * width), whole(sums)],
        grid=grid,
        scratch=[pltpu.VMEM((heads, cells, cells), full)],
        mib=56,
    )


def offset_hot():
    places = np.arange(WIN_T * WIN_T)
    rows = places[:, None] // WIN_T - places[None, :] // WIN_T + WIN_T - 1
    cols = places[:, None] % WIN_T - places[None, :] % WIN_T + WIN_T - 1
    spots = (rows * (2 * WIN_T - 1) + cols).reshape(-1).astype(np.int32)
    return jnp.arange((2 * WIN_T - 1) ** 2, dtype=jnp.int32)[:, None] == jnp.asarray(spots)[None]


def fast_local(
    latents,
    cotangent,
    frame_counts,
    band_ids,
    class_ids,
    time_table,
    class_table,
    ada_weight,
    ada_bias,
    qkv_weight,
    out_weight,
    up_weight,
    down_weight,
    spatial_bias,
    joint_bias,
):
    frames = latents.shape[1]
    model_width = latents.shape[4]
    heads = spatial_bias.shape[0]
    width = heads * HEAD_DIM
    hidden = up_weight.shape[2]
    col_width = ada_weight.shape[2]
    rows = frames * 128
    z, y, c, x = (lax.axis_index(name) for name in ("z", "y", "c", "x"))
    count = swap(frame_counts.astype(full)).astype(jnp.int32)
    chain = Chain(jnp.concatenate([jnp.stack([z, y, x]).astype(jnp.int32), count]))

    def rearranged(values):
        shaped = values.reshape(frames, 8, 2, 8, model_width).transpose(0, 2, 1, 3, 4)
        return shaped.reshape(rows, model_width)

    qkv_rows = qkv_weight.reshape(2, -1, 3 * width)
    out_rows = out_weight.transpose(0, 2, 1)
    down_rows = down_weight.transpose(0, 2, 1)
    first_shard = swap(jnp.concatenate([qkv_rows[0], out_rows[0]], axis=1))
    traded_latents = swap(latents)
    packed = swap(
        jnp.concatenate(
            [up_weight[0], down_rows[0], qkv_rows[1], out_rows[1], up_weight[1], down_rows[1]],
            axis=1,
        )
    )

    band_hot = (band_ids[:, None] == jnp.arange(BANDS)[None, :]).astype(low)
    class_hot = (class_ids[:, None] == jnp.arange(CLASSES)[None, :]).astype(low)
    condition = jnp.dot(band_hot, time_table, preferred_element_type=full) + jnp.dot(
        class_hot, class_table, preferred_element_type=full
    )
    activity = jax.nn.silu(condition).astype(low)
    everyone = ("z", "y", "c", "x")
    mod_part = jnp.einsum(
        "cd,bde->cbe", activity, ada_weight, preferred_element_type=full
    ) + ada_bias[None].astype(full)
    mod_part = jnp.broadcast_to(
        mod_part.reshape(8, 1, 2, 2, col_width), (8, 2, 2, 2, col_width)
    ).reshape(32, 2, col_width)
    own_mod = lax.all_to_all(mod_part, everyone, split_axis=0, concat_axis=0, tiled=True)
    own_mod = own_mod.transpose(1, 0, 2).reshape(2, 6, model_width)
    rows_of = lambda *items: jnp.stack([own_mod[k, at] for k, at in items])

    hot = offset_hot()
    wide = 2 * WIN_T - 1
    square = spatial_bias.reshape(heads, 2 * WIN_S - 1, 2 * WIN_S - 1)
    spatial_parts = jnp.stack(
        [
            square[:, 8 * a : 8 * a + wide, 8 * b : 8 * b + wide].reshape(heads, -1)
            for a in range(3)
            for b in range(3)
        ],
        axis=1,
    )
    parts = swap(jnp.concatenate([spatial_parts, joint_bias.reshape(heads, 9, -1)]))
    blocks = jnp.dot(
        parts.reshape(heads * 18, wide * wide), hot.astype(low), preferred_element_type=full
    ).astype(low)
    blocks = blocks.reshape(2, heads, 9, 64, 64)
    near = blocks[0].reshape(heads, 3, 3, 64, 64)
    near = jnp.where(c == 0, near, near[:, ::-1])
    bias_blocks = [near.reshape(heads, 9, 64, 64), blocks[1]]

    windowed = lambda values: values.reshape(2, frames, 2, 64, values.shape[-1])

    latent_rows = rearranged(traded_latents)
    cuts = [shape_of((64, PIECE))] * 5
    shards = chain.run(
        "cut_shards", cut_kernel, [packed], [whole(packed)], cuts, [whole(a) for a in cuts]
    )
    gather = Gather(chain, [first_shard] + list(shards))
    gather.over_z(0)
    gather.step()
    gather.over_z(1)
    normed_0, inverse_0, moved_0 = first_norm(chain, latent_rows, rows_of((0, 0), (0, 1)))
    other_0 = flip_rows(moved_0)
    gather.step()
    gather.over_z(2)
    gather.step()
    gather.over_z(3)
    qkv_0, out_0 = gather.place(0, [3 * width, width])
    (joined_0,) = both_times(chain, "plain", moved_0, other_0, qkv_0)
    joined_0 = windowed(joined_0)
    mixed_0, probs_0 = attend(chain, bias_blocks[0], joined_0, False)
    mixed_0 = mixed_0.reshape(2, rows, width)
    away = other_rows(chain, mixed_0, out_0)
    gather.step()
    gather.over_z(4)
    (up_0,) = gather.place(1, [hidden])
    after_0, branch_one_0, normed_1, inverse_1, moved_1 = forward_step(
        chain, mixed_0, out_0, away, latent_rows, rows_of((0, 2), (0, 3), (0, 4)), False
    )
    other_1 = flip_rows(moved_1)
    act_0, slope_0 = both_times(chain, "gelu", moved_1, other_1, up_0)
    gather.step()
    gather.over_z(5)
    (down_0,) = gather.place(2, [hidden])
    away = other_rows(chain, act_0, down_0)
    current_1, branch_two_0, normed_2, inverse_2, moved_2 = forward_step(
        chain, act_0, down_0, away, after_0, rows_of((0, 5), (1, 0), (1, 1)), False
    )
    other_2 = flip_rows(moved_2)

    gather.step()
    qkv_1, out_1 = gather.place(3, [3 * width, width])
    (joined_1,) = both_times(chain, "plain", moved_2, other_2, qkv_1)
    joined_1 = windowed(joined_1)
    mixed_1, probs_1 = attend(chain, bias_blocks[1], joined_1, True)
    mixed_1 = mixed_1.reshape(2, rows, width)
    away = other_rows(chain, mixed_1, out_1)
    gather.step()
    (up_1,) = gather.place(4, [hidden])
    after_1, branch_one_1, normed_3, inverse_3, moved_3 = forward_step(
        chain, mixed_1, out_1, away, current_1, rows_of((1, 2), (1, 3), (1, 4)), False
    )
    other_3 = flip_rows(moved_3)
    traded_cotangent = swap(cotangent)
    act_1, slope_1 = both_times(chain, "gelu", moved_3, other_3, up_1)
    (down_1,) = gather.place(5, [hidden])
    away = other_rows(chain, act_1, down_1)
    final, branch_two_1 = forward_step(
        chain, act_1, down_1, away, after_1, rows_of((1, 5)), True
    )

    def restored(sent):
        shaped = sent.reshape(frames, 2, 8, 8, model_width).transpose(0, 2, 1, 3, 4)
        return shaped.astype(full).reshape(1, frames, 8, 16, model_width)

    traded_final = swap(final)

    state = rearranged(traded_cotangent)
    own_g, sums_a = first_back(chain, state, branch_two_1, rows_of((1, 5)))
    other_g = flip_rows(own_g)
    scatter = Scatter(chain)
    (hidden_g,) = both_times(chain, "slope", own_g, other_g, down_1, slope_1)
    away = other_rows(chain, hidden_g, up_1)
    scatter.weight_grad((own_g, other_g, act_1))
    state, sums_b, own_g = backward_step(
        chain, hidden_g, up_1, away, normed_3, inverse_3, state, rows_of((1, 4), (1, 2)), branch_one_1
    )
    other_g = flip_rows(own_g)
    scatter.weight_grad((moved_3, other_3, hidden_g))
    chain.wait(traded_final)
    scatter.step(6)
    (mixed_g,) = both_times(chain, "plain", own_g, other_g, out_1)
    back, joint_sums = attend_back(chain, joined_1, windowed(mixed_g), probs_1, True)
    back = back.reshape(2, rows, 3 * width)
    away = other_rows(chain, back, qkv_1)
    scatter.weight_grad((moved_2, other_2, back), (own_g, other_g, mixed_1))
    scatter.step(6)
    state, sums_c, own_g = backward_step(
        chain, back, qkv_1, away, normed_2, inverse_2, state, rows_of((1, 1), (0, 5)), branch_two_0
    )
    other_g = flip_rows(own_g)

    (hidden_g,) = both_times(chain, "slope", own_g, other_g, down_0, slope_0)
    away = other_rows(chain, hidden_g, up_0)
    scatter.weight_grad((own_g, other_g, act_0))
    scatter.step(6)
    state, sums_d, own_g = backward_step(
        chain, hidden_g, up_0, away, normed_1, inverse_1, state, rows_of((0, 4), (0, 2)), branch_one_0
    )
    other_g = flip_rows(own_g)
    scatter.weight_grad((moved_1, other_1, hidden_g))
    (mixed_g,) = both_times(chain, "plain", own_g, other_g, out_0)
    scatter.step(6)
    back, spatial_sums = attend_back(chain, joined_0, windowed(mixed_g), probs_0, False)
    back = back.reshape(2, rows, 3 * width)
    away = other_rows(chain, back, qkv_0)
    scatter.weight_grad((moved_0, other_0, back), (own_g, other_g, mixed_0))
    scatter.step(6)
    state, sums_e = backward_step(
        chain, back, qkv_0, away, normed_0, inverse_0, state, rows_of((0, 1)), None
    )
    traded_state = swap(state)
    output = restored(traded_final)

    exact = lax.Precision.HIGHEST
    grad_mod = jnp.stack(
        [
            sums_e[0], sums_e[1], sums_d[2], sums_d[0], sums_d[1], sums_c[2],
            sums_c[0], sums_c[1], sums_b[2], sums_b[0], sums_b[1], sums_a[0],
        ]
    )
    ordered = grad_mod.reshape(2, 32, col_width).transpose(1, 0, 2)
    cols = lax.all_to_all(ordered, everyone, split_axis=0, concat_axis=0, tiled=True)
    cols = cols.reshape(8, 2, 2, 2, col_width)
    cols = (cols[:, 0] + cols[:, 1]).reshape(16, 2, col_width)
    grad_ada_weight = jnp.einsum("cd,cbe->bde", activity.astype(full), cols, precision=exact)
    grad_ada_bias = jnp.sum(cols, axis=0)
    grad_activity = jnp.einsum("cbe,bde->cd", cols, ada_weight.astype(full), precision=exact)
    grad_activity = grad_activity + flip(grad_activity, "c")

    near = spatial_sums.reshape(heads, 3, 3, 64, 64)
    near = jnp.where(c == 0, near, near[:, ::-1]).reshape(heads, 9, 64, 64)
    tables = jnp.dot(
        jnp.stack([near, joint_sums]).reshape(heads * 18, 64 * 64),
        hot.astype(full).T,
        precision=exact,
    )

    scatter.step(6)
    shared = add_all(chain, grad_activity)
    shared_tables = add_all(chain, tables)
    scatter.step(6)
    sent = flip(shared, "x"), flip(shared_tables, "x")
    shared = add_all(chain, shared, sent[0])
    shared_tables = add_all(chain, shared_tables, sent[1])
    sent = flip(shared, "y"), flip(shared_tables, "y")
    early = swap(join_pieces(chain, scatter.done))
    shared = add_all(chain, shared, sent[0])
    shared_tables = add_all(chain, shared_tables, sent[1])
    sent = [[z_trade(values, k) for k in (1, 2, 3)] for values in (shared, shared_tables)]
    scatter.step(6)
    late = swap(scatter.done[5]).astype(full)
    grad_activity = add_all(chain, shared, *sent[0])
    tables = add_all(chain, shared_tables, *sent[1])
    grad_latents = restored(traded_state)
    early = early.astype(full)
    piece = lambda at: early[:, at * PIECE : (at + 1) * PIECE]
    grad_down = jnp.stack([piece(3).T, piece(0).T])
    grad_up = jnp.stack([piece(4), piece(1)])
    grad_qkv = jnp.stack([late[:, : 3 * width], piece(2)[:, : 3 * width]])
    grad_out = jnp.stack([late[:, 3 * width :].T, piece(2)[:, 3 * width :].T])

    tables = jnp.where(c == x, tables, flip(tables, "c")).reshape(2, heads, 9, wide, wide)
    grad_joint = tables[1].reshape(heads, 9 * wide * wide)
    near = tables[0].reshape(heads, 3, 3, wide, wide)
    long = 2 * WIN_S - 1
    grad_spatial = 0.0
    for a in range(3):
        for b in range(3):
            grad_spatial = grad_spatial + jnp.pad(
                near[:, a, b],
                ((0, 0), (8 * a, long - wide - 8 * a), (8 * b, long - wide - 8 * b)),
            )
    grad_spatial = grad_spatial.reshape(heads, long * long)
    grad_condition = jax.vjp(jax.nn.silu, condition)[1](grad_activity)[0]
    grad_time = jnp.dot(band_hot.astype(full).T, grad_condition, precision=exact)
    grad_class = jnp.dot(class_hot.astype(full).T, grad_condition, precision=exact)

    return (
        output,
        grad_latents,
        grad_time,
        grad_class,
        grad_ada_weight,
        grad_ada_bias,
        grad_qkv.reshape(2, -1, 3, width),
        grad_out,
        grad_up,
        grad_down,
        grad_spatial,
        grad_joint,
    )


def solution(mesh):
    if mesh.shape["dp"] != 16 or mesh.shape["mp"] != 2:
        return solution_any(mesh)
    fine = Mesh(mesh.devices.reshape(4, 2, 2, 2), ("z", "y", "c", "x"))
    dp, mp = ("z", "y", "c"), "x"
    both = dp + (mp,)
    tokens = P(dp, None, mp, None, None)
    weight_specs = (
        P(None, None, both),
        P(None, both),
        P(None, dp, None, mp),
        P(None, mp, dp),
        P(None, dp, mp),
        P(None, mp, dp),
        P(mp, None),
        P(mp, None),
    )
    return jax.shard_map(
        fast_local,
        mesh=fine,
        in_specs=(tokens, tokens, P(dp), P(), P(), P(), P()) + weight_specs,
        out_specs=(tokens, tokens, P(), P()) + weight_specs,
        check_vma=False,
    )
```

```python
import jax
import jax.numpy as jnp
import numpy as np
from jax import lax
from jax.experimental import pallas as pl
from jax.experimental.pallas import tpu as pltpu
from jax.sharding import Mesh
from jax.sharding import PartitionSpec as P

HEAD_DIM = 64
CLASSES = 101
BANDS = 32
FRAMES = 5
WIN_S = 16
WIN_T = 8


epsilon = 1e-06
masked_score = -1e30


def spatial_table():
    places = np.arange(WIN_S * WIN_S)
    row_at = places // WIN_S
    col_at = places % WIN_S
    row_rel = row_at[:, None] - row_at[None, :] + WIN_S - 1
    col_rel = col_at[:, None] - col_at[None, :] + WIN_S - 1
    return (row_rel * (2 * WIN_S - 1) + col_rel).astype(np.int32)


def joint_table():
    places = np.arange(FRAMES * WIN_T * WIN_T)
    time_at = places // (WIN_T * WIN_T)
    row_at = places // WIN_T % WIN_T
    col_at = places % WIN_T
    time_rel = time_at[:, None] - time_at[None, :] + FRAMES - 1
    row_rel = row_at[:, None] - row_at[None, :] + WIN_T - 1
    col_rel = col_at[:, None] - col_at[None, :] + WIN_T - 1
    return ((time_rel * (2 * WIN_T - 1) + row_rel) * (2 * WIN_T - 1) + col_rel).astype(np.int32)


def to_windows(values, window, is_joint):
    clip_count, frames, side_cells, channels = (
        values.shape[0],
        values.shape[1],
        values.shape[2],
        values.shape[4],
    )
    per_side = side_cells // window
    if is_joint:
        shaped = values.reshape(clip_count, frames, per_side, window, per_side, window, channels)
        shaped = shaped.transpose(0, 2, 4, 1, 3, 5, 6)
        return shaped.reshape(clip_count * per_side * per_side, frames * window * window, channels)
    shaped = values.reshape(clip_count, frames, per_side, window, per_side, window, channels)
    shaped = shaped.transpose(0, 1, 2, 4, 3, 5, 6)
    return shaped.reshape(clip_count * frames * per_side * per_side, window * window, channels)


def from_windows(values, clip_count, frames, side_cells, window, is_joint):
    per_side = side_cells // window
    channels = values.shape[-1]
    if is_joint:
        shaped = values.reshape(clip_count, per_side, per_side, frames, window, window, channels)
        shaped = shaped.transpose(0, 3, 1, 4, 2, 5, 6)
    else:
        shaped = values.reshape(clip_count, frames, per_side, per_side, window, window, channels)
        shaped = shaped.transpose(0, 1, 2, 4, 3, 5, 6)
    return shaped.reshape(clip_count, frames, side_cells, side_cells, channels)


def normalize(values):
    center = values - jnp.mean(values, axis=-1, keepdims=True)
    spread = jnp.mean(center * center, axis=-1, keepdims=True)
    inverse = lax.rsqrt(spread + epsilon)
    return (center * inverse, inverse)


def norm_back(grad_normed, normed, inverse):
    first_mean = jnp.mean(grad_normed, axis=-1, keepdims=True)
    second_mean = jnp.mean(grad_normed * normed, axis=-1, keepdims=True)
    return inverse * (grad_normed - first_mean - normed * second_mean)


def exact_gelu(values):
    return jax.nn.gelu(values, approximate=False)


def gather_rows(values):
    return lax.all_gather(values, "mp", axis=2, tiled=True)


def sum_rows(values):
    return lax.psum_scatter(
        values.astype(jnp.bfloat16), "mp", scatter_dimension=2, tiled=True
    ).astype(jnp.float32)


def gather_grads(values):
    return lax.all_gather(values, "mp", axis=2, tiled=True)


def input_sums(values):
    return lax.psum_scatter(
        values.astype(jnp.bfloat16), "mp", scatter_dimension=2, tiled=True
    ).astype(jnp.float32)


def inputs_again(moved):
    return lax.all_gather(moved, "mp", axis=2, tiled=True)


def attention_scores(query_part, key_part, bias_matrix, key_valid):
    scores = (
        jnp.einsum("nqhe,nkhe->nhqk", query_part, key_part, preferred_element_type=jnp.float32)
        * HEAD_DIM ** (-0.5)
        + bias_matrix[None]
    )
    if key_valid is not None:
        scores = jnp.where(key_valid[:, None, None, :] > 0, scores, masked_score)
    return scores


def local(
    latents,
    cotangent,
    frame_counts,
    band_ids,
    class_ids,
    time_table,
    class_table,
    ada_weight,
    ada_bias,
    qkv_weight,
    out_weight,
    up_weight,
    down_weight,
    spatial_bias,
    joint_bias,
):
    clip_count = latents.shape[0]
    frames = latents.shape[1]
    side_cells = latents.shape[3]
    model_width = latents.shape[4]
    heads_local = spatial_bias.shape[0]
    local_width = heads_local * HEAD_DIM
    dp_count = lax.axis_size("dp")
    mp_count = lax.axis_size("mp")
    col_width = ada_weight.shape[2]
    band_hot = (band_ids[:, None] == jnp.arange(BANDS)[None, :]).astype(jnp.bfloat16)
    class_hot = (class_ids[:, None] == jnp.arange(CLASSES)[None, :]).astype(jnp.bfloat16)
    condition = jnp.dot(band_hot, time_table, preferred_element_type=jnp.float32) + jnp.dot(
        class_hot, class_table, preferred_element_type=jnp.float32
    )
    activity_low = jax.nn.silu(condition).astype(jnp.bfloat16)
    ada_cols, ada_bias_cols = (
        lax.all_gather(ada_weight, "mp", axis=2, tiled=True),
        lax.all_gather(ada_bias, "mp", axis=1, tiled=True),
    )
    mod_part = jnp.einsum(
        "cd,bde->bce", activity_low, ada_cols, preferred_element_type=jnp.float32
    ) + ada_bias_cols[:, None, :].astype(jnp.float32)
    modulation = lax.all_gather(mod_part, "dp", axis=2, tiled=True)
    first_clip = lax.axis_index("dp") * clip_count
    own_mod = lax.dynamic_slice_in_dim(modulation, first_clip, clip_count, 1).reshape(
        2, clip_count, 6, model_width
    )
    frame_valid = (jnp.arange(frames)[None, :] < frame_counts[:, None]).astype(jnp.float32)
    frame_mask = frame_valid[:, :, None, None, None]
    key_frames = np.arange(frames * WIN_T * WIN_T) // (WIN_T * WIN_T)
    joint_cells = key_frames.shape[0]
    per_side = side_cells // WIN_T
    key_valid = frame_valid[:, key_frames]
    key_valid = jnp.broadcast_to(
        key_valid[:, None, :], (clip_count, per_side * per_side, joint_cells)
    ).reshape(clip_count * per_side * per_side, joint_cells)
    w_qkv, w_out, w_up, w_down = (
        lax.all_gather(qkv_weight, "dp", axis=1, tiled=True),
        lax.all_gather(out_weight, "dp", axis=2, tiled=True),
        lax.all_gather(up_weight, "dp", axis=1, tiled=True),
        lax.all_gather(down_weight, "dp", axis=2, tiled=True),
    )
    spatial_index = spatial_table()
    joint_index = joint_table()
    spatial_matrix = spatial_bias.astype(jnp.float32)[:, spatial_index]
    joint_matrix = joint_bias.astype(jnp.float32)[:, joint_index]
    current = latents.astype(jnp.float32)
    stored = []
    for which_block in range(2):
        is_joint = which_block == 1
        window = WIN_T if is_joint else WIN_S
        bias_matrix = joint_matrix if is_joint else spatial_matrix
        mask_keys = key_valid if is_joint else None
        block_mod = own_mod[which_block][:, :, None, None, None, :]
        normed_one, inverse_one = normalize(current)
        moved_one = (normed_one * (1.0 + block_mod[:, 1]) + block_mod[:, 0]).astype(jnp.bfloat16)
        gathered_one = gather_rows(moved_one)
        projected = jnp.einsum(
            "cfyxd,dkh->cfyxkh",
            gathered_one,
            w_qkv[which_block],
            preferred_element_type=jnp.float32,
        ).astype(jnp.bfloat16)
        windows = to_windows(
            projected.reshape(clip_count, frames, side_cells, side_cells, 3 * local_width),
            window,
            is_joint,
        )
        windows = windows.reshape(windows.shape[0], windows.shape[1], 3, heads_local, HEAD_DIM)
        scores = attention_scores(windows[:, :, 0], windows[:, :, 1], bias_matrix, mask_keys)
        row_max = jnp.max(scores, axis=-1, keepdims=True)
        log_total = row_max + jnp.log(jnp.sum(jnp.exp(scores - row_max), axis=-1, keepdims=True))
        probs_low = jnp.exp(scores - log_total).astype(jnp.bfloat16)
        mixed_win = jnp.einsum(
            "nhqk,nkhe->nqhe", probs_low, windows[:, :, 2], preferred_element_type=jnp.float32
        ).astype(jnp.bfloat16)
        mixed_rows = from_windows(
            mixed_win.reshape(mixed_win.shape[0], mixed_win.shape[1], local_width),
            clip_count,
            frames,
            side_cells,
            window,
            is_joint,
        )
        branch_one = sum_rows(
            jnp.einsum(
                "cfyxk,kd->cfyxd",
                mixed_rows,
                w_out[which_block],
                preferred_element_type=jnp.float32,
            )
        )
        after_attn = current + frame_mask * block_mod[:, 2] * branch_one
        normed_two, inverse_two = normalize(after_attn)
        moved_two = (normed_two * (1.0 + block_mod[:, 4]) + block_mod[:, 3]).astype(jnp.bfloat16)
        gathered_two = gather_rows(moved_two)
        hidden = jnp.einsum(
            "cfyxd,dk->cfyxk", gathered_two, w_up[which_block], preferred_element_type=jnp.float32
        )
        activated = exact_gelu(hidden).astype(jnp.bfloat16)
        branch_two = sum_rows(
            jnp.einsum(
                "cfyxk,kd->cfyxd",
                activated,
                w_down[which_block],
                preferred_element_type=jnp.float32,
            )
        )
        current = after_attn + frame_mask * block_mod[:, 5] * branch_two
        stored.append(
            (
                normed_one,
                inverse_one,
                moved_one,
                gathered_one,
                windows,
                log_total,
                mixed_rows,
                branch_one,
                normed_two,
                inverse_two,
                moved_two,
                gathered_two,
                hidden,
                activated,
                branch_two,
            )
        )
    grad_state = cotangent.astype(jnp.float32)
    mod_grads = []
    qkv_grads = []
    out_grads = []
    up_grads = []
    down_grads = []
    table_parts = []
    for which_block in (1, 0):
        is_joint = which_block == 1
        window = WIN_T if is_joint else WIN_S
        bias_matrix = joint_matrix if is_joint else spatial_matrix
        mask_keys = key_valid if is_joint else None
        block_mod = own_mod[which_block][:, :, None, None, None, :]
        (
            normed_one,
            inverse_one,
            moved_one,
            gathered_one,
            windows,
            log_total,
            mixed_rows,
            branch_one,
            normed_two,
            inverse_two,
            moved_two,
            gathered_two,
            hidden,
            activated,
            branch_two,
        ) = stored[which_block]
        grad_gate_two = jnp.sum(frame_mask * grad_state * branch_two, axis=(1, 2, 3))
        grad_rows = gather_grads((frame_mask * block_mod[:, 5] * grad_state).astype(jnp.bfloat16))
        down_grads.append(
            jnp.einsum("cfyxk,cfyxd->kd", activated, grad_rows, preferred_element_type=jnp.float32)
        )
        grad_act = jnp.einsum(
            "cfyxd,kd->cfyxk", grad_rows, w_down[which_block], preferred_element_type=jnp.float32
        )
        grad_hidden = jax.vjp(exact_gelu, hidden)[1](grad_act)[0].astype(jnp.bfloat16)
        inputs_two = inputs_again(moved_two)
        up_grads.append(
            jnp.einsum(
                "cfyxd,cfyxk->dk", inputs_two, grad_hidden, preferred_element_type=jnp.float32
            )
        )
        grad_moved = input_sums(
            jnp.einsum(
                "cfyxk,dk->cfyxd",
                grad_hidden,
                w_up[which_block],
                preferred_element_type=jnp.float32,
            )
        )
        grad_shift_two = jnp.sum(grad_moved, axis=(1, 2, 3))
        grad_scale_two = jnp.sum(grad_moved * normed_two, axis=(1, 2, 3))
        grad_state = grad_state + norm_back(
            grad_moved * (1.0 + block_mod[:, 4]), normed_two, inverse_two
        )
        grad_gate_one = jnp.sum(frame_mask * grad_state * branch_one, axis=(1, 2, 3))
        grad_rows = gather_grads((frame_mask * block_mod[:, 2] * grad_state).astype(jnp.bfloat16))
        out_grads.append(
            jnp.einsum("cfyxk,cfyxd->kd", mixed_rows, grad_rows, preferred_element_type=jnp.float32)
        )
        grad_mixed = jnp.einsum(
            "cfyxd,kd->cfyxk", grad_rows, w_out[which_block], preferred_element_type=jnp.float32
        ).astype(jnp.bfloat16)
        grad_win = to_windows(grad_mixed, window, is_joint)
        grad_win = grad_win.reshape(grad_win.shape[0], grad_win.shape[1], heads_local, HEAD_DIM)
        query_part = windows[:, :, 0]
        key_part = windows[:, :, 1]
        value_part = windows[:, :, 2]
        probs_full = jnp.exp(
            attention_scores(query_part, key_part, bias_matrix, mask_keys) - log_total
        )
        grad_value = jnp.einsum(
            "nhqk,nqhe->nkhe",
            probs_full.astype(jnp.bfloat16),
            grad_win,
            preferred_element_type=jnp.float32,
        ).astype(jnp.bfloat16)
        grad_probs = jnp.einsum(
            "nqhe,nkhe->nhqk", grad_win, value_part, preferred_element_type=jnp.float32
        )
        row_dot = jnp.sum(probs_full * grad_probs, axis=-1, keepdims=True)
        grad_scores = (probs_full * (grad_probs - row_dot)).astype(jnp.bfloat16)
        bias_sum = jnp.sum(grad_scores.astype(jnp.float32), axis=0)
        if is_joint:
            table_parts.append(
                jnp.zeros((heads_local, joint_bias.shape[1]), jnp.float32)
                .at[:, joint_index]
                .add(bias_sum)
            )
        else:
            table_parts.append(
                jnp.zeros((heads_local, spatial_bias.shape[1]), jnp.float32)
                .at[:, spatial_index]
                .add(bias_sum)
            )
        grad_query = (
            jnp.einsum("nhqk,nkhe->nqhe", grad_scores, key_part, preferred_element_type=jnp.float32)
            * HEAD_DIM ** (-0.5)
        ).astype(jnp.bfloat16)
        grad_key = (
            jnp.einsum(
                "nhqk,nqhe->nkhe", grad_scores, query_part, preferred_element_type=jnp.float32
            )
            * HEAD_DIM ** (-0.5)
        ).astype(jnp.bfloat16)
        stacked = jnp.stack([grad_query, grad_key, grad_value], axis=2).reshape(
            grad_query.shape[0], grad_query.shape[1], 3 * local_width
        )
        grad_projected = from_windows(
            stacked, clip_count, frames, side_cells, window, is_joint
        ).reshape(clip_count, frames, side_cells, side_cells, 3, local_width)
        inputs_one = inputs_again(moved_one)
        qkv_grads.append(
            jnp.einsum(
                "cfyxd,cfyxkh->dkh", inputs_one, grad_projected, preferred_element_type=jnp.float32
            )
        )
        grad_moved = input_sums(
            jnp.einsum(
                "cfyxkh,dkh->cfyxd",
                grad_projected,
                w_qkv[which_block],
                preferred_element_type=jnp.float32,
            )
        )
        grad_shift_one = jnp.sum(grad_moved, axis=(1, 2, 3))
        grad_scale_one = jnp.sum(grad_moved * normed_one, axis=(1, 2, 3))
        grad_state = grad_state + norm_back(
            grad_moved * (1.0 + block_mod[:, 1]), normed_one, inverse_one
        )
        mod_grads.append(
            jnp.stack(
                [
                    grad_shift_one,
                    grad_scale_one,
                    grad_gate_one,
                    grad_shift_two,
                    grad_scale_two,
                    grad_gate_two,
                ],
                axis=1,
            )
        )
    grad_mod = jnp.stack(mod_grads[::-1], axis=0).reshape(2, clip_count, 6 * model_width)
    ordered = (
        grad_mod.reshape(2, clip_count, dp_count, mp_count, col_width)
        .transpose(0, 1, 3, 2, 4)
        .reshape(2, clip_count, 6 * model_width)
    )
    summed_cols = lax.psum_scatter(ordered, "mp", scatter_dimension=2, tiled=True)
    grad_mod_cols = lax.all_to_all(summed_cols, "dp", split_axis=2, concat_axis=1, tiled=True)
    grad_ada_weight = jnp.einsum(
        "cd,bce->bde",
        activity_low.astype(jnp.float32),
        grad_mod_cols,
        precision=lax.Precision.HIGHEST,
    )
    grad_ada_bias = jnp.sum(grad_mod_cols, axis=1)
    grad_mod_block = lax.all_gather(grad_mod_cols, "mp", axis=2, tiled=True)
    activity_part = jnp.einsum(
        "bce,bde->cd", grad_mod_block, ada_cols.astype(jnp.float32), precision=lax.Precision.HIGHEST
    )
    grad_activity = lax.psum(activity_part, "dp")
    grad_condition = jax.vjp(jax.nn.silu, condition)[1](grad_activity)[0]
    grad_time = jnp.dot(
        band_hot.astype(jnp.float32).T, grad_condition, precision=lax.Precision.HIGHEST
    )
    grad_class = jnp.dot(
        class_hot.astype(jnp.float32).T, grad_condition, precision=lax.Precision.HIGHEST
    )
    grad_spatial, grad_joint = lax.psum((table_parts[1], table_parts[0]), "dp")
    grad_qkv, grad_out, grad_up, grad_down = (
        lax.psum_scatter(jnp.stack(qkv_grads[::-1], axis=0), "dp", scatter_dimension=1, tiled=True),
        lax.psum_scatter(jnp.stack(out_grads[::-1], axis=0), "dp", scatter_dimension=2, tiled=True),
        lax.psum_scatter(jnp.stack(up_grads[::-1], axis=0), "dp", scatter_dimension=1, tiled=True),
        lax.psum_scatter(
            jnp.stack(down_grads[::-1], axis=0), "dp", scatter_dimension=2, tiled=True
        ),
    )
    return (
        current,
        grad_state,
        grad_time,
        grad_class,
        grad_ada_weight,
        grad_ada_bias,
        grad_qkv,
        grad_out,
        grad_up,
        grad_down,
        grad_spatial,
        grad_joint,
    )


def solution_any(mesh):
    placed = (
        P("dp", None, "mp", None, None),
        P("dp", None, "mp", None, None),
        P("dp"),
        P(),
        P(),
        P(),
        P(),
        P(None, None, ("dp", "mp")),
        P(None, ("dp", "mp")),
        P(None, "dp", None, "mp"),
        P(None, "mp", "dp"),
        P(None, "dp", "mp"),
        P(None, "mp", "dp"),
        P("mp", None),
        P("mp", None),
    )
    return jax.shard_map(
        local,
        mesh=mesh,
        in_specs=placed,
        out_specs=(
            P("dp", None, "mp", None, None),
            P("dp", None, "mp", None, None),
            P(),
            P(),
            P(None, None, ("dp", "mp")),
            P(None, ("dp", "mp")),
            P(None, "dp", None, "mp"),
            P(None, "mp", "dp"),
            P(None, "dp", "mp"),
            P(None, "mp", "dp"),
            P("mp", None),
            P("mp", None),
        ),
        check_vma=False,
    )


low = jnp.bfloat16
full = jnp.float32
HALF_ROOT = 0.7071067811865476
PHI_AT_ZERO = 0.3989422804014327
MIB = 1024 * 1024


def flip(values, axis):
    return lax.ppermute(values, axis, [(0, 1), (1, 0)])


def z_trade(values, step):
    return lax.ppermute(values, "z", [(place, place ^ step) for place in range(4)])


def swap_only(values):
    return lax.ppermute(values, ("c", "x"), [(1, 2), (2, 1)])


def swap(values):
    return jnp.where(lax.axis_index("c") == lax.axis_index("x"), values, swap_only(values))


def shape_of(dims, dtype=low):
    return jax.ShapeDtypeStruct(tuple(dims), dtype)


def whole(array):
    zeros = (0,) * len(array.shape)
    return pl.BlockSpec(tuple(array.shape), lambda *at: zeros)


def whole_once(array):
    zeros = (0,) * len(array.shape)
    return pl.BlockSpec(
        tuple(array.shape), lambda *at: zeros, pipeline_mode=pl.Buffered(1)
    )


def space_of(dims, dtype):
    dims = [1] * (2 - len(dims)) + list(dims)
    size = jnp.dtype(dtype).itemsize
    rows = 32 // size
    dims[-1] = -(-dims[-1] // 128) * 128
    dims[-2] = -(-dims[-2] // rows) * rows
    return int(np.prod(dims)) * size


def room_for(specs, arrays, scratch):
    total = 0
    for spec, array in zip(specs, arrays):
        if spec.block_shape is not None:
            once = spec.pipeline_mode is not None
            total += space_of(spec.block_shape, array.dtype) * (1 if once else 2)
    return total + sum(space_of(held.shape, held.dtype) for held in scratch)


class Chain:
    def __init__(self, info):
        self.info = info
        self.last = []
        self.pending = []

    def wait(self, *values):
        self.pending += values

    def run(self, name, kernel, args, in_specs, outs, out_specs, grid=(1,), scratch=(), extra=4, waits=()):
        count = len(args)
        unread = self.last + self.pending + list(waits)
        self.pending = []
        held = len(unread)

        limit = room_for(list(in_specs) + list(out_specs), list(args) + list(outs), scratch)

        def body(*refs):
            kernel(*refs[: 1 + count], *refs[1 + count + held :])

        results = pl.pallas_call(
            body,
            grid_spec=pltpu.PrefetchScalarGridSpec(
                num_scalar_prefetch=1,
                grid=grid,
                in_specs=list(in_specs) + [pl.BlockSpec(memory_space=pl.ANY)] * held,
                out_specs=list(out_specs),
                scratch_shapes=list(scratch),
            ),
            out_shape=list(outs),
            compiler_params=pltpu.CompilerParams(vmem_limit_bytes=limit + extra * MIB),
            cost_estimate=pl.CostEstimate(flops=1, bytes_accessed=1, transcendentals=0),
            name=name,
        )(self.info, *args, *unread)
        self.last = [results[0]]
        return results


def pack_arguments(chain, rows_in, up, down, qkv, out):
    def kernel(info, rows_from, up_in, down_in, qkv_in, out_in, rows_to, packed):
        rows_to[...] = rows_from[...]
        start = 0
        for part in (up_in[0], down_in[0], qkv_in[1], out_in[1], up_in[1], down_in[1]):
            packed[:, start : start + part.shape[1]] = part
            start += part.shape[1]

    args = [rows_in, up, down, qkv, out]
    outs = [shape_of(rows_in.shape), shape_of((up.shape[1], 5 * PIECE))]
    return chain.run(
        "pack_arguments", kernel, args, [whole(v) for v in args], outs, [whole(v) for v in outs]
    )


def cut_kernel(info, packed, traded, *outs):
    start = 0
    for out in outs:
        width = out.shape[1]
        cols = slice(start, start + width)

        @pl.when(info[4] == 1)
        def _():
            out[...] = packed[:, cols]

        @pl.when(info[4] == 0)
        def _():
            out[...] = traded[:, cols]

        start += width


PIECE = 2048
PIECE_TILE = 512


def tile_spec(count, rows=64):
    return pl.BlockSpec((count, rows, PIECE_TILE), lambda j, info: (0, 0, j))


def flat_spec(rows=64):
    return pl.BlockSpec((rows, PIECE_TILE), lambda j, info: (0, j))


class Gather:
    def __init__(self, chain, shards):
        self.chain = chain
        self.shards = shards
        self.near = {}
        self.sent = {}
        self.got = {}
        self.step_at = 0

    def over_z(self, at):
        self.near[at] = [z_trade(self.shards[at], k) for k in (1, 2, 3)]

    def step(self):
        at = self.step_at
        self.step_at += 1
        own = at < len(self.shards)
        far = at > 0
        args, specs = [], []
        if own:
            args += [self.shards[at]] + self.near[at]
            specs += [flat_spec()] * 4
        start = 0
        if far:
            got_x, got_y = self.got[at - 1]
            start = (got_x.shape[0] - 4) // 2
            args += [got_x, got_y]
            specs += [
                pl.BlockSpec((2, 64, PIECE_TILE), lambda j, info: (start + 1, 0, j)),
                pl.BlockSpec((2, 64, PIECE_TILE), lambda j, info: (start, 0, j)),
            ]

        def kernel(info, *refs):
            to_x, to_y = refs[-2:]
            if own:
                for k in range(4):
                    to_x[(2 if far else 0) + k] = refs[k][...]
                    to_y[(2 if far else 0) + k] = refs[k][...]
            if far:
                from_x, from_y = refs[-4:-2]
                to_x[0:2] = from_y[...]
                to_y[0:2] = from_x[...]

        count = (2 if far else 0) + (4 if own else 0)
        outs = [shape_of((count, 64, PIECE))] * 2
        to_x, to_y = self.chain.run(
            "gather_step",
            kernel,
            args,
            specs,
            outs,
            [tile_spec(count)] * 2,
            grid=(PIECE // PIECE_TILE,),
        )
        self.sent[at] = to_x
        self.got[at] = (flip(to_x, "x"), flip(to_y, "y"))

    def place(self, at, widths):
        def kernel(info, own, from_x, from_y, far_lo, far_hi, *outs):
            k = pl.program_id(0)
            place = info[1] * 2 + info[2]

            def put(rel, block):
                start = 0
                for out in outs:
                    width = out.shape[3]
                    out[0, place ^ rel] = block[0, :, start : start + width]
                    start += width

            put(0, own)
            put(1, from_x)
            put(2, from_y)

            @pl.when(k < 2)
            def _():
                put(3, far_lo)

            @pl.when(k >= 2)
            def _():
                put(3, far_hi)

        got_x, got_y = self.got[at]
        start = got_x.shape[0] - 4
        block = (1, 64, PIECE)
        quad = pl.BlockSpec(block, lambda k, info: (k + start, 0, 0))
        results = self.chain.run(
            "place_weights",
            kernel,
            [self.sent[at], got_x, got_y, *self.got[at + 1]],
            [
                quad,
                quad,
                quad,
                pl.BlockSpec(block, lambda k, info: (jnp.minimum(k, 1), 0, 0)),
                pl.BlockSpec(block, lambda k, info: (jnp.maximum(k - 2, 0), 0, 0)),
            ],
            [shape_of((4, 4, 64, w)) for w in widths],
            [pl.BlockSpec((1, 4, 64, w), lambda k, info: (info[0] ^ k, 0, 0, 0)) for w in widths],
            grid=(4,),
        )
        return [a.reshape(16 * 64, a.shape[3]) for a in results]


GRAD_TILE = 512


def weight_grad_kernel(info, *refs, pairs, tiles):
    lhs = refs[: 4 * pairs]
    rhs = refs[4 * pairs : 5 * pairs]
    near, to_x, to_y, far_lo, far_hi = refs[5 * pairs : 5 * pairs + 5]
    held = refs[5 * pairs + 5]
    across = refs[5 * pairs + 6 :]
    j = pl.program_id(0)
    place = info[1] * 2 + info[2]
    begin = 0
    for at in range(pairs):

        @pl.when(j == begin)
        def _():
            for part in range(4):
                cols = slice(part * ROW_TILE, (part + 1) * ROW_TILE)
                across[at][:, cols] = lhs[4 * at + part][...].T

        @pl.when((j >= begin) & (j < begin + tiles[at]))
        def _():
            tokens = rhs[at][...].reshape(4 * ROW_TILE, GRAD_TILE)
            for rows in range(0, held.shape[0], 256):
                block = jnp.dot(
                    across[at][rows : rows + 256], tokens, preferred_element_type=full
                )
                held[rows : rows + 256] = block.astype(low)

        begin += tiles[at]

    def part(z, rel):
        return held[pl.ds(pl.multiple_of(z * 256 + (place ^ rel) * 64, 64), 64), :]

    for z in range(4):
        near[z] = part(z, 0)
        to_x[z] = part(z, 1)
        to_y[z] = part(z, 2)
        if z < 2:
            far_lo[z] = part(z, 3)
        else:
            far_hi[z - 2] = part(z, 3)


class Scatter:
    def __init__(self, chain):
        self.chain = chain
        self.parts = []
        self.got = None
        self.held = None
        self.done = []
        self.step_at = 0

    def weight_grad(self, *items):
        pairs = len(items)
        widths = tuple(item[2].shape[2] for item in items)
        rows, features = items[0][0][0].shape
        tiles = [w // GRAD_TILE for w in widths]
        quads = shape_of((4, 64, PIECE))
        twos = shape_of((2, 64, PIECE))

        def rhs_spec(at):
            first, last = sum(tiles[:at]), tiles[at] - 1
            return pl.BlockSpec(
                (2, 2 * rows, GRAD_TILE),
                lambda j, info: (0, 0, jnp.clip(j - first, 0, last)),
            )

        quad_spec = pl.BlockSpec((4, 64, GRAD_TILE), lambda j, info: (0, 0, j))
        two_spec = pl.BlockSpec((2, 64, GRAD_TILE), lambda j, info: (0, 0, j))
        lhs = [part for item in items for pair in item[:2] for part in pair]
        self.parts.append(
            self.chain.run(
                "weight_grad",
                lambda *refs: weight_grad_kernel(*refs, pairs=pairs, tiles=tiles),
                lhs + [item[2] for item in items],
                [whole_once(v) for v in lhs] + [rhs_spec(at) for at in range(pairs)],
                [quads, quads, quads, twos, twos],
                [quad_spec] * 3 + [two_spec] * 2,
                grid=(PIECE // GRAD_TILE,),
                scratch=[pltpu.VMEM((features, GRAD_TILE), low)]
                + [pltpu.VMEM((features, 4 * rows), low)] * pairs,
                extra=4,
            )
        )
        if len(self.parts) == 1:
            self.got = (flip(self.parts[0][3], "x"), flip(self.parts[0][4], "y"))

    def step(self, total):
        at = self.step_at
        self.step_at += 1
        far = at + 1 < total
        mid = at < total
        near = 0 <= at - 1 < total
        last = 0 <= at - 2 < total
        args, specs = [], []

        def put(array, spec):
            args.append(array)
            specs.append(spec)
            return len(args) - 1

        names = {}
        if far:
            names["far_lo"] = put(self.parts[at + 1][3], tile_spec(2))
            names["far_hi"] = put(self.parts[at + 1][4], tile_spec(2))
        if mid:
            names["to_x"] = put(self.parts[at][1], tile_spec(4))
            names["to_y"] = put(self.parts[at][2], tile_spec(4))
        if near:
            names["near"] = put(self.parts[at - 1][0], tile_spec(4))
        if mid or near:
            count = self.got[0].shape[0]
            names["got_x"] = put(self.got[0], tile_spec(count))
            names["got_y"] = put(self.got[1], tile_spec(count))
        if last:
            for k in range(4):
                names["held%d" % k] = put(self.held[k], flat_spec())
        outs, out_specs = [], []
        sent = (2 if far else 0) + (4 if mid else 0)
        if mid:
            outs += [shape_of((sent, 64, PIECE))] * 2
            out_specs += [tile_spec(sent)] * 2
        if near:
            outs += [shape_of((64, PIECE), full)] + [shape_of((64, PIECE))] * 3
            out_specs += [flat_spec()] * 4
        if last:
            outs.append(shape_of((64, PIECE)))
            out_specs.append(flat_spec())
        number = len(args)

        def kernel(info, *refs):
            out = list(refs[number:])
            get = {name: refs[spot] for name, spot in names.items()}
            if mid:
                out_x, out_y = out[:2]
                del out[:2]
                start = 0
                if far:
                    out_x[0:2] = get["far_lo"][...]
                    out_y[0:2] = get["far_hi"][...]
                    start = 2
                for k in range(4):
                    part_x = get["to_x"][k]
                    part_y = get["to_y"][k]
                    if k < 2:
                        part_y = (part_y.astype(full) + get["got_x"][k].astype(full)).astype(low)
                    else:
                        part_x = (
                            part_x.astype(full) + get["got_y"][k - 2].astype(full)
                        ).astype(low)
                    out_x[start + k] = part_x
                    out_y[start + k] = part_y
            if near:
                start = get["got_x"].shape[0] - 4
                for k in range(4):
                    spot = info[0] ^ k
                    value = get["near"][spot].astype(full)
                    value = value + get["got_x"][start + spot].astype(full)
                    value = value + get["got_y"][start + spot].astype(full)
                    out[k][...] = value.astype(out[k].dtype)
                del out[:4]
            if last:
                value = get["held0"][...]
                for k in (1, 2, 3):
                    value = value + get["held%d" % k][...].astype(full)
                out[0][...] = value.astype(low)

        results = list(
            self.chain.run(
                "scatter_step", kernel, args, specs, outs, out_specs, grid=(PIECE // PIECE_TILE,)
            )
        )
        if mid:
            self.got = (flip(results[0], "x"), flip(results[1], "y"))
            del results[:2]
        if near:
            self.held = [results[0]] + [z_trade(results[k], k) for k in (1, 2, 3)]
            del results[:4]
        if last:
            self.done.append(results[0])


def collect_sums(chain, sums):
    spots = [(4, 0), (4, 1), (3, 2), (3, 0), (3, 1), (2, 2), (2, 0), (2, 1), (1, 2), (1, 0), (1, 1), (0, 0)]

    def kernel(info, *refs):
        for row, (at, spot) in enumerate(spots):
            refs[-1][row : row + 1] = refs[at][spot : spot + 1]

    out = shape_of((len(spots), sums[0].shape[1]), full)
    (result,) = chain.run(
        "collect_sums", kernel, list(sums), [whole(v) for v in sums], [out], [whole(out)]
    )
    return result


def add_all(chain, *values):
    def kernel(info, *refs):
        total = refs[0][...]
        for other in refs[1:-1]:
            total = total + other[...]
        refs[-1][...] = total

    out = shape_of(values[0].shape, full)
    (result,) = chain.run(
        "add_all", kernel, list(values), [whole(a) for a in values], [out], [whole(out)]
    )
    return result


def join_pieces(chain, pieces, *copied):
    count = len(pieces)

    def kernel(info, *refs):
        out = refs[count + len(copied)]
        for at in range(count):
            out[:, at * PIECE : (at + 1) * PIECE] = refs[at][...]
        for at in range(len(copied)):
            refs[count + len(copied) + 1 + at][...] = refs[count + at][...]

    args = list(pieces) + list(copied)
    outs = [shape_of((64, PIECE * count))] + [shape_of(v.shape) for v in copied]
    return chain.run(
        "join_pieces", kernel, args, [whole(v) for v in args], outs, [whole(v) for v in outs]
    )


def gelu_and_slope(values):
    bell = jnp.exp(-0.5 * values * values)
    t = 1.0 / (1.0 + (0.3275911 * HALF_ROOT) * jnp.abs(values))
    poly = t * (
        0.254829592
        + t * (-0.284496736 + t * (1.421413741 + t * (-1.453152027 + t * 1.061405429)))
    )
    tail = 0.5 * poly * bell
    phi = jnp.where(values >= 0, 1.0 - tail, tail)
    return values * phi, phi + (PHI_AT_ZERO * values) * bell


ROW_TILE = 320


def flip_rows(pair):
    return tuple(flip(part, "c") for part in pair)


def both_kernel(info, *refs, kind):
    weight = refs[4][...]
    for part in range(4):
        half = part // 2
        rows = slice(part % 2 * ROW_TILE, (part % 2 + 1) * ROW_TILE)
        product = jnp.dot(refs[part][...], weight, preferred_element_type=full)
        if kind == "gelu":
            act, slope = gelu_and_slope(product)
            refs[5][half, rows] = act.astype(low)
            refs[6][half, rows] = slope.astype(low)
        elif kind == "slope":
            refs[6][half, rows] = (product * refs[5][half, rows].astype(full)).astype(low)
        else:
            refs[5][half, rows] = product.astype(low)


def both_times(chain, kind, own, other, weight, slope=None, waits=()):
    depth = weight.shape[0]
    rows = 2 * ROW_TILE
    width = weight.shape[1]
    tile = 256 if kind == "gelu" else 512
    out_spec = pl.BlockSpec((2, rows, tile), lambda j, info: (0, 0, j))
    extra = [] if slope is None else [slope]
    count = 2 if kind == "gelu" else 1
    return chain.run(
        "both_" + kind,
        lambda *refs: both_kernel(*refs, kind=kind),
        [*own, *other, weight] + extra,
        [whole_once(part) for part in (*own, *other)]
        + [pl.BlockSpec((depth, tile), lambda j, info: (0, j))]
        + [out_spec] * len(extra),
        [shape_of((2, rows, width))] * count,
        [out_spec] * count,
        grid=(width // tile,),
        waits=waits,
    )


def times_back(values, weight):
    return lax.dot_general(
        values, weight, (((1,), (1,)), ((), ())), preferred_element_type=full
    ).astype(low)


def other_rows(chain, values, weight):
    rows, depth = values.shape[1:]
    width = weight.shape[0]
    tile = 256

    def kernel(info, rows_in, weight_in, first, second):
        result = times_back(rows_in[0], weight_in[...])
        first[...] = result[:ROW_TILE]
        second[...] = result[ROW_TILE:]

    half = pl.BlockSpec((ROW_TILE, tile), lambda j, info: (0, j))
    results = chain.run(
        "other_rows",
        kernel,
        [values, weight],
        [
            pl.BlockSpec(
                (1, rows, depth), lambda j, info: (1, 0, 0), pipeline_mode=pl.Buffered(1)
            ),
            pl.BlockSpec((tile, depth), lambda j, info: (j, 0)),
        ],
        [shape_of((ROW_TILE, width))] * 2,
        [half] * 2,
        grid=(width // tile,),
    )
    return flip_rows(results)


def put_half(pair, values):
    @pl.when(pl.program_id(0) == 0)
    def _():
        pair[0][...] = values

    @pl.when(pl.program_id(0) == 1)
    def _():
        pair[1][...] = values


def get_half(pair):
    return jnp.where(pl.program_id(0) == 0, pair[0][...].astype(full), pair[1][...].astype(full))


def shown_rows(info):
    first = pl.program_id(0) * ROW_TILE
    row = first + lax.broadcasted_iota(jnp.int32, (ROW_TILE, 1), 0)
    return (row < info[3] * 128).astype(full)


def norm_and_move(values, shift, scale):
    center = values - jnp.mean(values, axis=-1, keepdims=True)
    spread = jnp.mean(center * center, axis=-1, keepdims=True)
    inverse = lax.rsqrt(spread + epsilon)
    normed = center * inverse
    return normed.astype(low), inverse, (normed * (1.0 + scale) + shift).astype(low)


def row_specs(model_width):
    tall = pl.BlockSpec((ROW_TILE, model_width), lambda i, info: (i, 0))
    thin = pl.BlockSpec((ROW_TILE, 1), lambda i, info: (i, 0))
    return tall, thin


def first_norm(chain, current, traded, rows_of):
    rows, model_width = current.shape
    tall, thin = row_specs(model_width)

    def kernel(info, ours, theirs, given, kept, normed, inverse, *moved):
        values = jnp.where(info[4] == 1, ours[...].astype(full), theirs[...].astype(full))
        kept[...] = values.astype(low)
        normed[...], inverse[...], result = norm_and_move(values, given[0:1], given[1:2])
        put_half(moved, result)

    half = shape_of((ROW_TILE, model_width))
    kept, normed, inverse, *moved = chain.run(
        "first_norm",
        kernel,
        [current, traded, rows_of],
        [tall, tall, whole_once(rows_of)],
        [shape_of(current.shape)] * 2 + [shape_of((rows, 1), full), half, half],
        [tall, tall, thin, whole(half), whole(half)],
        grid=(rows // ROW_TILE,),
    )
    return kept, normed, inverse, moved


def forward_step(chain, values, weight, away, current, rows_of, last, waits=()):
    rows, model_width = current.shape
    depth = values.shape[2]
    tall, thin = row_specs(model_width)

    def kernel(info, own, weight_in, first, second, current_in, given, after, branch_out, *rest):
        branch = times_back(own[0], weight_in[...]).astype(full) + get_half((first, second))
        total = current_in[...].astype(full) + shown_rows(info) * given[0:1] * branch
        after[...] = total.astype(after.dtype)
        branch_out[...] = branch.astype(low)
        if not last:
            normed, inverse, *moved = rest
            normed[...], inverse[...], result = norm_and_move(total, given[1:2], given[2:3])
            put_half(moved, result)

    outs = [shape_of(current.shape, low if last else full), shape_of(current.shape)]
    specs = [tall, tall]
    if not last:
        half = shape_of((ROW_TILE, model_width))
        outs += [shape_of(current.shape), shape_of((rows, 1), full), half, half]
        specs += [tall, thin, whole(half), whole(half)]
    results = chain.run(
        "forward_step",
        kernel,
        [values, weight, *away, current, rows_of],
        [
            pl.BlockSpec((1, ROW_TILE, depth), lambda i, info: (0, i, 0)),
            whole_once(weight),
            whole_once(away[0]),
            whole_once(away[1]),
            tall,
            whole_once(rows_of),
        ],
        outs,
        specs,
        grid=(rows // ROW_TILE,),
        waits=waits,
    )
    return results if last else (*results[:4], results[4:])


def add_rows(out, at, values):
    total = jnp.sum(values, axis=0, keepdims=True)

    @pl.when(pl.program_id(0) == 0)
    def _():
        out[at : at + 1] = total

    @pl.when(pl.program_id(0) > 0)
    def _():
        out[at : at + 1] += total


def first_back(chain, state, branch, gate):
    rows, model_width = state.shape
    tall, _ = row_specs(model_width)

    def kernel(info, state_in, branch_in, gate_in, first, second, sums):
        values = state_in[...].astype(full) * shown_rows(info)
        put_half((first, second), (values * gate_in[...]).astype(low))
        add_rows(sums, 0, values * branch_in[...].astype(full))

    sums = shape_of((8, model_width), full)
    half = shape_of((ROW_TILE, model_width))
    first, second, sums = chain.run(
        "first_back",
        kernel,
        [state, branch, gate],
        [tall, tall, whole_once(gate)],
        [half, half, sums],
        [whole(half), whole(half), whole(sums)],
        grid=(rows // ROW_TILE,),
    )
    return (first, second), sums


def backward_step(chain, values, weight, away, normed, inverse, state, rows_of, branch):
    rows, model_width = state.shape
    depth = values.shape[2]
    tall, thin = row_specs(model_width)
    last = branch is None

    def kernel(
        info, own, weight_in, first, second, normed_in, inverse_in, state_in, given, *rest
    ):
        grad = times_back(own[0], weight_in[...]).astype(full) + get_half((first, second))
        normal = normed_in[...].astype(full)
        moved = grad * (1.0 + given[0:1])
        first_mean = jnp.mean(moved, axis=-1, keepdims=True)
        second_mean = jnp.mean(moved * normal, axis=-1, keepdims=True)
        total = state_in[...].astype(full) + inverse_in[...] * (
            moved - first_mean - normal * second_mean
        )
        if last:
            state_out, sums = rest
        else:
            branch_in, state_out, sums, *sent = rest
        state_out[...] = total.astype(state_out.dtype)
        add_rows(sums, 0, grad)
        add_rows(sums, 1, grad * normal)
        if not last:
            shown = total * shown_rows(info)
            put_half(sent, (shown * given[1:2]).astype(low))
            add_rows(sums, 2, shown * branch_in[...].astype(full))

    sums = shape_of((8, model_width), full)
    outs = [shape_of(state.shape, low if last else full), sums]
    specs = [tall, whole(sums)]
    if not last:
        half = shape_of((ROW_TILE, model_width))
        outs += [half, half]
        specs += [whole(half)] * 2
    extra = [] if last else [branch]
    results = chain.run(
        "backward_step",
        kernel,
        [values, weight, *away, normed, inverse, state, rows_of] + extra,
        [
            pl.BlockSpec((1, ROW_TILE, depth), lambda i, info: (0, i, 0)),
            whole_once(weight),
            whole_once(away[0]),
            whole_once(away[1]),
            tall,
            thin,
            tall,
            whole_once(rows_of),
        ]
        + [tall] * len(extra),
        outs,
        specs,
        grid=(rows // ROW_TILE,),
    )
    return results if last else (*results[:2], results[2:])


def attend_kernel(info, blocks, joined, mixed, probs, bias, *, heads, cells, masked, sides):
    width = heads * HEAD_DIM

    @pl.when((pl.program_id(0) == 0) & (pl.program_id(1) == 0))
    def _():
        for h in range(heads):
            for place, spots in enumerate(sides):
                block = blocks[h, place]
                for row, col in spots:
                    bias[h, row * 64 : row * 64 + 64, col * 64 : col * 64 + 64] = block

    values = joined[...].reshape(cells, 3 * width)
    lead = mixed.shape
    if masked:
        column = lax.broadcasted_iota(jnp.int32, (1, cells), 1)
        shown = column < info[3] * (WIN_T * WIN_T)
    outs = []
    for h in range(heads):
        cols = slice(h * HEAD_DIM, (h + 1) * HEAD_DIM)
        query = values[:, cols]
        key = values[:, width + h * HEAD_DIM : width + (h + 1) * HEAD_DIM]
        value = values[:, 2 * width + h * HEAD_DIM : 2 * width + (h + 1) * HEAD_DIM]
        scores = lax.dot_general(
            query, key, (((1,), (1,)), ((), ())), preferred_element_type=full
        ) * HEAD_DIM ** (-0.5) + bias[h].astype(full)
        if masked:
            scores = jnp.where(shown, scores, masked_score)
        weights = jnp.exp(scores - jnp.max(scores, axis=-1, keepdims=True))
        share = (weights * (1.0 / jnp.sum(weights, axis=-1, keepdims=True))).astype(low)
        probs[0, h] = share
        outs.append(jnp.dot(share, value, preferred_element_type=full).astype(low))
    mixed[...] = jnp.concatenate(outs, axis=1).reshape(lead)


def attend_back_kernel(info, joined, grad, probs, back, bias_out, total, *, heads, cells, sides):
    step = pl.program_id(0) * pl.num_programs(1) + pl.program_id(1)
    width = heads * HEAD_DIM
    values = joined[...].reshape(cells, 3 * width)
    grads = grad[...].reshape(cells, width)
    grads_t = grads.astype(full).T.astype(low)
    queries_t = values[:, :width].astype(full).T.astype(low)
    queries, keys_t, values_t = [], [], []

    @pl.when(step == 0)
    def _():
        total[...] = jnp.zeros(total.shape, full)

    for h in range(heads):
        cols = slice(h * HEAD_DIM, (h + 1) * HEAD_DIM)
        key = values[:, width + h * HEAD_DIM : width + (h + 1) * HEAD_DIM]
        value = values[:, 2 * width + h * HEAD_DIM : 2 * width + (h + 1) * HEAD_DIM]
        share = probs[0, h]
        values_t.append(jnp.dot(grads_t[cols], share, preferred_element_type=full).astype(low))
        grad_share = lax.dot_general(
            grads[:, cols], value, (((1,), (1,)), ((), ())), preferred_element_type=full
        )
        share_full = share.astype(full)
        product = share_full * grad_share
        row_dot = jnp.sum(product, axis=-1, keepdims=True)
        grad_scores = (product - share_full * row_dot).astype(low)
        total[h] += grad_scores.astype(full)
        queries.append(
            (jnp.dot(grad_scores, key, preferred_element_type=full) * HEAD_DIM ** (-0.5)).astype(
                low
            )
        )
        keys_t.append(
            (
                jnp.dot(queries_t[cols], grad_scores, preferred_element_type=full)
                * HEAD_DIM ** (-0.5)
            ).astype(low)
        )
    key_grads = jnp.concatenate(keys_t, axis=0).astype(full).T.astype(low)
    value_grads = jnp.concatenate(values_t, axis=0).astype(full).T.astype(low)
    back[...] = jnp.concatenate(queries + [key_grads, value_grads], axis=1).reshape(back.shape)

    @pl.when(step == pl.num_programs(0) * pl.num_programs(1) - 1)
    def _():
        for h in range(heads):
            for place, spots in enumerate(sides):
                part = None
                for row, col in spots:
                    block = total[h, row * 64 : row * 64 + 64, :][:, col * 64 : col * 64 + 64]
                    part = block if part is None else part + block
                bias_out[h, place] = part


def spatial_sides():
    sides = [[] for _ in range(9)]
    for row in range(4):
        for col in range(4):
            place = (row // 2 - col // 2 + 1) * 3 + (row % 2 - col % 2 + 1)
            sides[place].append((row, col))
    return sides


def joint_sides():
    sides = [[] for _ in range(2 * FRAMES - 1)]
    for row in range(FRAMES):
        for col in range(FRAMES):
            sides[row - col + FRAMES - 1].append((row, col))
    return sides


def window_specs(is_joint, frames, width):
    if is_joint:
        shape, at = (1, frames, 1, 64, width), lambda i, j, info: (i, 0, j, 0, 0)
    else:
        shape, at = (2, 1, 2, 64, width), lambda i, j, info: (0, j, 0, 0, 0)
    return pl.BlockSpec(shape, at)


def attend(chain, blocks, joined, is_joint):
    frames = joined.shape[1]
    heads = blocks.shape[0]
    width = heads * HEAD_DIM
    grid = (2, 2) if is_joint else (1, frames)
    cells = 64 * frames if is_joint else 256
    number = grid[0] * grid[1]
    sides = joint_sides() if is_joint else spatial_sides()
    fetch = lambda i, j, info: (i * grid[1] + j, 0, 0, 0)
    return chain.run(
        "attend_joint" if is_joint else "attend_spatial",
        lambda *refs: attend_kernel(
            *refs, heads=heads, cells=cells, masked=is_joint, sides=sides
        ),
        [blocks, joined],
        [whole_once(blocks), window_specs(is_joint, frames, 3 * width)],
        [shape_of(joined.shape[:4] + (width,)), shape_of((number, heads, cells, cells))],
        [window_specs(is_joint, frames, width), pl.BlockSpec((1, heads, cells, cells), fetch)],
        grid=grid,
        scratch=[pltpu.VMEM((heads, cells, cells), low)],
    )


def attend_back(chain, joined, grad, probs, is_joint):
    frames = joined.shape[1]
    number, heads, cells, _ = probs.shape
    width = heads * HEAD_DIM
    grid = (2, 2) if is_joint else (1, frames)
    sides = joint_sides() if is_joint else spatial_sides()
    fetch = lambda i, j, info: (i * grid[1] + j, 0, 0, 0)
    sums = shape_of((heads, 9, 64, 64), full)
    return chain.run(
        "attend_back_joint" if is_joint else "attend_back_spatial",
        lambda *refs: attend_back_kernel(*refs, heads=heads, cells=cells, sides=sides),
        [joined, grad, probs],
        [
            window_specs(is_joint, frames, 3 * width),
            window_specs(is_joint, frames, width),
            pl.BlockSpec((1, heads, cells, cells), fetch),
        ],
        [shape_of(joined.shape), sums],
        [window_specs(is_joint, frames, 3 * width), whole(sums)],
        grid=grid,
        scratch=[pltpu.VMEM((heads, cells, cells), full)],
        extra=6,
    )


def offset_hot():
    places = np.arange(WIN_T * WIN_T)
    rows = places[:, None] // WIN_T - places[None, :] // WIN_T + WIN_T - 1
    cols = places[:, None] % WIN_T - places[None, :] % WIN_T + WIN_T - 1
    spots = (rows * (2 * WIN_T - 1) + cols).reshape(-1).astype(np.int32)
    return jnp.arange((2 * WIN_T - 1) ** 2, dtype=jnp.int32)[:, None] == jnp.asarray(spots)[None]


def fast_local(
    latents,
    cotangent,
    frame_counts,
    band_ids,
    class_ids,
    time_table,
    class_table,
    ada_weight,
    ada_bias,
    qkv_weight,
    out_weight,
    up_weight,
    down_weight,
    spatial_bias,
    joint_bias,
):
    frames = latents.shape[1]
    model_width = latents.shape[4]
    heads = spatial_bias.shape[0]
    width = heads * HEAD_DIM
    hidden = up_weight.shape[2]
    col_width = ada_weight.shape[2]
    rows = frames * 128
    z, y, c, x = (lax.axis_index(name) for name in ("z", "y", "c", "x"))
    counts = frame_counts.astype(full)
    count = jnp.where(c == x, counts, flip(counts, "c")).astype(jnp.int32)
    same = (c == x).astype(jnp.int32)
    chain = Chain(
        jnp.concatenate([jnp.stack([z, y, x]).astype(jnp.int32), count, same.reshape(1)])
    )

    def rearranged(values):
        shaped = values.reshape(frames, 8, 2, 8, model_width).transpose(0, 2, 1, 3, 4)
        return shaped.reshape(rows, model_width)

    qkv_rows = qkv_weight.reshape(2, -1, 3 * width)
    out_rows = out_weight.transpose(0, 2, 1)
    down_rows = down_weight.transpose(0, 2, 1)
    first_shard = swap(jnp.concatenate([qkv_rows[0], out_rows[0]], axis=1))
    band_hot = (band_ids[:, None] == jnp.arange(BANDS)[None, :]).astype(low)
    class_hot = (class_ids[:, None] == jnp.arange(CLASSES)[None, :]).astype(low)
    condition = jnp.dot(band_hot, time_table, preferred_element_type=full) + jnp.dot(
        class_hot, class_table, preferred_element_type=full
    )
    activity = jax.nn.silu(condition).astype(low)
    everyone = ("z", "y", "c", "x")
    mod_part = jnp.einsum(
        "cd,bde->cbe", activity, ada_weight, preferred_element_type=full
    ) + ada_bias[None].astype(full)
    mod_part = jnp.broadcast_to(
        mod_part.reshape(8, 1, 2, 2, col_width), (8, 2, 2, 2, col_width)
    ).reshape(32, 2, col_width)
    own_mod = lax.all_to_all(mod_part, everyone, split_axis=0, concat_axis=0, tiled=True)
    own_mod = own_mod.transpose(1, 0, 2).reshape(2, 6, model_width)
    rows_of = lambda *items: jnp.stack([own_mod[k, at] for k, at in items])

    hot = offset_hot()
    wide = 2 * WIN_T - 1
    square = spatial_bias.reshape(heads, 2 * WIN_S - 1, 2 * WIN_S - 1)
    spatial_parts = jnp.stack(
        [
            square[:, 8 * a : 8 * a + wide, 8 * b : 8 * b + wide].reshape(heads, -1)
            for a in range(3)
            for b in range(3)
        ],
        axis=1,
    )
    parts = swap(jnp.concatenate([spatial_parts, joint_bias.reshape(heads, 9, -1)]))
    blocks = jnp.dot(
        parts.reshape(heads * 18, wide * wide), hot.astype(low), preferred_element_type=full
    ).astype(low)
    blocks = blocks.reshape(2, heads, 9, 64, 64)
    near = blocks[0].reshape(heads, 3, 3, 64, 64)
    near = jnp.where(c == 0, near, near[:, ::-1])
    bias_blocks = [near.reshape(heads, 9, 64, 64), blocks[1]]

    windowed = lambda values: values.reshape(2, frames, 2, 64, values.shape[-1])

    chain.wait(own_mod, parts)
    latent_rows, packed = pack_arguments(
        chain, rearranged(latents), up_weight, down_rows, qkv_rows, out_rows
    )
    traded_rows, traded = swap_only(latent_rows), swap_only(packed)
    gather = Gather(chain, [first_shard] + [None] * 5)
    gather.over_z(0)
    gather.step()
    cuts = [shape_of((64, PIECE))] * 5
    gather.shards[1:] = chain.run(
        "cut_shards",
        cut_kernel,
        [packed, traded],
        [whole(packed)] * 2,
        cuts,
        [whole(a) for a in cuts],
    )
    gather.over_z(1)
    chain.wait(*bias_blocks)
    latent_rows, normed_0, inverse_0, moved_0 = first_norm(
        chain, latent_rows, traded_rows, rows_of((0, 0), (0, 1))
    )
    other_0 = flip_rows(moved_0)
    gather.step()
    gather.over_z(2)
    gather.step()
    gather.over_z(3)
    qkv_0, out_0 = gather.place(0, [3 * width, width])
    (joined_0,) = both_times(chain, "plain", moved_0, other_0, qkv_0)
    joined_0 = windowed(joined_0)
    mixed_0, probs_0 = attend(chain, bias_blocks[0], joined_0, False)
    mixed_0 = mixed_0.reshape(2, rows, width)
    away = other_rows(chain, mixed_0, out_0)
    gather.step()
    gather.over_z(4)
    (up_0,) = gather.place(1, [hidden])
    after_0, branch_one_0, normed_1, inverse_1, moved_1 = forward_step(
        chain, mixed_0, out_0, away, latent_rows, rows_of((0, 2), (0, 3), (0, 4)), False
    )
    other_1 = flip_rows(moved_1)
    act_0, slope_0 = both_times(chain, "gelu", moved_1, other_1, up_0)
    gather.step()
    gather.over_z(5)
    (down_0,) = gather.place(2, [hidden])
    away = other_rows(chain, act_0, down_0)
    current_1, branch_two_0, normed_2, inverse_2, moved_2 = forward_step(
        chain, act_0, down_0, away, after_0, rows_of((0, 5), (1, 0), (1, 1)), False
    )
    other_2 = flip_rows(moved_2)

    gather.step()
    qkv_1, out_1 = gather.place(3, [3 * width, width])
    (joined_1,) = both_times(chain, "plain", moved_2, other_2, qkv_1)
    joined_1 = windowed(joined_1)
    mixed_1, probs_1 = attend(chain, bias_blocks[1], joined_1, True)
    mixed_1 = mixed_1.reshape(2, rows, width)
    away = other_rows(chain, mixed_1, out_1)
    gather.step()
    (up_1,) = gather.place(4, [hidden])
    after_1, branch_one_1, normed_3, inverse_3, moved_3 = forward_step(
        chain, mixed_1, out_1, away, current_1, rows_of((1, 2), (1, 3), (1, 4)), False
    )
    other_3 = flip_rows(moved_3)
    traded_cotangent = swap(rearranged(cotangent))
    act_1, slope_1 = both_times(chain, "gelu", moved_3, other_3, up_1)
    (down_1,) = gather.place(5, [hidden])
    away = other_rows(chain, act_1, down_1)
    final, branch_two_1 = forward_step(
        chain, act_1, down_1, away, after_1, rows_of((1, 5)), True
    )

    def restored(sent):
        shaped = sent.reshape(frames, 2, 8, 8, model_width).transpose(0, 2, 1, 3, 4)
        return shaped.astype(full).reshape(1, frames, 8, 16, model_width)

    traded_final = swap(final)

    exact = lax.Precision.HIGHEST
    hot_wide = jnp.pad(hot.astype(full), ((0, 256 - wide * wide), (0, 0)))
    table_sums = lambda sums: jnp.dot(
        sums.reshape(heads * 9, 64 * 64), hot_wide.T, precision=exact
    )

    state = traded_cotangent
    own_g, sums_a = first_back(chain, state, branch_two_1, rows_of((1, 5)))
    other_g = flip_rows(own_g)
    scatter = Scatter(chain)
    (hidden_g,) = both_times(chain, "slope", own_g, other_g, down_1, slope_1)
    away = other_rows(chain, hidden_g, up_1)
    scatter.weight_grad((own_g, other_g, act_1))
    state, sums_b, own_g = backward_step(
        chain, hidden_g, up_1, away, normed_3, inverse_3, state, rows_of((1, 4), (1, 2)), branch_one_1
    )
    other_g = flip_rows(own_g)
    scatter.weight_grad((moved_3, other_3, hidden_g))
    chain.wait(traded_final)
    scatter.step(6)
    (mixed_g,) = both_times(chain, "plain", own_g, other_g, out_1)
    back, joint_sums = attend_back(chain, joined_1, windowed(mixed_g), probs_1, True)
    joint_tables = table_sums(joint_sums)
    back = back.reshape(2, rows, 3 * width)
    away = other_rows(chain, back, qkv_1)
    scatter.weight_grad((moved_2, other_2, back), (own_g, other_g, mixed_1))
    scatter.step(6)
    state, sums_c, own_g = backward_step(
        chain, back, qkv_1, away, normed_2, inverse_2, state, rows_of((1, 1), (0, 5)), branch_two_0
    )
    other_g = flip_rows(own_g)

    (hidden_g,) = both_times(chain, "slope", own_g, other_g, down_0, slope_0)
    away = other_rows(chain, hidden_g, up_0)
    scatter.weight_grad((own_g, other_g, act_0))
    chain.wait(joint_tables)
    scatter.step(6)
    state, sums_d, own_g = backward_step(
        chain, hidden_g, up_0, away, normed_1, inverse_1, state, rows_of((0, 4), (0, 2)), branch_one_0
    )
    other_g = flip_rows(own_g)
    scatter.weight_grad((moved_1, other_1, hidden_g))
    (mixed_g,) = both_times(chain, "plain", own_g, other_g, out_0)
    scatter.step(6)
    first_done = swap(join_pieces(chain, scatter.done[:2])[0])
    back, spatial_sums = attend_back(chain, joined_0, windowed(mixed_g), probs_0, False)
    back = back.reshape(2, rows, 3 * width)
    away = other_rows(chain, back, qkv_0)
    scatter.weight_grad((moved_0, other_0, back), (own_g, other_g, mixed_0))
    chain.wait(first_done)
    scatter.step(6)
    state, sums_e = backward_step(
        chain, back, qkv_0, away, normed_0, inverse_0, state, rows_of((0, 1)), None
    )
    output = restored(traded_final)

    chain.wait(*scatter.held[1:])
    grad_mod = collect_sums(chain, [sums_a, sums_b, sums_c, sums_d, sums_e])
    ordered = grad_mod.reshape(2, 32, col_width).transpose(1, 0, 2)
    cols = lax.all_to_all(ordered, everyone, split_axis=0, concat_axis=0, tiled=True)
    cols = cols.reshape(8, 2, 2, 2, col_width)
    cols = (cols[:, 0] + cols[:, 1]).reshape(16, 2, col_width)
    grad_ada_weight = jnp.einsum("cd,cbe->bde", activity.astype(full), cols, precision=exact)
    grad_ada_bias = jnp.sum(cols, axis=0)
    grad_activity = jnp.einsum("cbe,bde->cd", cols, ada_weight.astype(full), precision=exact)

    near = spatial_sums.reshape(heads, 3, 3, 64, 64)
    near = jnp.where(c == 0, near, near[:, ::-1]).reshape(heads, 9, 64, 64)
    tables = jnp.concatenate([table_sums(near), joint_tables])

    shared = jnp.concatenate([grad_activity.reshape(-1, 256), tables])
    chain.wait(shared)
    scatter.step(6)
    scatter.step(6)
    sent = flip(shared, "x")
    early, state_copy = join_pieces(chain, scatter.done[2:], state)
    early = swap(early)
    traded_state = swap(state_copy)
    shared = add_all(chain, shared, sent)
    shared = add_all(chain, shared, flip(shared, "y"))
    sent = [z_trade(shared, k) for k in (1, 2, 3)]
    scatter.step(6)
    late = swap(scatter.done[5]).astype(full)
    shared = add_all(chain, shared, *sent)
    tables = shared[-heads * 18 :]
    across = flip(shared, "c")
    grad_activity = (shared + across)[: -heads * 18].reshape(16, model_width)
    tables = jnp.where(c == x, tables, across[-heads * 18 :])[:, : wide * wide]
    grad_latents = restored(traded_state)
    done = jnp.concatenate([first_done, early], axis=1).astype(full)
    piece = lambda at: done[:, at * PIECE : (at + 1) * PIECE]
    grad_down = jnp.stack([piece(3).T, piece(0).T])
    grad_up = jnp.stack([piece(4), piece(1)])
    grad_qkv = jnp.stack([late[:, : 3 * width], piece(2)[:, : 3 * width]])
    grad_out = jnp.stack([late[:, 3 * width :].T, piece(2)[:, 3 * width :].T])

    tables = tables.reshape(2, heads, 9, wide, wide)
    grad_joint = tables[1].reshape(heads, 9 * wide * wide)
    near = tables[0].reshape(heads, 3, 3, wide, wide)
    long = 2 * WIN_S - 1
    grad_spatial = 0.0
    for a in range(3):
        for b in range(3):
            grad_spatial = grad_spatial + jnp.pad(
                near[:, a, b],
                ((0, 0), (8 * a, long - wide - 8 * a), (8 * b, long - wide - 8 * b)),
            )
    grad_spatial = grad_spatial.reshape(heads, long * long)
    grad_condition = jax.vjp(jax.nn.silu, condition)[1](grad_activity)[0]
    grad_time = jnp.dot(band_hot.astype(full).T, grad_condition, precision=exact)
    grad_class = jnp.dot(class_hot.astype(full).T, grad_condition, precision=exact)

    return (
        output,
        grad_latents,
        grad_time,
        grad_class,
        grad_ada_weight,
        grad_ada_bias,
        grad_qkv.reshape(2, -1, 3, width),
        grad_out,
        grad_up,
        grad_down,
        grad_spatial,
        grad_joint,
    )


def solution(mesh):
    if mesh.shape["dp"] != 16 or mesh.shape["mp"] != 2:
        return solution_any(mesh)
    fine = Mesh(mesh.devices.reshape(4, 2, 2, 2), ("z", "y", "c", "x"))
    dp, mp = ("z", "y", "c"), "x"
    both = dp + (mp,)
    tokens = P(dp, None, mp, None, None)
    weight_specs = (
        P(None, None, both),
        P(None, both),
        P(None, dp, None, mp),
        P(None, mp, dp),
        P(None, dp, mp),
        P(None, mp, dp),
        P(mp, None),
        P(mp, None),
    )
    return jax.shard_map(
        fast_local,
        mesh=fine,
        in_specs=(tokens, tokens, P(dp), P(), P(), P(), P()) + weight_specs,
        out_specs=(tokens, tokens, P(), P()) + weight_specs,
        check_vma=False,
    )
```

```python
import jax
import jax.numpy as jnp
import numpy as np
from jax import lax
from jax.experimental import pallas as pl
from jax.experimental.pallas import tpu as pltpu
from jax.sharding import Mesh
from jax.sharding import PartitionSpec as P

HEAD_DIM = 64
CLASSES = 101
BANDS = 32
FRAMES = 5
WIN_S = 16
WIN_T = 8


epsilon = 1e-06
masked_score = -1e30


def spatial_table():
    places = np.arange(WIN_S * WIN_S)
    row_at = places // WIN_S
    col_at = places % WIN_S
    row_rel = row_at[:, None] - row_at[None, :] + WIN_S - 1
    col_rel = col_at[:, None] - col_at[None, :] + WIN_S - 1
    return (row_rel * (2 * WIN_S - 1) + col_rel).astype(np.int32)


def joint_table():
    places = np.arange(FRAMES * WIN_T * WIN_T)
    time_at = places // (WIN_T * WIN_T)
    row_at = places // WIN_T % WIN_T
    col_at = places % WIN_T
    time_rel = time_at[:, None] - time_at[None, :] + FRAMES - 1
    row_rel = row_at[:, None] - row_at[None, :] + WIN_T - 1
    col_rel = col_at[:, None] - col_at[None, :] + WIN_T - 1
    return ((time_rel * (2 * WIN_T - 1) + row_rel) * (2 * WIN_T - 1) + col_rel).astype(np.int32)


def to_windows(values, window, is_joint):
    clip_count, frames, side_cells, channels = (
        values.shape[0],
        values.shape[1],
        values.shape[2],
        values.shape[4],
    )
    per_side = side_cells // window
    if is_joint:
        shaped = values.reshape(clip_count, frames, per_side, window, per_side, window, channels)
        shaped = shaped.transpose(0, 2, 4, 1, 3, 5, 6)
        return shaped.reshape(clip_count * per_side * per_side, frames * window * window, channels)
    shaped = values.reshape(clip_count, frames, per_side, window, per_side, window, channels)
    shaped = shaped.transpose(0, 1, 2, 4, 3, 5, 6)
    return shaped.reshape(clip_count * frames * per_side * per_side, window * window, channels)


def from_windows(values, clip_count, frames, side_cells, window, is_joint):
    per_side = side_cells // window
    channels = values.shape[-1]
    if is_joint:
        shaped = values.reshape(clip_count, per_side, per_side, frames, window, window, channels)
        shaped = shaped.transpose(0, 3, 1, 4, 2, 5, 6)
    else:
        shaped = values.reshape(clip_count, frames, per_side, per_side, window, window, channels)
        shaped = shaped.transpose(0, 1, 2, 4, 3, 5, 6)
    return shaped.reshape(clip_count, frames, side_cells, side_cells, channels)


def normalize(values):
    center = values - jnp.mean(values, axis=-1, keepdims=True)
    spread = jnp.mean(center * center, axis=-1, keepdims=True)
    inverse = lax.rsqrt(spread + epsilon)
    return (center * inverse, inverse)


def norm_back(grad_normed, normed, inverse):
    first_mean = jnp.mean(grad_normed, axis=-1, keepdims=True)
    second_mean = jnp.mean(grad_normed * normed, axis=-1, keepdims=True)
    return inverse * (grad_normed - first_mean - normed * second_mean)


def exact_gelu(values):
    return jax.nn.gelu(values, approximate=False)


def gather_rows(values):
    return lax.all_gather(values, "mp", axis=2, tiled=True)


def sum_rows(values):
    return lax.psum_scatter(
        values.astype(jnp.bfloat16), "mp", scatter_dimension=2, tiled=True
    ).astype(jnp.float32)


def gather_grads(values):
    return lax.all_gather(values, "mp", axis=2, tiled=True)


def input_sums(values):
    return lax.psum_scatter(
        values.astype(jnp.bfloat16), "mp", scatter_dimension=2, tiled=True
    ).astype(jnp.float32)


def inputs_again(moved):
    return lax.all_gather(moved, "mp", axis=2, tiled=True)


def attention_scores(query_part, key_part, bias_matrix, key_valid):
    scores = (
        jnp.einsum("nqhe,nkhe->nhqk", query_part, key_part, preferred_element_type=jnp.float32)
        * HEAD_DIM ** (-0.5)
        + bias_matrix[None]
    )
    if key_valid is not None:
        scores = jnp.where(key_valid[:, None, None, :] > 0, scores, masked_score)
    return scores


def local(
    latents,
    cotangent,
    frame_counts,
    band_ids,
    class_ids,
    time_table,
    class_table,
    ada_weight,
    ada_bias,
    qkv_weight,
    out_weight,
    up_weight,
    down_weight,
    spatial_bias,
    joint_bias,
):
    clip_count = latents.shape[0]
    frames = latents.shape[1]
    side_cells = latents.shape[3]
    model_width = latents.shape[4]
    heads_local = spatial_bias.shape[0]
    local_width = heads_local * HEAD_DIM
    dp_count = lax.axis_size("dp")
    mp_count = lax.axis_size("mp")
    col_width = ada_weight.shape[2]
    band_hot = (band_ids[:, None] == jnp.arange(BANDS)[None, :]).astype(jnp.bfloat16)
    class_hot = (class_ids[:, None] == jnp.arange(CLASSES)[None, :]).astype(jnp.bfloat16)
    condition = jnp.dot(band_hot, time_table, preferred_element_type=jnp.float32) + jnp.dot(
        class_hot, class_table, preferred_element_type=jnp.float32
    )
    activity_low = jax.nn.silu(condition).astype(jnp.bfloat16)
    ada_cols, ada_bias_cols = (
        lax.all_gather(ada_weight, "mp", axis=2, tiled=True),
        lax.all_gather(ada_bias, "mp", axis=1, tiled=True),
    )
    mod_part = jnp.einsum(
        "cd,bde->bce", activity_low, ada_cols, preferred_element_type=jnp.float32
    ) + ada_bias_cols[:, None, :].astype(jnp.float32)
    modulation = lax.all_gather(mod_part, "dp", axis=2, tiled=True)
    first_clip = lax.axis_index("dp") * clip_count
    own_mod = lax.dynamic_slice_in_dim(modulation, first_clip, clip_count, 1).reshape(
        2, clip_count, 6, model_width
    )
    frame_valid = (jnp.arange(frames)[None, :] < frame_counts[:, None]).astype(jnp.float32)
    frame_mask = frame_valid[:, :, None, None, None]
    key_frames = np.arange(frames * WIN_T * WIN_T) // (WIN_T * WIN_T)
    joint_cells = key_frames.shape[0]
    per_side = side_cells // WIN_T
    key_valid = frame_valid[:, key_frames]
    key_valid = jnp.broadcast_to(
        key_valid[:, None, :], (clip_count, per_side * per_side, joint_cells)
    ).reshape(clip_count * per_side * per_side, joint_cells)
    w_qkv, w_out, w_up, w_down = (
        lax.all_gather(qkv_weight, "dp", axis=1, tiled=True),
        lax.all_gather(out_weight, "dp", axis=2, tiled=True),
        lax.all_gather(up_weight, "dp", axis=1, tiled=True),
        lax.all_gather(down_weight, "dp", axis=2, tiled=True),
    )
    spatial_index = spatial_table()
    joint_index = joint_table()
    spatial_matrix = spatial_bias.astype(jnp.float32)[:, spatial_index]
    joint_matrix = joint_bias.astype(jnp.float32)[:, joint_index]
    current = latents.astype(jnp.float32)
    stored = []
    for which_block in range(2):
        is_joint = which_block == 1
        window = WIN_T if is_joint else WIN_S
        bias_matrix = joint_matrix if is_joint else spatial_matrix
        mask_keys = key_valid if is_joint else None
        block_mod = own_mod[which_block][:, :, None, None, None, :]
        normed_one, inverse_one = normalize(current)
        moved_one = (normed_one * (1.0 + block_mod[:, 1]) + block_mod[:, 0]).astype(jnp.bfloat16)
        gathered_one = gather_rows(moved_one)
        projected = jnp.einsum(
            "cfyxd,dkh->cfyxkh",
            gathered_one,
            w_qkv[which_block],
            preferred_element_type=jnp.float32,
        ).astype(jnp.bfloat16)
        windows = to_windows(
            projected.reshape(clip_count, frames, side_cells, side_cells, 3 * local_width),
            window,
            is_joint,
        )
        windows = windows.reshape(windows.shape[0], windows.shape[1], 3, heads_local, HEAD_DIM)
        scores = attention_scores(windows[:, :, 0], windows[:, :, 1], bias_matrix, mask_keys)
        row_max = jnp.max(scores, axis=-1, keepdims=True)
        log_total = row_max + jnp.log(jnp.sum(jnp.exp(scores - row_max), axis=-1, keepdims=True))
        probs_low = jnp.exp(scores - log_total).astype(jnp.bfloat16)
        mixed_win = jnp.einsum(
            "nhqk,nkhe->nqhe", probs_low, windows[:, :, 2], preferred_element_type=jnp.float32
        ).astype(jnp.bfloat16)
        mixed_rows = from_windows(
            mixed_win.reshape(mixed_win.shape[0], mixed_win.shape[1], local_width),
            clip_count,
            frames,
            side_cells,
            window,
            is_joint,
        )
        branch_one = sum_rows(
            jnp.einsum(
                "cfyxk,kd->cfyxd",
                mixed_rows,
                w_out[which_block],
                preferred_element_type=jnp.float32,
            )
        )
        after_attn = current + frame_mask * block_mod[:, 2] * branch_one
        normed_two, inverse_two = normalize(after_attn)
        moved_two = (normed_two * (1.0 + block_mod[:, 4]) + block_mod[:, 3]).astype(jnp.bfloat16)
        gathered_two = gather_rows(moved_two)
        hidden = jnp.einsum(
            "cfyxd,dk->cfyxk", gathered_two, w_up[which_block], preferred_element_type=jnp.float32
        )
        activated = exact_gelu(hidden).astype(jnp.bfloat16)
        branch_two = sum_rows(
            jnp.einsum(
                "cfyxk,kd->cfyxd",
                activated,
                w_down[which_block],
                preferred_element_type=jnp.float32,
            )
        )
        current = after_attn + frame_mask * block_mod[:, 5] * branch_two
        stored.append(
            (
                normed_one,
                inverse_one,
                moved_one,
                gathered_one,
                windows,
                log_total,
                mixed_rows,
                branch_one,
                normed_two,
                inverse_two,
                moved_two,
                gathered_two,
                hidden,
                activated,
                branch_two,
            )
        )
    grad_state = cotangent.astype(jnp.float32)
    mod_grads = []
    qkv_grads = []
    out_grads = []
    up_grads = []
    down_grads = []
    table_parts = []
    for which_block in (1, 0):
        is_joint = which_block == 1
        window = WIN_T if is_joint else WIN_S
        bias_matrix = joint_matrix if is_joint else spatial_matrix
        mask_keys = key_valid if is_joint else None
        block_mod = own_mod[which_block][:, :, None, None, None, :]
        (
            normed_one,
            inverse_one,
            moved_one,
            gathered_one,
            windows,
            log_total,
            mixed_rows,
            branch_one,
            normed_two,
            inverse_two,
            moved_two,
            gathered_two,
            hidden,
            activated,
            branch_two,
        ) = stored[which_block]
        grad_gate_two = jnp.sum(frame_mask * grad_state * branch_two, axis=(1, 2, 3))
        grad_rows = gather_grads((frame_mask * block_mod[:, 5] * grad_state).astype(jnp.bfloat16))
        down_grads.append(
            jnp.einsum("cfyxk,cfyxd->kd", activated, grad_rows, preferred_element_type=jnp.float32)
        )
        grad_act = jnp.einsum(
            "cfyxd,kd->cfyxk", grad_rows, w_down[which_block], preferred_element_type=jnp.float32
        )
        grad_hidden = jax.vjp(exact_gelu, hidden)[1](grad_act)[0].astype(jnp.bfloat16)
        inputs_two = inputs_again(moved_two)
        up_grads.append(
            jnp.einsum(
                "cfyxd,cfyxk->dk", inputs_two, grad_hidden, preferred_element_type=jnp.float32
            )
        )
        grad_moved = input_sums(
            jnp.einsum(
                "cfyxk,dk->cfyxd",
                grad_hidden,
                w_up[which_block],
                preferred_element_type=jnp.float32,
            )
        )
        grad_shift_two = jnp.sum(grad_moved, axis=(1, 2, 3))
        grad_scale_two = jnp.sum(grad_moved * normed_two, axis=(1, 2, 3))
        grad_state = grad_state + norm_back(
            grad_moved * (1.0 + block_mod[:, 4]), normed_two, inverse_two
        )
        grad_gate_one = jnp.sum(frame_mask * grad_state * branch_one, axis=(1, 2, 3))
        grad_rows = gather_grads((frame_mask * block_mod[:, 2] * grad_state).astype(jnp.bfloat16))
        out_grads.append(
            jnp.einsum("cfyxk,cfyxd->kd", mixed_rows, grad_rows, preferred_element_type=jnp.float32)
        )
        grad_mixed = jnp.einsum(
            "cfyxd,kd->cfyxk", grad_rows, w_out[which_block], preferred_element_type=jnp.float32
        ).astype(jnp.bfloat16)
        grad_win = to_windows(grad_mixed, window, is_joint)
        grad_win = grad_win.reshape(grad_win.shape[0], grad_win.shape[1], heads_local, HEAD_DIM)
        query_part = windows[:, :, 0]
        key_part = windows[:, :, 1]
        value_part = windows[:, :, 2]
        probs_full = jnp.exp(
            attention_scores(query_part, key_part, bias_matrix, mask_keys) - log_total
        )
        grad_value = jnp.einsum(
            "nhqk,nqhe->nkhe",
            probs_full.astype(jnp.bfloat16),
            grad_win,
            preferred_element_type=jnp.float32,
        ).astype(jnp.bfloat16)
        grad_probs = jnp.einsum(
            "nqhe,nkhe->nhqk", grad_win, value_part, preferred_element_type=jnp.float32
        )
        row_dot = jnp.sum(probs_full * grad_probs, axis=-1, keepdims=True)
        grad_scores = (probs_full * (grad_probs - row_dot)).astype(jnp.bfloat16)
        bias_sum = jnp.sum(grad_scores.astype(jnp.float32), axis=0)
        if is_joint:
            table_parts.append(
                jnp.zeros((heads_local, joint_bias.shape[1]), jnp.float32)
                .at[:, joint_index]
                .add(bias_sum)
            )
        else:
            table_parts.append(
                jnp.zeros((heads_local, spatial_bias.shape[1]), jnp.float32)
                .at[:, spatial_index]
                .add(bias_sum)
            )
        grad_query = (
            jnp.einsum("nhqk,nkhe->nqhe", grad_scores, key_part, preferred_element_type=jnp.float32)
            * HEAD_DIM ** (-0.5)
        ).astype(jnp.bfloat16)
        grad_key = (
            jnp.einsum(
                "nhqk,nqhe->nkhe", grad_scores, query_part, preferred_element_type=jnp.float32
            )
            * HEAD_DIM ** (-0.5)
        ).astype(jnp.bfloat16)
        stacked = jnp.stack([grad_query, grad_key, grad_value], axis=2).reshape(
            grad_query.shape[0], grad_query.shape[1], 3 * local_width
        )
        grad_projected = from_windows(
            stacked, clip_count, frames, side_cells, window, is_joint
        ).reshape(clip_count, frames, side_cells, side_cells, 3, local_width)
        inputs_one = inputs_again(moved_one)
        qkv_grads.append(
            jnp.einsum(
                "cfyxd,cfyxkh->dkh", inputs_one, grad_projected, preferred_element_type=jnp.float32
            )
        )
        grad_moved = input_sums(
            jnp.einsum(
                "cfyxkh,dkh->cfyxd",
                grad_projected,
                w_qkv[which_block],
                preferred_element_type=jnp.float32,
            )
        )
        grad_shift_one = jnp.sum(grad_moved, axis=(1, 2, 3))
        grad_scale_one = jnp.sum(grad_moved * normed_one, axis=(1, 2, 3))
        grad_state = grad_state + norm_back(
            grad_moved * (1.0 + block_mod[:, 1]), normed_one, inverse_one
        )
        mod_grads.append(
            jnp.stack(
                [
                    grad_shift_one,
                    grad_scale_one,
                    grad_gate_one,
                    grad_shift_two,
                    grad_scale_two,
                    grad_gate_two,
                ],
                axis=1,
            )
        )
    grad_mod = jnp.stack(mod_grads[::-1], axis=0).reshape(2, clip_count, 6 * model_width)
    ordered = (
        grad_mod.reshape(2, clip_count, dp_count, mp_count, col_width)
        .transpose(0, 1, 3, 2, 4)
        .reshape(2, clip_count, 6 * model_width)
    )
    summed_cols = lax.psum_scatter(ordered, "mp", scatter_dimension=2, tiled=True)
    grad_mod_cols = lax.all_to_all(summed_cols, "dp", split_axis=2, concat_axis=1, tiled=True)
    grad_ada_weight = jnp.einsum(
        "cd,bce->bde",
        activity_low.astype(jnp.float32),
        grad_mod_cols,
        precision=lax.Precision.HIGHEST,
    )
    grad_ada_bias = jnp.sum(grad_mod_cols, axis=1)
    grad_mod_block = lax.all_gather(grad_mod_cols, "mp", axis=2, tiled=True)
    activity_part = jnp.einsum(
        "bce,bde->cd", grad_mod_block, ada_cols.astype(jnp.float32), precision=lax.Precision.HIGHEST
    )
    grad_activity = lax.psum(activity_part, "dp")
    grad_condition = jax.vjp(jax.nn.silu, condition)[1](grad_activity)[0]
    grad_time = jnp.dot(
        band_hot.astype(jnp.float32).T, grad_condition, precision=lax.Precision.HIGHEST
    )
    grad_class = jnp.dot(
        class_hot.astype(jnp.float32).T, grad_condition, precision=lax.Precision.HIGHEST
    )
    grad_spatial, grad_joint = lax.psum((table_parts[1], table_parts[0]), "dp")
    grad_qkv, grad_out, grad_up, grad_down = (
        lax.psum_scatter(jnp.stack(qkv_grads[::-1], axis=0), "dp", scatter_dimension=1, tiled=True),
        lax.psum_scatter(jnp.stack(out_grads[::-1], axis=0), "dp", scatter_dimension=2, tiled=True),
        lax.psum_scatter(jnp.stack(up_grads[::-1], axis=0), "dp", scatter_dimension=1, tiled=True),
        lax.psum_scatter(
            jnp.stack(down_grads[::-1], axis=0), "dp", scatter_dimension=2, tiled=True
        ),
    )
    return (
        current,
        grad_state,
        grad_time,
        grad_class,
        grad_ada_weight,
        grad_ada_bias,
        grad_qkv,
        grad_out,
        grad_up,
        grad_down,
        grad_spatial,
        grad_joint,
    )


def solution_any(mesh):
    placed = (
        P("dp", None, "mp", None, None),
        P("dp", None, "mp", None, None),
        P("dp"),
        P(),
        P(),
        P(),
        P(),
        P(None, None, ("dp", "mp")),
        P(None, ("dp", "mp")),
        P(None, "dp", None, "mp"),
        P(None, "mp", "dp"),
        P(None, "dp", "mp"),
        P(None, "mp", "dp"),
        P("mp", None),
        P("mp", None),
    )
    return jax.shard_map(
        local,
        mesh=mesh,
        in_specs=placed,
        out_specs=(
            P("dp", None, "mp", None, None),
            P("dp", None, "mp", None, None),
            P(),
            P(),
            P(None, None, ("dp", "mp")),
            P(None, ("dp", "mp")),
            P(None, "dp", None, "mp"),
            P(None, "mp", "dp"),
            P(None, "dp", "mp"),
            P(None, "mp", "dp"),
            P("mp", None),
            P("mp", None),
        ),
        check_vma=False,
    )


low = jnp.bfloat16
full = jnp.float32
HALF_ROOT = 0.7071067811865476
PHI_AT_ZERO = 0.3989422804014327
MIB = 1024 * 1024


def flip(values, axis):
    return lax.ppermute(values, axis, [(0, 1), (1, 0)])


def z_trade(values, step):
    return lax.ppermute(values, "z", [(place, place ^ step) for place in range(4)])


def swap_only(values):
    return lax.ppermute(values, ("c", "x"), [(1, 2), (2, 1)])


def swap(values):
    return jnp.where(lax.axis_index("c") == lax.axis_index("x"), values, swap_only(values))


def shape_of(dims, dtype=low):
    return jax.ShapeDtypeStruct(tuple(dims), dtype)


def whole(array):
    zeros = (0,) * len(array.shape)
    return pl.BlockSpec(tuple(array.shape), lambda *at: zeros)


def whole_once(array):
    zeros = (0,) * len(array.shape)
    return pl.BlockSpec(
        tuple(array.shape), lambda *at: zeros, pipeline_mode=pl.Buffered(1)
    )


def space_of(dims, dtype):
    dims = [1] * (2 - len(dims)) + list(dims)
    size = jnp.dtype(dtype).itemsize
    rows = 32 // size
    dims[-1] = -(-dims[-1] // 128) * 128
    dims[-2] = -(-dims[-2] // rows) * rows
    return int(np.prod(dims)) * size


def room_for(specs, arrays, scratch):
    total = 0
    for spec, array in zip(specs, arrays):
        if spec.block_shape is not None:
            once = spec.pipeline_mode is not None
            total += space_of(spec.block_shape, array.dtype) * (1 if once else 2)
    return total + sum(space_of(held.shape, held.dtype) for held in scratch)


class Chain:
    def __init__(self, info):
        self.info = info
        self.last = []
        self.pending = []

    def wait(self, *values):
        self.pending += values

    def run(self, name, kernel, args, in_specs, outs, out_specs, grid=(1,), scratch=(), extra=3, waits=()):
        count = len(args)
        unread = self.last + self.pending + list(waits)
        self.pending = []
        held = len(unread)

        limit = room_for(list(in_specs) + list(out_specs), list(args) + list(outs), scratch)

        def body(*refs):
            kernel(*refs[: 1 + count], *refs[1 + count + held :])

        results = pl.pallas_call(
            body,
            grid_spec=pltpu.PrefetchScalarGridSpec(
                num_scalar_prefetch=1,
                grid=grid,
                in_specs=list(in_specs) + [pl.BlockSpec(memory_space=pl.ANY)] * held,
                out_specs=list(out_specs),
                scratch_shapes=list(scratch),
            ),
            out_shape=list(outs),
            compiler_params=pltpu.CompilerParams(vmem_limit_bytes=limit + extra * MIB),
            cost_estimate=pl.CostEstimate(flops=1, bytes_accessed=1, transcendentals=0),
            name=name,
        )(self.info, *args, *unread)
        self.last = [results[0]]
        return results


def pack_arguments(chain, up, down, qkv, out):
    def kernel(info, up_in, down_in, qkv_in, out_in, packed):
        start = 0
        for part in (up_in[0], down_in[0], qkv_in[1], out_in[1], up_in[1], down_in[1]):
            packed[:, start : start + part.shape[1]] = part
            start += part.shape[1]

    args = [up, down, qkv, out]
    result = shape_of((up.shape[1], 5 * PIECE))
    (packed,) = chain.run(
        "pack_arguments", kernel, args, [whole(v) for v in args], [result], [whole(result)]
    )
    return packed


def copy_rows(chain, values):
    def kernel(info, source, result):
        result[...] = source[...]

    spec = pl.BlockSpec((ROW_TILE, values.shape[1]), lambda i, info: (i, 0))
    (result,) = chain.run(
        "copy_rows", kernel, [values], [spec], [shape_of(values.shape)], [spec], grid=(2,)
    )
    return result


def cut_kernel(info, packed, traded, *outs):
    start = 0
    for out in outs:
        width = out.shape[1]
        cols = slice(start, start + width)

        @pl.when(info[4] == 1)
        def _():
            out[...] = packed[:, cols]

        @pl.when(info[4] == 0)
        def _():
            out[...] = traded[:, cols]

        start += width


PIECE = 2048
PIECE_TILE = 512


def tile_spec(count, rows=64):
    return pl.BlockSpec((count, rows, PIECE_TILE), lambda j, info: (0, 0, j))


def flat_spec(rows=64):
    return pl.BlockSpec((rows, PIECE_TILE), lambda j, info: (0, j))


class Gather:
    def __init__(self, chain, shards):
        self.chain = chain
        self.shards = shards
        self.near = {}
        self.sent = {}
        self.got = {}
        self.step_at = 0

    def over_z(self, at):
        self.near[at] = [z_trade(self.shards[at], k) for k in (1, 2, 3)]

    def step(self):
        at = self.step_at
        self.step_at += 1
        own = at < len(self.shards)
        far = at > 0
        args, specs = [], []
        if own:
            args += [self.shards[at]] + self.near[at]
            specs += [flat_spec()] * 4
        start = 0
        if far:
            got_x, got_y = self.got[at - 1]
            start = (got_x.shape[0] - 4) // 2
            args += [got_x, got_y]
            specs += [
                pl.BlockSpec((2, 64, PIECE_TILE), lambda j, info: (start + 1, 0, j)),
                pl.BlockSpec((2, 64, PIECE_TILE), lambda j, info: (start, 0, j)),
            ]

        def kernel(info, *refs):
            to_x, to_y = refs[-2:]
            if own:
                for k in range(4):
                    to_x[(2 if far else 0) + k] = refs[k][...]
                    to_y[(2 if far else 0) + k] = refs[k][...]
            if far:
                from_x, from_y = refs[-4:-2]
                to_x[0:2] = from_y[...]
                to_y[0:2] = from_x[...]

        count = (2 if far else 0) + (4 if own else 0)
        outs = [shape_of((count, 64, PIECE))] * 2
        to_x, to_y = self.chain.run(
            "gather_step",
            kernel,
            args,
            specs,
            outs,
            [tile_spec(count)] * 2,
            grid=(PIECE // PIECE_TILE,),
        )
        self.sent[at] = to_x
        self.got[at] = (flip(to_x, "x"), flip(to_y, "y"))

    def place(self, at, widths):
        def kernel(info, own, from_x, from_y, far_lo, far_hi, *outs):
            k = pl.program_id(0)
            place = info[1] * 2 + info[2]

            def put(rel, block):
                start = 0
                for out in outs:
                    width = out.shape[3]
                    out[0, place ^ rel] = block[0, :, start : start + width]
                    start += width

            put(0, own)
            put(1, from_x)
            put(2, from_y)

            @pl.when(k < 2)
            def _():
                put(3, far_lo)

            @pl.when(k >= 2)
            def _():
                put(3, far_hi)

        got_x, got_y = self.got[at]
        start = got_x.shape[0] - 4
        block = (1, 64, PIECE)
        quad = pl.BlockSpec(block, lambda k, info: (k + start, 0, 0))
        results = self.chain.run(
            "place_weights",
            kernel,
            [self.sent[at], got_x, got_y, *self.got[at + 1]],
            [
                quad,
                quad,
                quad,
                pl.BlockSpec(block, lambda k, info: (jnp.minimum(k, 1), 0, 0)),
                pl.BlockSpec(block, lambda k, info: (jnp.maximum(k - 2, 0), 0, 0)),
            ],
            [shape_of((4, 4, 64, w)) for w in widths],
            [pl.BlockSpec((1, 4, 64, w), lambda k, info: (info[0] ^ k, 0, 0, 0)) for w in widths],
            grid=(4,),
        )
        return [a.reshape(16 * 64, a.shape[3]) for a in results]


GRAD_TILE = 512


def weight_grad_kernel(info, *refs, pairs, tiles):
    lhs = refs[: 4 * pairs]
    rhs = refs[4 * pairs : 5 * pairs]
    near, to_x, to_y, far_lo, far_hi = refs[5 * pairs : 5 * pairs + 5]
    held = refs[5 * pairs + 5]
    across = refs[5 * pairs + 6 :]
    j = pl.program_id(0)
    place = info[1] * 2 + info[2]
    begin = 0
    for at in range(pairs):

        @pl.when(j == begin)
        def _():
            for part in range(4):
                cols = slice(part * ROW_TILE, (part + 1) * ROW_TILE)
                across[at][:, cols] = lhs[4 * at + part][...].T

        @pl.when((j >= begin) & (j < begin + tiles[at]))
        def _():
            tokens = rhs[at][...].reshape(4 * ROW_TILE, GRAD_TILE)
            for rows in range(0, held.shape[0], 256):
                block = jnp.dot(
                    across[at][rows : rows + 256], tokens, preferred_element_type=full
                )
                held[rows : rows + 256] = block.astype(low)

        begin += tiles[at]

    def part(z, rel):
        return held[pl.ds(pl.multiple_of(z * 256 + (place ^ rel) * 64, 64), 64), :]

    for z in range(4):
        near[z] = part(z, 0)
        to_x[z] = part(z, 1)
        to_y[z] = part(z, 2)
        if z < 2:
            far_lo[z] = part(z, 3)
        else:
            far_hi[z - 2] = part(z, 3)


class Scatter:
    def __init__(self, chain):
        self.chain = chain
        self.parts = []
        self.got = None
        self.held = None
        self.done = []
        self.step_at = 0

    def weight_grad(self, *items):
        pairs = len(items)
        widths = tuple(item[2].shape[2] for item in items)
        rows, features = items[0][0][0].shape
        tiles = [w // GRAD_TILE for w in widths]
        quads = shape_of((4, 64, PIECE))
        twos = shape_of((2, 64, PIECE))

        def rhs_spec(at):
            first, last = sum(tiles[:at]), tiles[at] - 1
            return pl.BlockSpec(
                (2, 2 * rows, GRAD_TILE),
                lambda j, info: (0, 0, jnp.clip(j - first, 0, last)),
            )

        quad_spec = pl.BlockSpec((4, 64, GRAD_TILE), lambda j, info: (0, 0, j))
        two_spec = pl.BlockSpec((2, 64, GRAD_TILE), lambda j, info: (0, 0, j))
        lhs = [part for item in items for pair in item[:2] for part in pair]
        self.parts.append(
            self.chain.run(
                "weight_grad",
                lambda *refs: weight_grad_kernel(*refs, pairs=pairs, tiles=tiles),
                lhs + [item[2] for item in items],
                [whole_once(v) for v in lhs] + [rhs_spec(at) for at in range(pairs)],
                [quads, quads, quads, twos, twos],
                [quad_spec] * 3 + [two_spec] * 2,
                grid=(PIECE // GRAD_TILE,),
                scratch=[pltpu.VMEM((features, GRAD_TILE), low)]
                + [pltpu.VMEM((features, 4 * rows), low)] * pairs,
                extra=3,
            )
        )
        if len(self.parts) == 1:
            self.got = (flip(self.parts[0][3], "x"), flip(self.parts[0][4], "y"))

    def step(self, total):
        at = self.step_at
        self.step_at += 1
        far = at + 1 < total
        mid = at < total
        near = 0 <= at - 1 < total
        last = 0 <= at - 2 < total
        args, specs = [], []

        def put(array, spec):
            args.append(array)
            specs.append(spec)
            return len(args) - 1

        names = {}
        if far:
            names["far_lo"] = put(self.parts[at + 1][3], tile_spec(2))
            names["far_hi"] = put(self.parts[at + 1][4], tile_spec(2))
        if mid:
            names["to_x"] = put(self.parts[at][1], tile_spec(4))
            names["to_y"] = put(self.parts[at][2], tile_spec(4))
        if near:
            names["near"] = put(self.parts[at - 1][0], tile_spec(4))
        if mid or near:
            count = self.got[0].shape[0]
            names["got_x"] = put(self.got[0], tile_spec(count))
            names["got_y"] = put(self.got[1], tile_spec(count))
        if last:
            for k in range(4):
                names["held%d" % k] = put(self.held[k], flat_spec())
        outs, out_specs = [], []
        sent = (2 if far else 0) + (4 if mid else 0)
        if mid:
            outs += [shape_of((sent, 64, PIECE))] * 2
            out_specs += [tile_spec(sent)] * 2
        if near:
            outs += [shape_of((64, PIECE), full)] + [shape_of((64, PIECE))] * 3
            out_specs += [flat_spec()] * 4
        if last:
            outs.append(shape_of((64, PIECE)))
            out_specs.append(flat_spec())
        number = len(args)

        def kernel(info, *refs):
            out = list(refs[number:])
            get = {name: refs[spot] for name, spot in names.items()}
            if mid:
                out_x, out_y = out[:2]
                del out[:2]
                start = 0
                if far:
                    out_x[0:2] = get["far_lo"][...]
                    out_y[0:2] = get["far_hi"][...]
                    start = 2
                for k in range(4):
                    part_x = get["to_x"][k]
                    part_y = get["to_y"][k]
                    if k < 2:
                        part_y = (part_y.astype(full) + get["got_x"][k].astype(full)).astype(low)
                    else:
                        part_x = (
                            part_x.astype(full) + get["got_y"][k - 2].astype(full)
                        ).astype(low)
                    out_x[start + k] = part_x
                    out_y[start + k] = part_y
            if near:
                start = get["got_x"].shape[0] - 4
                for k in range(4):
                    spot = info[0] ^ k
                    value = get["near"][spot].astype(full)
                    value = value + get["got_x"][start + spot].astype(full)
                    value = value + get["got_y"][start + spot].astype(full)
                    out[k][...] = value.astype(out[k].dtype)
                del out[:4]
            if last:
                value = get["held0"][...]
                for k in (1, 2, 3):
                    value = value + get["held%d" % k][...].astype(full)
                out[0][...] = value.astype(low)

        results = list(
            self.chain.run(
                "scatter_step", kernel, args, specs, outs, out_specs, grid=(PIECE // PIECE_TILE,)
            )
        )
        if mid:
            self.got = (flip(results[0], "x"), flip(results[1], "y"))
            del results[:2]
        if near:
            self.held = [results[0]] + [z_trade(results[k], k) for k in (1, 2, 3)]
            del results[:4]
        if last:
            self.done.append(results[0])


def collect_sums(chain, sums):
    spots = [(4, 0), (4, 1), (3, 2), (3, 0), (3, 1), (2, 2), (2, 0), (2, 1), (1, 2), (1, 0), (1, 1), (0, 0)]

    def kernel(info, *refs):
        for row, (at, spot) in enumerate(spots):
            refs[-1][row : row + 1] = refs[at][spot : spot + 1]

    out = shape_of((len(spots), sums[0].shape[1]), full)
    (result,) = chain.run(
        "collect_sums", kernel, list(sums), [whole(v) for v in sums], [out], [whole(out)]
    )
    return result


def add_all(chain, *values):
    def kernel(info, *refs):
        total = refs[0][...]
        for other in refs[1:-1]:
            total = total + other[...]
        refs[-1][...] = total

    out = shape_of(values[0].shape, full)
    (result,) = chain.run(
        "add_all", kernel, list(values), [whole(a) for a in values], [out], [whole(out)]
    )
    return result


def join_pieces(chain, pieces, *copied):
    count = len(pieces)

    def kernel(info, *refs):
        out = refs[count + len(copied)]
        for at in range(count):
            out[:, at * PIECE : (at + 1) * PIECE] = refs[at][...]
        for at in range(len(copied)):
            refs[count + len(copied) + 1 + at][...] = refs[count + at][...]

    args = list(pieces) + list(copied)
    outs = [shape_of((64, PIECE * count))] + [shape_of(v.shape) for v in copied]
    return chain.run(
        "join_pieces", kernel, args, [whole(v) for v in args], outs, [whole(v) for v in outs]
    )


def gelu_and_slope(values):
    bell = jnp.exp(-0.5 * values * values)
    t = 1.0 / (1.0 + (0.3275911 * HALF_ROOT) * jnp.abs(values))
    poly = t * (
        0.254829592
        + t * (-0.284496736 + t * (1.421413741 + t * (-1.453152027 + t * 1.061405429)))
    )
    tail = 0.5 * poly * bell
    phi = jnp.where(values >= 0, 1.0 - tail, tail)
    return values * phi, phi + (PHI_AT_ZERO * values) * bell


ROW_TILE = 320


def flip_rows(pair):
    return tuple(flip(part, "c") for part in pair)


def both_kernel(info, *refs, kind):
    weight = refs[4][...]
    for part in range(4):
        half = part // 2
        rows = slice(part % 2 * ROW_TILE, (part % 2 + 1) * ROW_TILE)
        product = jnp.dot(refs[part][...], weight, preferred_element_type=full)
        if kind == "gelu":
            act, slope = gelu_and_slope(product)
            refs[5][half, rows] = act.astype(low)
            refs[6][half, rows] = slope.astype(low)
        elif kind == "slope":
            refs[6][half, rows] = (product * refs[5][half, rows].astype(full)).astype(low)
        else:
            refs[5][half, rows] = product.astype(low)


def both_times(chain, kind, own, other, weight, slope=None, waits=()):
    depth = weight.shape[0]
    rows = 2 * ROW_TILE
    width = weight.shape[1]
    tile = 256 if kind == "gelu" else 512
    out_spec = pl.BlockSpec((2, rows, tile), lambda j, info: (0, 0, j))
    extra = [] if slope is None else [slope]
    count = 2 if kind == "gelu" else 1
    return chain.run(
        "both_" + kind,
        lambda *refs: both_kernel(*refs, kind=kind),
        [*own, *other, weight] + extra,
        [whole_once(part) for part in (*own, *other)]
        + [pl.BlockSpec((depth, tile), lambda j, info: (0, j))]
        + [out_spec] * len(extra),
        [shape_of((2, rows, width))] * count,
        [out_spec] * count,
        grid=(width // tile,),
        waits=waits,
    )


def times_back(values, weight):
    return lax.dot_general(
        values, weight, (((1,), (1,)), ((), ())), preferred_element_type=full
    ).astype(low)


def other_rows(chain, values, weight):
    rows, depth = values.shape[1:]
    width = weight.shape[0]
    tile = 256

    def kernel(info, rows_in, weight_in, first, second):
        result = times_back(rows_in[0], weight_in[...])
        first[...] = result[:ROW_TILE]
        second[...] = result[ROW_TILE:]

    half = pl.BlockSpec((ROW_TILE, tile), lambda j, info: (0, j))
    results = chain.run(
        "other_rows",
        kernel,
        [values, weight],
        [
            pl.BlockSpec(
                (1, rows, depth), lambda j, info: (1, 0, 0), pipeline_mode=pl.Buffered(1)
            ),
            pl.BlockSpec((tile, depth), lambda j, info: (j, 0)),
        ],
        [shape_of((ROW_TILE, width))] * 2,
        [half] * 2,
        grid=(width // tile,),
    )
    return flip_rows(results)


def put_half(pair, values):
    @pl.when(pl.program_id(0) == 0)
    def _():
        pair[0][...] = values

    @pl.when(pl.program_id(0) == 1)
    def _():
        pair[1][...] = values


def get_half(pair):
    return jnp.where(pl.program_id(0) == 0, pair[0][...].astype(full), pair[1][...].astype(full))


def shown_rows(info):
    first = pl.program_id(0) * ROW_TILE
    row = first + lax.broadcasted_iota(jnp.int32, (ROW_TILE, 1), 0)
    return (row < info[3] * 128).astype(full)


def norm_and_move(values, shift, scale):
    center = values - jnp.mean(values, axis=-1, keepdims=True)
    spread = jnp.mean(center * center, axis=-1, keepdims=True)
    inverse = lax.rsqrt(spread + epsilon)
    normed = center * inverse
    return normed.astype(low), inverse, (normed * (1.0 + scale) + shift).astype(low)


def row_specs(model_width):
    tall = pl.BlockSpec((ROW_TILE, model_width), lambda i, info: (i, 0))
    thin = pl.BlockSpec((ROW_TILE, 1), lambda i, info: (i, 0))
    return tall, thin


def first_norm(chain, current, traded, rows_of):
    rows, model_width = current.shape
    tall, thin = row_specs(model_width)

    def kernel(info, ours, theirs, given, kept, normed, inverse, *moved):
        values = jnp.where(info[4] == 1, ours[...].astype(full), theirs[...].astype(full))
        kept[...] = values.astype(low)
        normed[...], inverse[...], result = norm_and_move(values, given[0:1], given[1:2])
        put_half(moved, result)

    half = shape_of((ROW_TILE, model_width))
    kept, normed, inverse, *moved = chain.run(
        "first_norm",
        kernel,
        [current, traded, rows_of],
        [tall, tall, whole_once(rows_of)],
        [shape_of(current.shape)] * 2 + [shape_of((rows, 1), full), half, half],
        [tall, tall, thin, whole(half), whole(half)],
        grid=(rows // ROW_TILE,),
    )
    return kept, normed, inverse, moved


def forward_step(chain, values, weight, away, current, rows_of, last, waits=()):
    rows, model_width = current.shape
    depth = values.shape[2]
    tall, thin = row_specs(model_width)

    def kernel(info, own, weight_in, first, second, current_in, given, after, branch_out, *rest):
        branch = times_back(own[0], weight_in[...]).astype(full) + get_half((first, second))
        total = current_in[...].astype(full) + shown_rows(info) * given[0:1] * branch
        after[...] = total.astype(after.dtype)
        branch_out[...] = branch.astype(low)
        if not last:
            normed, inverse, *moved = rest
            normed[...], inverse[...], result = norm_and_move(total, given[1:2], given[2:3])
            put_half(moved, result)

    outs = [shape_of(current.shape, low if last else full), shape_of(current.shape)]
    specs = [tall, tall]
    if not last:
        half = shape_of((ROW_TILE, model_width))
        outs += [shape_of(current.shape), shape_of((rows, 1), full), half, half]
        specs += [tall, thin, whole(half), whole(half)]
    results = chain.run(
        "forward_step",
        kernel,
        [values, weight, *away, current, rows_of],
        [
            pl.BlockSpec((1, ROW_TILE, depth), lambda i, info: (0, i, 0)),
            whole_once(weight),
            whole_once(away[0]),
            whole_once(away[1]),
            tall,
            whole_once(rows_of),
        ],
        outs,
        specs,
        grid=(rows // ROW_TILE,),
        waits=waits,
    )
    return results if last else (*results[:4], results[4:])


def add_rows(out, at, values):
    total = jnp.sum(values, axis=0, keepdims=True)

    @pl.when(pl.program_id(0) == 0)
    def _():
        out[at : at + 1] = total

    @pl.when(pl.program_id(0) > 0)
    def _():
        out[at : at + 1] += total


def first_back(chain, state, branch, gate):
    rows, model_width = state.shape
    tall, _ = row_specs(model_width)

    def kernel(info, state_in, branch_in, gate_in, first, second, sums):
        values = state_in[...].astype(full) * shown_rows(info)
        put_half((first, second), (values * gate_in[...]).astype(low))
        add_rows(sums, 0, values * branch_in[...].astype(full))

    sums = shape_of((8, model_width), full)
    half = shape_of((ROW_TILE, model_width))
    first, second, sums = chain.run(
        "first_back",
        kernel,
        [state, branch, gate],
        [tall, tall, whole_once(gate)],
        [half, half, sums],
        [whole(half), whole(half), whole(sums)],
        grid=(rows // ROW_TILE,),
    )
    return (first, second), sums


def backward_step(chain, values, weight, away, normed, inverse, state, rows_of, branch):
    rows, model_width = state.shape
    depth = values.shape[2]
    tall, thin = row_specs(model_width)
    last = branch is None

    def kernel(
        info, own, weight_in, first, second, normed_in, inverse_in, state_in, given, *rest
    ):
        grad = times_back(own[0], weight_in[...]).astype(full) + get_half((first, second))
        normal = normed_in[...].astype(full)
        moved = grad * (1.0 + given[0:1])
        first_mean = jnp.mean(moved, axis=-1, keepdims=True)
        second_mean = jnp.mean(moved * normal, axis=-1, keepdims=True)
        total = state_in[...].astype(full) + inverse_in[...] * (
            moved - first_mean - normal * second_mean
        )
        if last:
            state_out, sums = rest
        else:
            branch_in, state_out, sums, *sent = rest
        state_out[...] = total.astype(state_out.dtype)
        add_rows(sums, 0, grad)
        add_rows(sums, 1, grad * normal)
        if not last:
            shown = total * shown_rows(info)
            put_half(sent, (shown * given[1:2]).astype(low))
            add_rows(sums, 2, shown * branch_in[...].astype(full))

    sums = shape_of((8, model_width), full)
    outs = [shape_of(state.shape, low if last else full), sums]
    specs = [tall, whole(sums)]
    if not last:
        half = shape_of((ROW_TILE, model_width))
        outs += [half, half]
        specs += [whole(half)] * 2
    extra = [] if last else [branch]
    results = chain.run(
        "backward_step",
        kernel,
        [values, weight, *away, normed, inverse, state, rows_of] + extra,
        [
            pl.BlockSpec((1, ROW_TILE, depth), lambda i, info: (0, i, 0)),
            whole_once(weight),
            whole_once(away[0]),
            whole_once(away[1]),
            tall,
            thin,
            tall,
            whole_once(rows_of),
        ]
        + [tall] * len(extra),
        outs,
        specs,
        grid=(rows // ROW_TILE,),
    )
    return results if last else (*results[:2], results[2:])


def attend_kernel(info, blocks, joined, mixed, probs, bias, *, heads, cells, masked, sides):
    width = heads * HEAD_DIM

    @pl.when((pl.program_id(0) == 0) & (pl.program_id(1) == 0))
    def _():
        for h in range(heads):
            for place, spots in enumerate(sides):
                block = blocks[h, place]
                for row, col in spots:
                    bias[h, row * 64 : row * 64 + 64, col * 64 : col * 64 + 64] = block

    values = joined[...].reshape(cells, 3 * width)
    lead = mixed.shape
    if masked:
        column = lax.broadcasted_iota(jnp.int32, (1, cells), 1)
        shown = column < info[3] * (WIN_T * WIN_T)
    outs = []
    for h in range(heads):
        cols = slice(h * HEAD_DIM, (h + 1) * HEAD_DIM)
        query = values[:, cols]
        key = values[:, width + h * HEAD_DIM : width + (h + 1) * HEAD_DIM]
        value = values[:, 2 * width + h * HEAD_DIM : 2 * width + (h + 1) * HEAD_DIM]
        scores = lax.dot_general(
            query, key, (((1,), (1,)), ((), ())), preferred_element_type=full
        ) * HEAD_DIM ** (-0.5) + bias[h].astype(full)
        if masked:
            scores = jnp.where(shown, scores, masked_score)
        weights = jnp.exp(scores - jnp.max(scores, axis=-1, keepdims=True))
        share = (weights * (1.0 / jnp.sum(weights, axis=-1, keepdims=True))).astype(low)
        probs[0, h] = share
        outs.append(jnp.dot(share, value, preferred_element_type=full).astype(low))
    mixed[...] = jnp.concatenate(outs, axis=1).reshape(lead)


def attend_back_kernel(info, joined, grad, probs, back, bias_out, total, *, heads, cells, sides):
    step = pl.program_id(0) * pl.num_programs(1) + pl.program_id(1)
    width = heads * HEAD_DIM
    values = joined[...].reshape(cells, 3 * width)
    grads = grad[...].reshape(cells, width)
    grads_t = grads.astype(full).T.astype(low)
    queries_t = values[:, :width].astype(full).T.astype(low)
    queries, keys_t, values_t = [], [], []

    @pl.when(step == 0)
    def _():
        total[...] = jnp.zeros(total.shape, full)

    for h in range(heads):
        cols = slice(h * HEAD_DIM, (h + 1) * HEAD_DIM)
        key = values[:, width + h * HEAD_DIM : width + (h + 1) * HEAD_DIM]
        value = values[:, 2 * width + h * HEAD_DIM : 2 * width + (h + 1) * HEAD_DIM]
        share = probs[0, h]
        values_t.append(jnp.dot(grads_t[cols], share, preferred_element_type=full).astype(low))
        grad_share = lax.dot_general(
            grads[:, cols], value, (((1,), (1,)), ((), ())), preferred_element_type=full
        )
        share_full = share.astype(full)
        product = share_full * grad_share
        row_dot = jnp.sum(product, axis=-1, keepdims=True)
        grad_scores = (product - share_full * row_dot).astype(low)
        total[h] += grad_scores.astype(full)
        queries.append(
            (jnp.dot(grad_scores, key, preferred_element_type=full) * HEAD_DIM ** (-0.5)).astype(
                low
            )
        )
        keys_t.append(
            (
                jnp.dot(queries_t[cols], grad_scores, preferred_element_type=full)
                * HEAD_DIM ** (-0.5)
            ).astype(low)
        )
    key_grads = jnp.concatenate(keys_t, axis=0).astype(full).T.astype(low)
    value_grads = jnp.concatenate(values_t, axis=0).astype(full).T.astype(low)
    back[...] = jnp.concatenate(queries + [key_grads, value_grads], axis=1).reshape(back.shape)

    @pl.when(step == pl.num_programs(0) * pl.num_programs(1) - 1)
    def _():
        for h in range(heads):
            for place, spots in enumerate(sides):
                part = None
                for row, col in spots:
                    block = total[h, row * 64 : row * 64 + 64, :][:, col * 64 : col * 64 + 64]
                    part = block if part is None else part + block
                bias_out[h, place] = part


def spatial_sides():
    sides = [[] for _ in range(9)]
    for row in range(4):
        for col in range(4):
            place = (row // 2 - col // 2 + 1) * 3 + (row % 2 - col % 2 + 1)
            sides[place].append((row, col))
    return sides


def joint_sides():
    sides = [[] for _ in range(2 * FRAMES - 1)]
    for row in range(FRAMES):
        for col in range(FRAMES):
            sides[row - col + FRAMES - 1].append((row, col))
    return sides


def window_specs(is_joint, frames, width):
    if is_joint:
        shape, at = (1, frames, 1, 64, width), lambda i, j, info: (i, 0, j, 0, 0)
    else:
        shape, at = (2, 1, 2, 64, width), lambda i, j, info: (0, j, 0, 0, 0)
    return pl.BlockSpec(shape, at)


def attend(chain, blocks, joined, is_joint):
    frames = joined.shape[1]
    heads = blocks.shape[0]
    width = heads * HEAD_DIM
    grid = (2, 2) if is_joint else (1, frames)
    cells = 64 * frames if is_joint else 256
    number = grid[0] * grid[1]
    sides = joint_sides() if is_joint else spatial_sides()
    fetch = lambda i, j, info: (i * grid[1] + j, 0, 0, 0)
    return chain.run(
        "attend_joint" if is_joint else "attend_spatial",
        lambda *refs: attend_kernel(
            *refs, heads=heads, cells=cells, masked=is_joint, sides=sides
        ),
        [blocks, joined],
        [whole_once(blocks), window_specs(is_joint, frames, 3 * width)],
        [shape_of(joined.shape[:4] + (width,)), shape_of((number, heads, cells, cells))],
        [window_specs(is_joint, frames, width), pl.BlockSpec((1, heads, cells, cells), fetch)],
        grid=grid,
        scratch=[pltpu.VMEM((heads, cells, cells), low)],
    )


def attend_back(chain, joined, grad, probs, is_joint):
    frames = joined.shape[1]
    number, heads, cells, _ = probs.shape
    width = heads * HEAD_DIM
    grid = (2, 2) if is_joint else (1, frames)
    sides = joint_sides() if is_joint else spatial_sides()
    fetch = lambda i, j, info: (i * grid[1] + j, 0, 0, 0)
    sums = shape_of((heads, 9, 64, 64), full)
    return chain.run(
        "attend_back_joint" if is_joint else "attend_back_spatial",
        lambda *refs: attend_back_kernel(*refs, heads=heads, cells=cells, sides=sides),
        [joined, grad, probs],
        [
            window_specs(is_joint, frames, 3 * width),
            window_specs(is_joint, frames, width),
            pl.BlockSpec((1, heads, cells, cells), fetch),
        ],
        [shape_of(joined.shape), sums],
        [window_specs(is_joint, frames, 3 * width), whole(sums)],
        grid=grid,
        scratch=[pltpu.VMEM((heads, cells, cells), full)],
        extra=5,
    )


def offset_hot():
    places = np.arange(WIN_T * WIN_T)
    rows = places[:, None] // WIN_T - places[None, :] // WIN_T + WIN_T - 1
    cols = places[:, None] % WIN_T - places[None, :] % WIN_T + WIN_T - 1
    spots = (rows * (2 * WIN_T - 1) + cols).reshape(-1).astype(np.int32)
    return jnp.arange((2 * WIN_T - 1) ** 2, dtype=jnp.int32)[:, None] == jnp.asarray(spots)[None]


def fast_local(
    latents,
    cotangent,
    frame_counts,
    band_ids,
    class_ids,
    time_table,
    class_table,
    ada_weight,
    ada_bias,
    qkv_weight,
    out_weight,
    up_weight,
    down_weight,
    spatial_bias,
    joint_bias,
):
    frames = latents.shape[1]
    model_width = latents.shape[4]
    heads = spatial_bias.shape[0]
    width = heads * HEAD_DIM
    hidden = up_weight.shape[2]
    col_width = ada_weight.shape[2]
    rows = frames * 128
    z, y, c, x = (lax.axis_index(name) for name in ("z", "y", "c", "x"))
    counts = frame_counts.astype(full)
    count = jnp.where(c == x, counts, flip(counts, "c")).astype(jnp.int32)
    same = (c == x).astype(jnp.int32)
    chain = Chain(
        jnp.concatenate([jnp.stack([z, y, x]).astype(jnp.int32), count, same.reshape(1)])
    )

    def rearranged(values):
        shaped = values.reshape(frames, 8, 2, 8, model_width).transpose(0, 2, 1, 3, 4)
        return shaped.reshape(rows, model_width)

    qkv_rows = qkv_weight.reshape(2, -1, 3 * width)
    out_rows = out_weight.transpose(0, 2, 1)
    down_rows = down_weight.transpose(0, 2, 1)
    first_shard = swap(jnp.concatenate([qkv_rows[0], out_rows[0]], axis=1))
    band_hot = (band_ids[:, None] == jnp.arange(BANDS)[None, :]).astype(low)
    class_hot = (class_ids[:, None] == jnp.arange(CLASSES)[None, :]).astype(low)
    condition = jnp.dot(band_hot, time_table, preferred_element_type=full) + jnp.dot(
        class_hot, class_table, preferred_element_type=full
    )
    activity = jax.nn.silu(condition).astype(low)
    everyone = ("z", "y", "c", "x")
    mod_part = jnp.einsum(
        "cd,bde->cbe", activity, ada_weight, preferred_element_type=full
    ) + ada_bias[None].astype(full)
    mod_part = jnp.broadcast_to(
        mod_part.reshape(8, 1, 2, 2, col_width), (8, 2, 2, 2, col_width)
    ).reshape(32, 2, col_width)
    own_mod = lax.all_to_all(mod_part, everyone, split_axis=0, concat_axis=0, tiled=True)
    own_mod = own_mod.transpose(1, 0, 2).reshape(2, 6, model_width)
    rows_of = lambda *items: jnp.stack([own_mod[k, at] for k, at in items])

    hot = offset_hot()
    wide = 2 * WIN_T - 1
    square = spatial_bias.reshape(heads, 2 * WIN_S - 1, 2 * WIN_S - 1)
    spatial_parts = jnp.stack(
        [
            square[:, 8 * a : 8 * a + wide, 8 * b : 8 * b + wide].reshape(heads, -1)
            for a in range(3)
            for b in range(3)
        ],
        axis=1,
    )
    parts = swap(jnp.concatenate([spatial_parts, joint_bias.reshape(heads, 9, -1)]))
    blocks = jnp.dot(
        parts.reshape(heads * 18, wide * wide), hot.astype(low), preferred_element_type=full
    ).astype(low)
    blocks = blocks.reshape(2, heads, 9, 64, 64)
    near = blocks[0].reshape(heads, 3, 3, 64, 64)
    near = jnp.where(c == 0, near, near[:, ::-1])
    bias_blocks = [near.reshape(heads, 9, 64, 64), blocks[1]]

    windowed = lambda values: values.reshape(2, frames, 2, 64, values.shape[-1])

    chain.wait(own_mod, parts)
    packed = pack_arguments(chain, up_weight, down_rows, qkv_rows, out_rows)
    traded = swap_only(packed)
    gather = Gather(chain, [first_shard] + [None] * 5)
    gather.over_z(0)
    gather.step()
    cuts = [shape_of((64, PIECE))] * 5
    gather.shards[1:] = chain.run(
        "cut_shards",
        cut_kernel,
        [packed, traded],
        [whole(packed)] * 2,
        cuts,
        [whole(a) for a in cuts],
    )
    gather.over_z(1)
    latent_rows = copy_rows(chain, rearranged(latents))
    traded_rows = swap_only(latent_rows)
    gather.step()
    gather.over_z(2)
    chain.wait(*bias_blocks)
    latent_rows, normed_0, inverse_0, moved_0 = first_norm(
        chain, latent_rows, traded_rows, rows_of((0, 0), (0, 1))
    )
    other_0 = flip_rows(moved_0)
    gather.step()
    gather.over_z(3)
    qkv_0, out_0 = gather.place(0, [3 * width, width])
    (joined_0,) = both_times(chain, "plain", moved_0, other_0, qkv_0)
    joined_0 = windowed(joined_0)
    mixed_0, probs_0 = attend(chain, bias_blocks[0], joined_0, False)
    mixed_0 = mixed_0.reshape(2, rows, width)
    away = other_rows(chain, mixed_0, out_0)
    gather.step()
    gather.over_z(4)
    (up_0,) = gather.place(1, [hidden])
    after_0, branch_one_0, normed_1, inverse_1, moved_1 = forward_step(
        chain, mixed_0, out_0, away, latent_rows, rows_of((0, 2), (0, 3), (0, 4)), False
    )
    other_1 = flip_rows(moved_1)
    act_0, slope_0 = both_times(chain, "gelu", moved_1, other_1, up_0)
    gather.step()
    gather.over_z(5)
    (down_0,) = gather.place(2, [hidden])
    away = other_rows(chain, act_0, down_0)
    current_1, branch_two_0, normed_2, inverse_2, moved_2 = forward_step(
        chain, act_0, down_0, away, after_0, rows_of((0, 5), (1, 0), (1, 1)), False
    )
    other_2 = flip_rows(moved_2)

    gather.step()
    qkv_1, out_1 = gather.place(3, [3 * width, width])
    (joined_1,) = both_times(chain, "plain", moved_2, other_2, qkv_1)
    joined_1 = windowed(joined_1)
    mixed_1, probs_1 = attend(chain, bias_blocks[1], joined_1, True)
    mixed_1 = mixed_1.reshape(2, rows, width)
    away = other_rows(chain, mixed_1, out_1)
    gather.step()
    (up_1,) = gather.place(4, [hidden])
    after_1, branch_one_1, normed_3, inverse_3, moved_3 = forward_step(
        chain, mixed_1, out_1, away, current_1, rows_of((1, 2), (1, 3), (1, 4)), False
    )
    other_3 = flip_rows(moved_3)
    act_1, slope_1 = both_times(chain, "gelu", moved_3, other_3, up_1)
    (down_1,) = gather.place(5, [hidden])
    traded_cotangent = swap(copy_rows(chain, rearranged(cotangent)))
    away = other_rows(chain, act_1, down_1)
    final, branch_two_1 = forward_step(
        chain, act_1, down_1, away, after_1, rows_of((1, 5)), True
    )

    def restored(sent):
        shaped = sent.reshape(frames, 2, 8, 8, model_width).transpose(0, 2, 1, 3, 4)
        return shaped.astype(full).reshape(1, frames, 8, 16, model_width)

    traded_final = swap(final)

    exact = lax.Precision.HIGHEST
    hot_wide = jnp.pad(hot.astype(full), ((0, 256 - wide * wide), (0, 0)))
    table_sums = lambda sums: jnp.dot(
        sums.reshape(heads * 9, 64 * 64), hot_wide.T, precision=exact
    )

    state = traded_cotangent
    own_g, sums_a = first_back(chain, state, branch_two_1, rows_of((1, 5)))
    other_g = flip_rows(own_g)
    scatter = Scatter(chain)
    (hidden_g,) = both_times(chain, "slope", own_g, other_g, down_1, slope_1)
    away = other_rows(chain, hidden_g, up_1)
    scatter.weight_grad((own_g, other_g, act_1))
    state, sums_b, own_g = backward_step(
        chain, hidden_g, up_1, away, normed_3, inverse_3, state, rows_of((1, 4), (1, 2)), branch_one_1
    )
    other_g = flip_rows(own_g)
    scatter.weight_grad((moved_3, other_3, hidden_g))
    chain.wait(traded_final)
    scatter.step(6)
    (mixed_g,) = both_times(chain, "plain", own_g, other_g, out_1)
    back, joint_sums = attend_back(chain, joined_1, windowed(mixed_g), probs_1, True)
    joint_tables = table_sums(joint_sums)
    back = back.reshape(2, rows, 3 * width)
    away = other_rows(chain, back, qkv_1)
    scatter.weight_grad((moved_2, other_2, back), (own_g, other_g, mixed_1))
    scatter.step(6)
    state, sums_c, own_g = backward_step(
        chain, back, qkv_1, away, normed_2, inverse_2, state, rows_of((1, 1), (0, 5)), branch_two_0
    )
    other_g = flip_rows(own_g)

    (hidden_g,) = both_times(chain, "slope", own_g, other_g, down_0, slope_0)
    away = other_rows(chain, hidden_g, up_0)
    scatter.weight_grad((own_g, other_g, act_0))
    scatter.step(6)
    state, sums_d, own_g = backward_step(
        chain, hidden_g, up_0, away, normed_1, inverse_1, state, rows_of((0, 4), (0, 2)), branch_one_0
    )
    other_g = flip_rows(own_g)
    scatter.weight_grad((moved_1, other_1, hidden_g))
    (mixed_g,) = both_times(chain, "plain", own_g, other_g, out_0)
    scatter.step(6)
    back, spatial_sums = attend_back(chain, joined_0, windowed(mixed_g), probs_0, False)
    back = back.reshape(2, rows, 3 * width)
    away = other_rows(chain, back, qkv_0)
    scatter.weight_grad((moved_0, other_0, back), (own_g, other_g, mixed_0))
    scatter.step(6)
    state, sums_e = backward_step(
        chain, back, qkv_0, away, normed_0, inverse_0, state, rows_of((0, 1)), None
    )
    output = restored(traded_final)

    chain.wait(*scatter.held[1:])
    grad_mod = collect_sums(chain, [sums_a, sums_b, sums_c, sums_d, sums_e])
    ordered = grad_mod.reshape(2, 32, col_width).transpose(1, 0, 2)
    cols = lax.all_to_all(ordered, everyone, split_axis=0, concat_axis=0, tiled=True)
    cols = cols.reshape(8, 2, 2, 2, col_width)
    cols = (cols[:, 0] + cols[:, 1]).reshape(16, 2, col_width)
    grad_ada_weight = jnp.einsum("cd,cbe->bde", activity.astype(full), cols, precision=exact)
    grad_ada_bias = jnp.sum(cols, axis=0)
    grad_activity = jnp.einsum("cbe,bde->cd", cols, ada_weight.astype(full), precision=exact)

    near = spatial_sums.reshape(heads, 3, 3, 64, 64)
    near = jnp.where(c == 0, near, near[:, ::-1]).reshape(heads, 9, 64, 64)
    tables = jnp.concatenate([table_sums(near), joint_tables])

    shared = jnp.concatenate([grad_activity.reshape(-1, 256), tables])
    chain.wait(shared)
    scatter.step(6)
    scatter.step(6)
    shared = add_all(chain, shared)
    sent = flip(shared, "y")
    traded_state = swap(copy_rows(chain, state))
    (early,) = join_pieces(chain, scatter.done)
    early = swap(early)
    shared = add_all(chain, shared, sent)
    sent = [z_trade(shared, k) for k in (1, 2, 3)]
    chain.wait(traded_state)
    scatter.step(6)
    late = swap(scatter.done[5]).astype(full)
    shared = add_all(chain, shared, *sent)
    sent = flip(shared, "x")
    chain.wait(early)
    shared = add_all(chain, shared, sent)
    tables = shared[-heads * 18 :]
    across = flip(shared, "c")
    grad_activity = (shared + across)[: -heads * 18].reshape(16, model_width)
    tables = jnp.where(c == x, tables, across[-heads * 18 :])[:, : wide * wide]
    grad_latents = restored(traded_state)
    done = early.astype(full)
    piece = lambda at: done[:, at * PIECE : (at + 1) * PIECE]
    grad_down = jnp.stack([piece(3).T, piece(0).T])
    grad_up = jnp.stack([piece(4), piece(1)])
    grad_qkv = jnp.stack([late[:, : 3 * width], piece(2)[:, : 3 * width]])
    grad_out = jnp.stack([late[:, 3 * width :].T, piece(2)[:, 3 * width :].T])

    tables = tables.reshape(2, heads, 9, wide, wide)
    grad_joint = tables[1].reshape(heads, 9 * wide * wide)
    near = tables[0].reshape(heads, 3, 3, wide, wide)
    long = 2 * WIN_S - 1
    grad_spatial = 0.0
    for a in range(3):
        for b in range(3):
            grad_spatial = grad_spatial + jnp.pad(
                near[:, a, b],
                ((0, 0), (8 * a, long - wide - 8 * a), (8 * b, long - wide - 8 * b)),
            )
    grad_spatial = grad_spatial.reshape(heads, long * long)
    grad_condition = jax.vjp(jax.nn.silu, condition)[1](grad_activity)[0]
    grad_time = jnp.dot(band_hot.astype(full).T, grad_condition, precision=exact)
    grad_class = jnp.dot(class_hot.astype(full).T, grad_condition, precision=exact)

    return (
        output,
        grad_latents,
        grad_time,
        grad_class,
        grad_ada_weight,
        grad_ada_bias,
        grad_qkv.reshape(2, -1, 3, width),
        grad_out,
        grad_up,
        grad_down,
        grad_spatial,
        grad_joint,
    )


def solution(mesh):
    if mesh.shape["dp"] != 16 or mesh.shape["mp"] != 2:
        return solution_any(mesh)
    fine = Mesh(mesh.devices.reshape(4, 2, 2, 2), ("z", "y", "c", "x"))
    dp, mp = ("z", "y", "c"), "x"
    both = dp + (mp,)
    tokens = P(dp, None, mp, None, None)
    weight_specs = (
        P(None, None, both),
        P(None, both),
        P(None, dp, None, mp),
        P(None, mp, dp),
        P(None, dp, mp),
        P(None, mp, dp),
        P(mp, None),
        P(mp, None),
    )
    return jax.shard_map(
        fast_local,
        mesh=fine,
        in_specs=(tokens, tokens, P(dp), P(), P(), P(), P()) + weight_specs,
        out_specs=(tokens, tokens, P(), P()) + weight_specs,
        check_vma=False,
    )
```

```python
import jax
import jax.numpy as jnp
import numpy as np
from jax import lax
from jax.experimental import pallas as pl
from jax.experimental.pallas import tpu as pltpu
from jax.sharding import Mesh
from jax.sharding import PartitionSpec as P

HEAD_DIM = 64
CLASSES = 101
BANDS = 32
FRAMES = 5
WIN_S = 16
WIN_T = 8


epsilon = 1e-06
masked_score = -1e30


def spatial_table():
    places = np.arange(WIN_S * WIN_S)
    row_at = places // WIN_S
    col_at = places % WIN_S
    row_rel = row_at[:, None] - row_at[None, :] + WIN_S - 1
    col_rel = col_at[:, None] - col_at[None, :] + WIN_S - 1
    return (row_rel * (2 * WIN_S - 1) + col_rel).astype(np.int32)


def joint_table():
    places = np.arange(FRAMES * WIN_T * WIN_T)
    time_at = places // (WIN_T * WIN_T)
    row_at = places // WIN_T % WIN_T
    col_at = places % WIN_T
    time_rel = time_at[:, None] - time_at[None, :] + FRAMES - 1
    row_rel = row_at[:, None] - row_at[None, :] + WIN_T - 1
    col_rel = col_at[:, None] - col_at[None, :] + WIN_T - 1
    return ((time_rel * (2 * WIN_T - 1) + row_rel) * (2 * WIN_T - 1) + col_rel).astype(np.int32)


def to_windows(values, window, is_joint):
    clip_count, frames, side_cells, channels = (
        values.shape[0],
        values.shape[1],
        values.shape[2],
        values.shape[4],
    )
    per_side = side_cells // window
    if is_joint:
        shaped = values.reshape(clip_count, frames, per_side, window, per_side, window, channels)
        shaped = shaped.transpose(0, 2, 4, 1, 3, 5, 6)
        return shaped.reshape(clip_count * per_side * per_side, frames * window * window, channels)
    shaped = values.reshape(clip_count, frames, per_side, window, per_side, window, channels)
    shaped = shaped.transpose(0, 1, 2, 4, 3, 5, 6)
    return shaped.reshape(clip_count * frames * per_side * per_side, window * window, channels)


def from_windows(values, clip_count, frames, side_cells, window, is_joint):
    per_side = side_cells // window
    channels = values.shape[-1]
    if is_joint:
        shaped = values.reshape(clip_count, per_side, per_side, frames, window, window, channels)
        shaped = shaped.transpose(0, 3, 1, 4, 2, 5, 6)
    else:
        shaped = values.reshape(clip_count, frames, per_side, per_side, window, window, channels)
        shaped = shaped.transpose(0, 1, 2, 4, 3, 5, 6)
    return shaped.reshape(clip_count, frames, side_cells, side_cells, channels)


def normalize(values):
    center = values - jnp.mean(values, axis=-1, keepdims=True)
    spread = jnp.mean(center * center, axis=-1, keepdims=True)
    inverse = lax.rsqrt(spread + epsilon)
    return (center * inverse, inverse)


def norm_back(grad_normed, normed, inverse):
    first_mean = jnp.mean(grad_normed, axis=-1, keepdims=True)
    second_mean = jnp.mean(grad_normed * normed, axis=-1, keepdims=True)
    return inverse * (grad_normed - first_mean - normed * second_mean)


def exact_gelu(values):
    return jax.nn.gelu(values, approximate=False)


def gather_rows(values):
    return lax.all_gather(values, "mp", axis=2, tiled=True)


def sum_rows(values):
    return lax.psum_scatter(
        values.astype(jnp.bfloat16), "mp", scatter_dimension=2, tiled=True
    ).astype(jnp.float32)


def gather_grads(values):
    return lax.all_gather(values, "mp", axis=2, tiled=True)


def input_sums(values):
    return lax.psum_scatter(
        values.astype(jnp.bfloat16), "mp", scatter_dimension=2, tiled=True
    ).astype(jnp.float32)


def inputs_again(moved):
    return lax.all_gather(moved, "mp", axis=2, tiled=True)


def attention_scores(query_part, key_part, bias_matrix, key_valid):
    scores = (
        jnp.einsum("nqhe,nkhe->nhqk", query_part, key_part, preferred_element_type=jnp.float32)
        * HEAD_DIM ** (-0.5)
        + bias_matrix[None]
    )
    if key_valid is not None:
        scores = jnp.where(key_valid[:, None, None, :] > 0, scores, masked_score)
    return scores


def local(
    latents,
    cotangent,
    frame_counts,
    band_ids,
    class_ids,
    time_table,
    class_table,
    ada_weight,
    ada_bias,
    qkv_weight,
    out_weight,
    up_weight,
    down_weight,
    spatial_bias,
    joint_bias,
):
    clip_count = latents.shape[0]
    frames = latents.shape[1]
    side_cells = latents.shape[3]
    model_width = latents.shape[4]
    heads_local = spatial_bias.shape[0]
    local_width = heads_local * HEAD_DIM
    dp_count = lax.axis_size("dp")
    mp_count = lax.axis_size("mp")
    col_width = ada_weight.shape[2]
    band_hot = (band_ids[:, None] == jnp.arange(BANDS)[None, :]).astype(jnp.bfloat16)
    class_hot = (class_ids[:, None] == jnp.arange(CLASSES)[None, :]).astype(jnp.bfloat16)
    condition = jnp.dot(band_hot, time_table, preferred_element_type=jnp.float32) + jnp.dot(
        class_hot, class_table, preferred_element_type=jnp.float32
    )
    activity_low = jax.nn.silu(condition).astype(jnp.bfloat16)
    ada_cols, ada_bias_cols = (
        lax.all_gather(ada_weight, "mp", axis=2, tiled=True),
        lax.all_gather(ada_bias, "mp", axis=1, tiled=True),
    )
    mod_part = jnp.einsum(
        "cd,bde->bce", activity_low, ada_cols, preferred_element_type=jnp.float32
    ) + ada_bias_cols[:, None, :].astype(jnp.float32)
    modulation = lax.all_gather(mod_part, "dp", axis=2, tiled=True)
    first_clip = lax.axis_index("dp") * clip_count
    own_mod = lax.dynamic_slice_in_dim(modulation, first_clip, clip_count, 1).reshape(
        2, clip_count, 6, model_width
    )
    frame_valid = (jnp.arange(frames)[None, :] < frame_counts[:, None]).astype(jnp.float32)
    frame_mask = frame_valid[:, :, None, None, None]
    key_frames = np.arange(frames * WIN_T * WIN_T) // (WIN_T * WIN_T)
    joint_cells = key_frames.shape[0]
    per_side = side_cells // WIN_T
    key_valid = frame_valid[:, key_frames]
    key_valid = jnp.broadcast_to(
        key_valid[:, None, :], (clip_count, per_side * per_side, joint_cells)
    ).reshape(clip_count * per_side * per_side, joint_cells)
    w_qkv, w_out, w_up, w_down = (
        lax.all_gather(qkv_weight, "dp", axis=1, tiled=True),
        lax.all_gather(out_weight, "dp", axis=2, tiled=True),
        lax.all_gather(up_weight, "dp", axis=1, tiled=True),
        lax.all_gather(down_weight, "dp", axis=2, tiled=True),
    )
    spatial_index = spatial_table()
    joint_index = joint_table()
    spatial_matrix = spatial_bias.astype(jnp.float32)[:, spatial_index]
    joint_matrix = joint_bias.astype(jnp.float32)[:, joint_index]
    current = latents.astype(jnp.float32)
    stored = []
    for which_block in range(2):
        is_joint = which_block == 1
        window = WIN_T if is_joint else WIN_S
        bias_matrix = joint_matrix if is_joint else spatial_matrix
        mask_keys = key_valid if is_joint else None
        block_mod = own_mod[which_block][:, :, None, None, None, :]
        normed_one, inverse_one = normalize(current)
        moved_one = (normed_one * (1.0 + block_mod[:, 1]) + block_mod[:, 0]).astype(jnp.bfloat16)
        gathered_one = gather_rows(moved_one)
        projected = jnp.einsum(
            "cfyxd,dkh->cfyxkh",
            gathered_one,
            w_qkv[which_block],
            preferred_element_type=jnp.float32,
        ).astype(jnp.bfloat16)
        windows = to_windows(
            projected.reshape(clip_count, frames, side_cells, side_cells, 3 * local_width),
            window,
            is_joint,
        )
        windows = windows.reshape(windows.shape[0], windows.shape[1], 3, heads_local, HEAD_DIM)
        scores = attention_scores(windows[:, :, 0], windows[:, :, 1], bias_matrix, mask_keys)
        row_max = jnp.max(scores, axis=-1, keepdims=True)
        log_total = row_max + jnp.log(jnp.sum(jnp.exp(scores - row_max), axis=-1, keepdims=True))
        probs_low = jnp.exp(scores - log_total).astype(jnp.bfloat16)
        mixed_win = jnp.einsum(
            "nhqk,nkhe->nqhe", probs_low, windows[:, :, 2], preferred_element_type=jnp.float32
        ).astype(jnp.bfloat16)
        mixed_rows = from_windows(
            mixed_win.reshape(mixed_win.shape[0], mixed_win.shape[1], local_width),
            clip_count,
            frames,
            side_cells,
            window,
            is_joint,
        )
        branch_one = sum_rows(
            jnp.einsum(
                "cfyxk,kd->cfyxd",
                mixed_rows,
                w_out[which_block],
                preferred_element_type=jnp.float32,
            )
        )
        after_attn = current + frame_mask * block_mod[:, 2] * branch_one
        normed_two, inverse_two = normalize(after_attn)
        moved_two = (normed_two * (1.0 + block_mod[:, 4]) + block_mod[:, 3]).astype(jnp.bfloat16)
        gathered_two = gather_rows(moved_two)
        hidden = jnp.einsum(
            "cfyxd,dk->cfyxk", gathered_two, w_up[which_block], preferred_element_type=jnp.float32
        )
        activated = exact_gelu(hidden).astype(jnp.bfloat16)
        branch_two = sum_rows(
            jnp.einsum(
                "cfyxk,kd->cfyxd",
                activated,
                w_down[which_block],
                preferred_element_type=jnp.float32,
            )
        )
        current = after_attn + frame_mask * block_mod[:, 5] * branch_two
        stored.append(
            (
                normed_one,
                inverse_one,
                moved_one,
                gathered_one,
                windows,
                log_total,
                mixed_rows,
                branch_one,
                normed_two,
                inverse_two,
                moved_two,
                gathered_two,
                hidden,
                activated,
                branch_two,
            )
        )
    grad_state = cotangent.astype(jnp.float32)
    mod_grads = []
    qkv_grads = []
    out_grads = []
    up_grads = []
    down_grads = []
    table_parts = []
    for which_block in (1, 0):
        is_joint = which_block == 1
        window = WIN_T if is_joint else WIN_S
        bias_matrix = joint_matrix if is_joint else spatial_matrix
        mask_keys = key_valid if is_joint else None
        block_mod = own_mod[which_block][:, :, None, None, None, :]
        (
            normed_one,
            inverse_one,
            moved_one,
            gathered_one,
            windows,
            log_total,
            mixed_rows,
            branch_one,
            normed_two,
            inverse_two,
            moved_two,
            gathered_two,
            hidden,
            activated,
            branch_two,
        ) = stored[which_block]
        grad_gate_two = jnp.sum(frame_mask * grad_state * branch_two, axis=(1, 2, 3))
        grad_rows = gather_grads((frame_mask * block_mod[:, 5] * grad_state).astype(jnp.bfloat16))
        down_grads.append(
            jnp.einsum("cfyxk,cfyxd->kd", activated, grad_rows, preferred_element_type=jnp.float32)
        )
        grad_act = jnp.einsum(
            "cfyxd,kd->cfyxk", grad_rows, w_down[which_block], preferred_element_type=jnp.float32
        )
        grad_hidden = jax.vjp(exact_gelu, hidden)[1](grad_act)[0].astype(jnp.bfloat16)
        inputs_two = inputs_again(moved_two)
        up_grads.append(
            jnp.einsum(
                "cfyxd,cfyxk->dk", inputs_two, grad_hidden, preferred_element_type=jnp.float32
            )
        )
        grad_moved = input_sums(
            jnp.einsum(
                "cfyxk,dk->cfyxd",
                grad_hidden,
                w_up[which_block],
                preferred_element_type=jnp.float32,
            )
        )
        grad_shift_two = jnp.sum(grad_moved, axis=(1, 2, 3))
        grad_scale_two = jnp.sum(grad_moved * normed_two, axis=(1, 2, 3))
        grad_state = grad_state + norm_back(
            grad_moved * (1.0 + block_mod[:, 4]), normed_two, inverse_two
        )
        grad_gate_one = jnp.sum(frame_mask * grad_state * branch_one, axis=(1, 2, 3))
        grad_rows = gather_grads((frame_mask * block_mod[:, 2] * grad_state).astype(jnp.bfloat16))
        out_grads.append(
            jnp.einsum("cfyxk,cfyxd->kd", mixed_rows, grad_rows, preferred_element_type=jnp.float32)
        )
        grad_mixed = jnp.einsum(
            "cfyxd,kd->cfyxk", grad_rows, w_out[which_block], preferred_element_type=jnp.float32
        ).astype(jnp.bfloat16)
        grad_win = to_windows(grad_mixed, window, is_joint)
        grad_win = grad_win.reshape(grad_win.shape[0], grad_win.shape[1], heads_local, HEAD_DIM)
        query_part = windows[:, :, 0]
        key_part = windows[:, :, 1]
        value_part = windows[:, :, 2]
        probs_full = jnp.exp(
            attention_scores(query_part, key_part, bias_matrix, mask_keys) - log_total
        )
        grad_value = jnp.einsum(
            "nhqk,nqhe->nkhe",
            probs_full.astype(jnp.bfloat16),
            grad_win,
            preferred_element_type=jnp.float32,
        ).astype(jnp.bfloat16)
        grad_probs = jnp.einsum(
            "nqhe,nkhe->nhqk", grad_win, value_part, preferred_element_type=jnp.float32
        )
        row_dot = jnp.sum(probs_full * grad_probs, axis=-1, keepdims=True)
        grad_scores = (probs_full * (grad_probs - row_dot)).astype(jnp.bfloat16)
        bias_sum = jnp.sum(grad_scores.astype(jnp.float32), axis=0)
        if is_joint:
            table_parts.append(
                jnp.zeros((heads_local, joint_bias.shape[1]), jnp.float32)
                .at[:, joint_index]
                .add(bias_sum)
            )
        else:
            table_parts.append(
                jnp.zeros((heads_local, spatial_bias.shape[1]), jnp.float32)
                .at[:, spatial_index]
                .add(bias_sum)
            )
        grad_query = (
            jnp.einsum("nhqk,nkhe->nqhe", grad_scores, key_part, preferred_element_type=jnp.float32)
            * HEAD_DIM ** (-0.5)
        ).astype(jnp.bfloat16)
        grad_key = (
            jnp.einsum(
                "nhqk,nqhe->nkhe", grad_scores, query_part, preferred_element_type=jnp.float32
            )
            * HEAD_DIM ** (-0.5)
        ).astype(jnp.bfloat16)
        stacked = jnp.stack([grad_query, grad_key, grad_value], axis=2).reshape(
            grad_query.shape[0], grad_query.shape[1], 3 * local_width
        )
        grad_projected = from_windows(
            stacked, clip_count, frames, side_cells, window, is_joint
        ).reshape(clip_count, frames, side_cells, side_cells, 3, local_width)
        inputs_one = inputs_again(moved_one)
        qkv_grads.append(
            jnp.einsum(
                "cfyxd,cfyxkh->dkh", inputs_one, grad_projected, preferred_element_type=jnp.float32
            )
        )
        grad_moved = input_sums(
            jnp.einsum(
                "cfyxkh,dkh->cfyxd",
                grad_projected,
                w_qkv[which_block],
                preferred_element_type=jnp.float32,
            )
        )
        grad_shift_one = jnp.sum(grad_moved, axis=(1, 2, 3))
        grad_scale_one = jnp.sum(grad_moved * normed_one, axis=(1, 2, 3))
        grad_state = grad_state + norm_back(
            grad_moved * (1.0 + block_mod[:, 1]), normed_one, inverse_one
        )
        mod_grads.append(
            jnp.stack(
                [
                    grad_shift_one,
                    grad_scale_one,
                    grad_gate_one,
                    grad_shift_two,
                    grad_scale_two,
                    grad_gate_two,
                ],
                axis=1,
            )
        )
    grad_mod = jnp.stack(mod_grads[::-1], axis=0).reshape(2, clip_count, 6 * model_width)
    ordered = (
        grad_mod.reshape(2, clip_count, dp_count, mp_count, col_width)
        .transpose(0, 1, 3, 2, 4)
        .reshape(2, clip_count, 6 * model_width)
    )
    summed_cols = lax.psum_scatter(ordered, "mp", scatter_dimension=2, tiled=True)
    grad_mod_cols = lax.all_to_all(summed_cols, "dp", split_axis=2, concat_axis=1, tiled=True)
    grad_ada_weight = jnp.einsum(
        "cd,bce->bde",
        activity_low.astype(jnp.float32),
        grad_mod_cols,
        precision=lax.Precision.HIGHEST,
    )
    grad_ada_bias = jnp.sum(grad_mod_cols, axis=1)
    grad_mod_block = lax.all_gather(grad_mod_cols, "mp", axis=2, tiled=True)
    activity_part = jnp.einsum(
        "bce,bde->cd", grad_mod_block, ada_cols.astype(jnp.float32), precision=lax.Precision.HIGHEST
    )
    grad_activity = lax.psum(activity_part, "dp")
    grad_condition = jax.vjp(jax.nn.silu, condition)[1](grad_activity)[0]
    grad_time = jnp.dot(
        band_hot.astype(jnp.float32).T, grad_condition, precision=lax.Precision.HIGHEST
    )
    grad_class = jnp.dot(
        class_hot.astype(jnp.float32).T, grad_condition, precision=lax.Precision.HIGHEST
    )
    grad_spatial, grad_joint = lax.psum((table_parts[1], table_parts[0]), "dp")
    grad_qkv, grad_out, grad_up, grad_down = (
        lax.psum_scatter(jnp.stack(qkv_grads[::-1], axis=0), "dp", scatter_dimension=1, tiled=True),
        lax.psum_scatter(jnp.stack(out_grads[::-1], axis=0), "dp", scatter_dimension=2, tiled=True),
        lax.psum_scatter(jnp.stack(up_grads[::-1], axis=0), "dp", scatter_dimension=1, tiled=True),
        lax.psum_scatter(
            jnp.stack(down_grads[::-1], axis=0), "dp", scatter_dimension=2, tiled=True
        ),
    )
    return (
        current,
        grad_state,
        grad_time,
        grad_class,
        grad_ada_weight,
        grad_ada_bias,
        grad_qkv,
        grad_out,
        grad_up,
        grad_down,
        grad_spatial,
        grad_joint,
    )


def solution_any(mesh):
    placed = (
        P("dp", None, "mp", None, None),
        P("dp", None, "mp", None, None),
        P("dp"),
        P(),
        P(),
        P(),
        P(),
        P(None, None, ("dp", "mp")),
        P(None, ("dp", "mp")),
        P(None, "dp", None, "mp"),
        P(None, "mp", "dp"),
        P(None, "dp", "mp"),
        P(None, "mp", "dp"),
        P("mp", None),
        P("mp", None),
    )
    return jax.shard_map(
        local,
        mesh=mesh,
        in_specs=placed,
        out_specs=(
            P("dp", None, "mp", None, None),
            P("dp", None, "mp", None, None),
            P(),
            P(),
            P(None, None, ("dp", "mp")),
            P(None, ("dp", "mp")),
            P(None, "dp", None, "mp"),
            P(None, "mp", "dp"),
            P(None, "dp", "mp"),
            P(None, "mp", "dp"),
            P("mp", None),
            P("mp", None),
        ),
        check_vma=False,
    )


low = jnp.bfloat16
full = jnp.float32
HALF_ROOT = 0.7071067811865476
PHI_AT_ZERO = 0.3989422804014327
MIB = 1024 * 1024


def flip(values, axis):
    return lax.ppermute(values, axis, [(0, 1), (1, 0)])


def z_trade(values, step):
    return lax.ppermute(values, "z", [(place, place ^ step) for place in range(4)])


def swap_only(values):
    return lax.ppermute(values, ("c", "x"), [(1, 2), (2, 1)])


def swap(values):
    return jnp.where(lax.axis_index("c") == lax.axis_index("x"), values, swap_only(values))


def shape_of(dims, dtype=low):
    return jax.ShapeDtypeStruct(tuple(dims), dtype)


def whole(array):
    zeros = (0,) * len(array.shape)
    return pl.BlockSpec(tuple(array.shape), lambda *at: zeros)


def whole_once(array):
    zeros = (0,) * len(array.shape)
    return pl.BlockSpec(
        tuple(array.shape), lambda *at: zeros, pipeline_mode=pl.Buffered(1)
    )


def space_of(dims, dtype):
    dims = [1] * (2 - len(dims)) + list(dims)
    size = jnp.dtype(dtype).itemsize
    rows = 32 // size
    dims[-1] = -(-dims[-1] // 128) * 128
    dims[-2] = -(-dims[-2] // rows) * rows
    return int(np.prod(dims)) * size


def room_for(specs, arrays, scratch):
    total = 0
    for spec, array in zip(specs, arrays):
        if spec.block_shape is not None:
            once = spec.pipeline_mode is not None
            total += space_of(spec.block_shape, array.dtype) * (1 if once else 2)
    return total + sum(space_of(held.shape, held.dtype) for held in scratch)


class Chain:
    def __init__(self, info):
        self.info = info
        self.last = []
        self.pending = []

    def wait(self, *values):
        self.pending += values

    def run(self, name, kernel, args, in_specs, outs, out_specs, grid=(1,), scratch=(), extra=3, waits=()):
        count = len(args)
        unread = self.last + self.pending + list(waits)
        self.pending = []
        held = len(unread)

        limit = room_for(list(in_specs) + list(out_specs), list(args) + list(outs), scratch)

        def body(*refs):
            kernel(*refs[: 1 + count], *refs[1 + count + held :])

        results = pl.pallas_call(
            body,
            grid_spec=pltpu.PrefetchScalarGridSpec(
                num_scalar_prefetch=1,
                grid=grid,
                in_specs=list(in_specs) + [pl.BlockSpec(memory_space=pl.ANY)] * held,
                out_specs=list(out_specs),
                scratch_shapes=list(scratch),
            ),
            out_shape=list(outs),
            compiler_params=pltpu.CompilerParams(vmem_limit_bytes=limit + extra * MIB),
            cost_estimate=pl.CostEstimate(flops=1, bytes_accessed=1, transcendentals=0),
            name=name,
        )(self.info, *args, *unread)
        self.last = [results[0]]
        return results


def pack_arguments(chain, up, down, qkv, out):
    def kernel(info, up_in, down_in, qkv_in, out_in, packed):
        start = 0
        for part in (up_in[0], down_in[0], qkv_in[1], out_in[1], up_in[1], down_in[1]):
            packed[:, start : start + part.shape[1]] = part
            start += part.shape[1]

    args = [up, down, qkv, out]
    result = shape_of((up.shape[1], 5 * PIECE))
    (packed,) = chain.run(
        "pack_arguments", kernel, args, [whole(v) for v in args], [result], [whole(result)]
    )
    return packed


def copy_rows(chain, values):
    def kernel(info, source, result):
        result[...] = source[...]

    spec = pl.BlockSpec((ROW_TILE, values.shape[1]), lambda i, info: (i, 0))
    (result,) = chain.run(
        "copy_rows", kernel, [values], [spec], [shape_of(values.shape)], [spec], grid=(2,)
    )
    return result


def cut_kernel(info, packed, traded, *outs):
    start = 0
    for out in outs:
        width = out.shape[1]
        cols = slice(start, start + width)

        @pl.when(info[4] == 1)
        def _():
            out[...] = packed[:, cols]

        @pl.when(info[4] == 0)
        def _():
            out[...] = traded[:, cols]

        start += width


PIECE = 2048
PIECE_TILE = 512


def tile_spec(count, rows=64):
    return pl.BlockSpec((count, rows, PIECE_TILE), lambda j, info: (0, 0, j))


def flat_spec(rows=64):
    return pl.BlockSpec((rows, PIECE_TILE), lambda j, info: (0, j))


class Gather:
    def __init__(self, chain, shards):
        self.chain = chain
        self.shards = shards
        self.near = {}
        self.sent = {}
        self.got = {}
        self.step_at = 0

    def over_z(self, at):
        self.near[at] = [z_trade(self.shards[at], k) for k in (1, 2, 3)]

    def step(self):
        at = self.step_at
        self.step_at += 1
        own = at < len(self.shards)
        far = at > 0
        args, specs = [], []
        if own:
            args += [self.shards[at]] + self.near[at]
            specs += [flat_spec()] * 4
        start = 0
        if far:
            got_x, got_y = self.got[at - 1]
            start = (got_x.shape[0] - 4) // 2
            args += [got_x, got_y]
            specs += [
                pl.BlockSpec((2, 64, PIECE_TILE), lambda j, info: (start + 1, 0, j)),
                pl.BlockSpec((2, 64, PIECE_TILE), lambda j, info: (start, 0, j)),
            ]

        def kernel(info, *refs):
            to_x, to_y = refs[-2:]
            if own:
                for k in range(4):
                    to_x[(2 if far else 0) + k] = refs[k][...]
                    to_y[(2 if far else 0) + k] = refs[k][...]
            if far:
                from_x, from_y = refs[-4:-2]
                to_x[0:2] = from_y[...]
                to_y[0:2] = from_x[...]

        count = (2 if far else 0) + (4 if own else 0)
        outs = [shape_of((count, 64, PIECE))] * 2
        to_x, to_y = self.chain.run(
            "gather_step",
            kernel,
            args,
            specs,
            outs,
            [tile_spec(count)] * 2,
            grid=(PIECE // PIECE_TILE,),
        )
        self.sent[at] = to_x
        self.got[at] = (flip(to_x, "x"), flip(to_y, "y"))

    def place(self, at, widths):
        def kernel(info, own, from_x, from_y, far_lo, far_hi, *outs):
            k = pl.program_id(0)
            place = info[1] * 2 + info[2]

            def put(rel, block):
                start = 0
                for out in outs:
                    width = out.shape[3]
                    out[0, place ^ rel] = block[0, :, start : start + width]
                    start += width

            put(0, own)
            put(1, from_x)
            put(2, from_y)

            @pl.when(k < 2)
            def _():
                put(3, far_lo)

            @pl.when(k >= 2)
            def _():
                put(3, far_hi)

        got_x, got_y = self.got[at]
        start = got_x.shape[0] - 4
        block = (1, 64, PIECE)
        quad = pl.BlockSpec(block, lambda k, info: (k + start, 0, 0))
        results = self.chain.run(
            "place_weights",
            kernel,
            [self.sent[at], got_x, got_y, *self.got[at + 1]],
            [
                quad,
                quad,
                quad,
                pl.BlockSpec(block, lambda k, info: (jnp.minimum(k, 1), 0, 0)),
                pl.BlockSpec(block, lambda k, info: (jnp.maximum(k - 2, 0), 0, 0)),
            ],
            [shape_of((4, 4, 64, w)) for w in widths],
            [pl.BlockSpec((1, 4, 64, w), lambda k, info: (info[0] ^ k, 0, 0, 0)) for w in widths],
            grid=(4,),
        )
        return [a.reshape(16 * 64, a.shape[3]) for a in results]


GRAD_TILE = 512


def weight_grad_kernel(info, *refs, pairs, tiles):
    lhs = refs[: 4 * pairs]
    rhs = refs[4 * pairs : 5 * pairs]
    near, to_x, to_y, far_lo, far_hi = refs[5 * pairs : 5 * pairs + 5]
    held = refs[5 * pairs + 5]
    across = refs[5 * pairs + 6 :]
    j = pl.program_id(0)
    place = info[1] * 2 + info[2]
    begin = 0
    for at in range(pairs):

        @pl.when(j == begin)
        def _():
            for part in range(4):
                cols = slice(part * ROW_TILE, (part + 1) * ROW_TILE)
                across[at][:, cols] = lhs[4 * at + part][...].T

        @pl.when((j >= begin) & (j < begin + tiles[at]))
        def _():
            tokens = rhs[at][...].reshape(4 * ROW_TILE, GRAD_TILE)
            for rows in range(0, held.shape[0], 256):
                block = jnp.dot(
                    across[at][rows : rows + 256], tokens, preferred_element_type=full
                )
                held[rows : rows + 256] = block.astype(low)

        begin += tiles[at]

    def part(z, rel):
        return held[pl.ds(pl.multiple_of(z * 256 + (place ^ rel) * 64, 64), 64), :]

    for z in range(4):
        near[z] = part(z, 0)
        to_x[z] = part(z, 1)
        to_y[z] = part(z, 2)
        if z < 2:
            far_lo[z] = part(z, 3)
        else:
            far_hi[z - 2] = part(z, 3)


class Scatter:
    def __init__(self, chain):
        self.chain = chain
        self.parts = []
        self.got = None
        self.held = None
        self.done = []
        self.step_at = 0

    def weight_grad(self, *items):
        pairs = len(items)
        widths = tuple(item[2].shape[2] for item in items)
        rows, features = items[0][0][0].shape
        tiles = [w // GRAD_TILE for w in widths]
        quads = shape_of((4, 64, PIECE))
        twos = shape_of((2, 64, PIECE))

        def rhs_spec(at):
            first, last = sum(tiles[:at]), tiles[at] - 1
            return pl.BlockSpec(
                (2, 2 * rows, GRAD_TILE),
                lambda j, info: (0, 0, jnp.clip(j - first, 0, last)),
            )

        quad_spec = pl.BlockSpec((4, 64, GRAD_TILE), lambda j, info: (0, 0, j))
        two_spec = pl.BlockSpec((2, 64, GRAD_TILE), lambda j, info: (0, 0, j))
        lhs = [part for item in items for pair in item[:2] for part in pair]
        self.parts.append(
            self.chain.run(
                "weight_grad",
                lambda *refs: weight_grad_kernel(*refs, pairs=pairs, tiles=tiles),
                lhs + [item[2] for item in items],
                [whole_once(v) for v in lhs] + [rhs_spec(at) for at in range(pairs)],
                [quads, quads, quads, twos, twos],
                [quad_spec] * 3 + [two_spec] * 2,
                grid=(PIECE // GRAD_TILE,),
                scratch=[pltpu.VMEM((features, GRAD_TILE), low)]
                + [pltpu.VMEM((features, 4 * rows), low)] * pairs,
                extra=3,
            )
        )
        if len(self.parts) == 1:
            self.got = (flip(self.parts[0][3], "x"), flip(self.parts[0][4], "y"))

    def step(self, total):
        at = self.step_at
        self.step_at += 1
        far = at + 1 < total
        mid = at < total
        near = 0 <= at - 1 < total
        last = 0 <= at - 2 < total
        args, specs = [], []

        def put(array, spec):
            args.append(array)
            specs.append(spec)
            return len(args) - 1

        names = {}
        if far:
            names["far_lo"] = put(self.parts[at + 1][3], tile_spec(2))
            names["far_hi"] = put(self.parts[at + 1][4], tile_spec(2))
        if mid:
            names["to_x"] = put(self.parts[at][1], tile_spec(4))
            names["to_y"] = put(self.parts[at][2], tile_spec(4))
        if near:
            names["near"] = put(self.parts[at - 1][0], tile_spec(4))
        if mid or near:
            count = self.got[0].shape[0]
            names["got_x"] = put(self.got[0], tile_spec(count))
            names["got_y"] = put(self.got[1], tile_spec(count))
        if last:
            for k in range(4):
                names["held%d" % k] = put(self.held[k], flat_spec())
        outs, out_specs = [], []
        sent = (2 if far else 0) + (4 if mid else 0)
        if mid:
            outs += [shape_of((sent, 64, PIECE))] * 2
            out_specs += [tile_spec(sent)] * 2
        if near:
            outs += [shape_of((64, PIECE), full)] + [shape_of((64, PIECE))] * 3
            out_specs += [flat_spec()] * 4
        if last:
            outs.append(shape_of((64, PIECE)))
            out_specs.append(flat_spec())
        number = len(args)

        def kernel(info, *refs):
            out = list(refs[number:])
            get = {name: refs[spot] for name, spot in names.items()}
            if mid:
                out_x, out_y = out[:2]
                del out[:2]
                start = 0
                if far:
                    out_x[0:2] = get["far_lo"][...]
                    out_y[0:2] = get["far_hi"][...]
                    start = 2
                for k in range(4):
                    part_x = get["to_x"][k]
                    part_y = get["to_y"][k]
                    if k < 2:
                        part_y = (part_y.astype(full) + get["got_x"][k].astype(full)).astype(low)
                    else:
                        part_x = (
                            part_x.astype(full) + get["got_y"][k - 2].astype(full)
                        ).astype(low)
                    out_x[start + k] = part_x
                    out_y[start + k] = part_y
            if near:
                start = get["got_x"].shape[0] - 4
                for k in range(4):
                    spot = info[0] ^ k
                    value = get["near"][spot].astype(full)
                    value = value + get["got_x"][start + spot].astype(full)
                    value = value + get["got_y"][start + spot].astype(full)
                    out[k][...] = value.astype(out[k].dtype)
                del out[:4]
            if last:
                value = get["held0"][...]
                for k in (1, 2, 3):
                    value = value + get["held%d" % k][...].astype(full)
                out[0][...] = value.astype(low)

        results = list(
            self.chain.run(
                "scatter_step", kernel, args, specs, outs, out_specs, grid=(PIECE // PIECE_TILE,)
            )
        )
        if mid:
            self.got = (flip(results[0], "x"), flip(results[1], "y"))
            del results[:2]
        if near:
            self.held = [results[0]] + [z_trade(results[k], k) for k in (1, 2, 3)]
            del results[:4]
        if last:
            self.done.append(results[0])


def offset_columns():
    cells = np.arange(WIN_T * WIN_T)
    spots = 119 - (cells // WIN_T * 16 + cells % WIN_T)
    hot = (spots[:, None] == np.arange(256)[None, :]).astype(np.float32)
    return jnp.asarray(np.concatenate([hot] * 3), low)


def bias_tables(chain, sums):
    heads, sides = sums[0].shape[:2]

    def kernel(info, *refs):
        hot = refs[len(sums)][...]
        for at, out in enumerate(refs[len(sums) + 1 :]):
            for h in range(heads):
                values = refs[at][h].reshape(sides * 64, 64)
                first = values.astype(low)
                rest = values - first.astype(full)
                second = rest.astype(low)
                third = (rest - second.astype(full)).astype(low)
                parts = jnp.concatenate([first, second, third], axis=1)
                spread = jnp.dot(parts, hot, preferred_element_type=full)
                spread = spread.reshape(sides, 8, 8, 256)
                by_row = spread[:, 0]
                for row in range(1, 8):
                    by_row = by_row + pltpu.roll(spread[:, row], 16 * row, 2)
                total = by_row[:, 0]
                for col in range(1, 8):
                    total = total + pltpu.roll(by_row[:, col], col, 1)
                out[h] = total

    hot = offset_columns()
    args = list(sums) + [hot]
    outs = [shape_of((heads, sides, 256), full)] * len(sums)
    return chain.run(
        "bias_tables", kernel, args, [whole(v) for v in args], outs, [whole(v) for v in outs], extra=8
    )


def collect_sums(chain, sums):
    spots = [(4, 0), (4, 1), (3, 2), (3, 0), (3, 1), (2, 2), (2, 0), (2, 1), (1, 2), (1, 0), (1, 1), (0, 0)]

    def kernel(info, *refs):
        for row, (at, spot) in enumerate(spots):
            refs[-1][row : row + 1] = refs[at][spot : spot + 1]

    out = shape_of((len(spots), sums[0].shape[1]), full)
    (result,) = chain.run(
        "collect_sums", kernel, list(sums), [whole(v) for v in sums], [out], [whole(out)]
    )
    return result


def add_all(chain, *values):
    def kernel(info, *refs):
        total = refs[0][...]
        for other in refs[1:-2]:
            total = total + other[...].astype(full)
        refs[-2][...] = total
        refs[-1][...] = total.astype(low)

    outs = [shape_of(values[0].shape, full), shape_of(values[0].shape)]
    return chain.run(
        "add_all",
        kernel,
        list(values),
        [whole(v) for v in values],
        outs,
        [whole(v) for v in outs],
    )


def join_pieces(chain, pieces, *copied):
    count = len(pieces)

    def kernel(info, *refs):
        out = refs[count + len(copied)]
        for at in range(count):
            out[:, at * PIECE : (at + 1) * PIECE] = refs[at][...]
        for at in range(len(copied)):
            refs[count + len(copied) + 1 + at][...] = refs[count + at][...]

    args = list(pieces) + list(copied)
    outs = [shape_of((64, PIECE * count))] + [shape_of(v.shape) for v in copied]
    return chain.run(
        "join_pieces", kernel, args, [whole(v) for v in args], outs, [whole(v) for v in outs]
    )


def gelu_and_slope(values):
    bell = jnp.exp(-0.5 * values * values)
    t = 1.0 / (1.0 + (0.3275911 * HALF_ROOT) * jnp.abs(values))
    poly = t * (
        0.254829592
        + t * (-0.284496736 + t * (1.421413741 + t * (-1.453152027 + t * 1.061405429)))
    )
    tail = 0.5 * poly * bell
    phi = jnp.where(values >= 0, 1.0 - tail, tail)
    return values * phi, phi + (PHI_AT_ZERO * values) * bell


ROW_TILE = 320


def flip_rows(pair):
    return tuple(flip(part, "c") for part in pair)


def both_kernel(info, *refs, kind):
    weight = refs[4][...]
    for part in range(4):
        half = part // 2
        rows = slice(part % 2 * ROW_TILE, (part % 2 + 1) * ROW_TILE)
        product = jnp.dot(refs[part][...], weight, preferred_element_type=full)
        if kind == "gelu":
            act, slope = gelu_and_slope(product)
            refs[5][half, rows] = act.astype(low)
            refs[6][half, rows] = slope.astype(low)
        elif kind == "slope":
            refs[6][half, rows] = (product * refs[5][half, rows].astype(full)).astype(low)
        else:
            refs[5][half, rows] = product.astype(low)


def both_times(chain, kind, own, other, weight, slope=None, waits=()):
    depth = weight.shape[0]
    rows = 2 * ROW_TILE
    width = weight.shape[1]
    tile = 512
    out_spec = pl.BlockSpec((2, rows, tile), lambda j, info: (0, 0, j))
    extra = [] if slope is None else [slope]
    count = 2 if kind == "gelu" else 1
    return chain.run(
        "both_" + kind,
        lambda *refs: both_kernel(*refs, kind=kind),
        [*own, *other, weight] + extra,
        [whole_once(part) for part in (*own, *other)]
        + [pl.BlockSpec((depth, tile), lambda j, info: (0, j))]
        + [out_spec] * len(extra),
        [shape_of((2, rows, width))] * count,
        [out_spec] * count,
        grid=(width // tile,),
        waits=waits,
    )


def times_back(values, weight):
    return lax.dot_general(
        values, weight, (((1,), (1,)), ((), ())), preferred_element_type=full
    ).astype(low)


def other_rows(chain, values, weight):
    rows, depth = values.shape[1:]
    width = weight.shape[0]
    tile = 256

    def kernel(info, rows_in, weight_in, first, second):
        result = times_back(rows_in[0], weight_in[...])
        first[...] = result[:ROW_TILE]
        second[...] = result[ROW_TILE:]

    half = pl.BlockSpec((ROW_TILE, tile), lambda j, info: (0, j))
    results = chain.run(
        "other_rows",
        kernel,
        [values, weight],
        [
            pl.BlockSpec(
                (1, rows, depth), lambda j, info: (1, 0, 0), pipeline_mode=pl.Buffered(1)
            ),
            pl.BlockSpec((tile, depth), lambda j, info: (j, 0)),
        ],
        [shape_of((ROW_TILE, width))] * 2,
        [half] * 2,
        grid=(width // tile,),
    )
    return flip_rows(results)


def put_half(pair, values):
    @pl.when(pl.program_id(0) == 0)
    def _():
        pair[0][...] = values

    @pl.when(pl.program_id(0) == 1)
    def _():
        pair[1][...] = values


def get_half(pair):
    return jnp.where(pl.program_id(0) == 0, pair[0][...].astype(full), pair[1][...].astype(full))


def shown_rows(info):
    first = pl.program_id(0) * ROW_TILE
    row = first + lax.broadcasted_iota(jnp.int32, (ROW_TILE, 1), 0)
    return (row < info[3] * 128).astype(full)


def norm_and_move(values, shift, scale):
    center = values - jnp.mean(values, axis=-1, keepdims=True)
    spread = jnp.mean(center * center, axis=-1, keepdims=True)
    inverse = lax.rsqrt(spread + epsilon)
    normed = center * inverse
    return normed.astype(low), inverse, (normed * (1.0 + scale) + shift).astype(low)


def row_specs(model_width):
    tall = pl.BlockSpec((ROW_TILE, model_width), lambda i, info: (i, 0))
    thin = pl.BlockSpec((ROW_TILE, 1), lambda i, info: (i, 0))
    return tall, thin


def first_norm(chain, current, traded, rows_of):
    rows, model_width = current.shape
    tall, thin = row_specs(model_width)

    def kernel(info, ours, theirs, given, kept, normed, inverse, *moved):
        values = jnp.where(info[4] == 1, ours[...].astype(full), theirs[...].astype(full))
        kept[...] = values.astype(low)
        normed[...], inverse[...], result = norm_and_move(values, given[0:1], given[1:2])
        put_half(moved, result)

    half = shape_of((ROW_TILE, model_width))
    kept, normed, inverse, *moved = chain.run(
        "first_norm",
        kernel,
        [current, traded, rows_of],
        [tall, tall, whole_once(rows_of)],
        [shape_of(current.shape)] * 2 + [shape_of((rows, 1), full), half, half],
        [tall, tall, thin, whole(half), whole(half)],
        grid=(rows // ROW_TILE,),
    )
    return kept, normed, inverse, moved


def forward_step(chain, values, weight, away, current, rows_of, last, waits=()):
    rows, model_width = current.shape
    depth = values.shape[2]
    tall, thin = row_specs(model_width)

    def kernel(info, own, weight_in, first, second, current_in, given, after, branch_out, *rest):
        branch = times_back(own[0], weight_in[...]).astype(full) + get_half((first, second))
        total = current_in[...].astype(full) + shown_rows(info) * given[0:1] * branch
        after[...] = total.astype(after.dtype)
        branch_out[...] = branch.astype(low)
        if not last:
            normed, inverse, *moved = rest
            normed[...], inverse[...], result = norm_and_move(total, given[1:2], given[2:3])
            put_half(moved, result)

    outs = [shape_of(current.shape, low if last else full), shape_of(current.shape)]
    specs = [tall, tall]
    if not last:
        half = shape_of((ROW_TILE, model_width))
        outs += [shape_of(current.shape), shape_of((rows, 1), full), half, half]
        specs += [tall, thin, whole(half), whole(half)]
    results = chain.run(
        "forward_step",
        kernel,
        [values, weight, *away, current, rows_of],
        [
            pl.BlockSpec((1, ROW_TILE, depth), lambda i, info: (0, i, 0)),
            whole_once(weight),
            whole_once(away[0]),
            whole_once(away[1]),
            tall,
            whole_once(rows_of),
        ],
        outs,
        specs,
        grid=(rows // ROW_TILE,),
        waits=waits,
    )
    return results if last else (*results[:4], results[4:])


def add_rows(out, at, values):
    total = jnp.sum(values, axis=0, keepdims=True)

    @pl.when(pl.program_id(0) == 0)
    def _():
        out[at : at + 1] = total

    @pl.when(pl.program_id(0) > 0)
    def _():
        out[at : at + 1] += total


def first_back(chain, state, branch, gate):
    rows, model_width = state.shape
    tall, _ = row_specs(model_width)

    def kernel(info, state_in, branch_in, gate_in, first, second, sums):
        values = state_in[...].astype(full) * shown_rows(info)
        put_half((first, second), (values * gate_in[...]).astype(low))
        add_rows(sums, 0, values * branch_in[...].astype(full))

    sums = shape_of((8, model_width), full)
    half = shape_of((ROW_TILE, model_width))
    first, second, sums = chain.run(
        "first_back",
        kernel,
        [state, branch, gate],
        [tall, tall, whole_once(gate)],
        [half, half, sums],
        [whole(half), whole(half), whole(sums)],
        grid=(rows // ROW_TILE,),
    )
    return (first, second), sums


def backward_step(chain, values, weight, away, normed, inverse, state, rows_of, branch):
    rows, model_width = state.shape
    depth = values.shape[2]
    tall, thin = row_specs(model_width)
    last = branch is None

    def kernel(
        info, own, weight_in, first, second, normed_in, inverse_in, state_in, given, *rest
    ):
        grad = times_back(own[0], weight_in[...]).astype(full) + get_half((first, second))
        normal = normed_in[...].astype(full)
        moved = grad * (1.0 + given[0:1])
        first_mean = jnp.mean(moved, axis=-1, keepdims=True)
        second_mean = jnp.mean(moved * normal, axis=-1, keepdims=True)
        total = state_in[...].astype(full) + inverse_in[...] * (
            moved - first_mean - normal * second_mean
        )
        if last:
            state_out, sums = rest
        else:
            branch_in, state_out, sums, *sent = rest
        state_out[...] = total.astype(state_out.dtype)
        add_rows(sums, 0, grad)
        add_rows(sums, 1, grad * normal)
        if not last:
            shown = total * shown_rows(info)
            put_half(sent, (shown * given[1:2]).astype(low))
            add_rows(sums, 2, shown * branch_in[...].astype(full))

    sums = shape_of((8, model_width), full)
    outs = [shape_of(state.shape, low if last else full), sums]
    specs = [tall, whole(sums)]
    if not last:
        half = shape_of((ROW_TILE, model_width))
        outs += [half, half]
        specs += [whole(half)] * 2
    extra = [] if last else [branch]
    results = chain.run(
        "backward_step",
        kernel,
        [values, weight, *away, normed, inverse, state, rows_of] + extra,
        [
            pl.BlockSpec((1, ROW_TILE, depth), lambda i, info: (0, i, 0)),
            whole_once(weight),
            whole_once(away[0]),
            whole_once(away[1]),
            tall,
            thin,
            tall,
            whole_once(rows_of),
        ]
        + [tall] * len(extra),
        outs,
        specs,
        grid=(rows // ROW_TILE,),
    )
    return results if last else (*results[:2], results[2:])


def attend_kernel(info, blocks, joined, mixed, probs, bias, *, heads, cells, masked, sides):
    width = heads * HEAD_DIM

    @pl.when((pl.program_id(0) == 0) & (pl.program_id(1) == 0))
    def _():
        for h in range(heads):
            for place, spots in enumerate(sides):
                block = blocks[h, place]
                for row, col in spots:
                    bias[h, row * 64 : row * 64 + 64, col * 64 : col * 64 + 64] = block

    values = joined[...].reshape(cells, 3 * width)
    lead = mixed.shape
    if masked:
        column = lax.broadcasted_iota(jnp.int32, (1, cells), 1)
        shown = column < info[3] * (WIN_T * WIN_T)
    outs = []
    for h in range(heads):
        cols = slice(h * HEAD_DIM, (h + 1) * HEAD_DIM)
        query = values[:, cols]
        key = values[:, width + h * HEAD_DIM : width + (h + 1) * HEAD_DIM]
        value = values[:, 2 * width + h * HEAD_DIM : 2 * width + (h + 1) * HEAD_DIM]
        scores = lax.dot_general(
            query, key, (((1,), (1,)), ((), ())), preferred_element_type=full
        ) * HEAD_DIM ** (-0.5) + bias[h].astype(full)
        if masked:
            scores = jnp.where(shown, scores, masked_score)
        weights = jnp.exp(scores - jnp.max(scores, axis=-1, keepdims=True))
        share = (weights * (1.0 / jnp.sum(weights, axis=-1, keepdims=True))).astype(low)
        probs[0, h] = share
        outs.append(jnp.dot(share, value, preferred_element_type=full).astype(low))
    mixed[...] = jnp.concatenate(outs, axis=1).reshape(lead)


def attend_back_kernel(info, joined, grad, probs, back, bias_out, total, *, heads, cells, sides):
    step = pl.program_id(0) * pl.num_programs(1) + pl.program_id(1)
    width = heads * HEAD_DIM
    values = joined[...].reshape(cells, 3 * width)
    grads = grad[...].reshape(cells, width)
    grads_t = grads.astype(full).T.astype(low)
    queries_t = values[:, :width].astype(full).T.astype(low)
    queries, keys_t, values_t = [], [], []

    @pl.when(step == 0)
    def _():
        total[...] = jnp.zeros(total.shape, full)

    for h in range(heads):
        cols = slice(h * HEAD_DIM, (h + 1) * HEAD_DIM)
        key = values[:, width + h * HEAD_DIM : width + (h + 1) * HEAD_DIM]
        value = values[:, 2 * width + h * HEAD_DIM : 2 * width + (h + 1) * HEAD_DIM]
        share = probs[0, h]
        values_t.append(jnp.dot(grads_t[cols], share, preferred_element_type=full).astype(low))
        grad_share = lax.dot_general(
            grads[:, cols], value, (((1,), (1,)), ((), ())), preferred_element_type=full
        )
        share_full = share.astype(full)
        product = share_full * grad_share
        row_dot = jnp.sum(product, axis=-1, keepdims=True)
        grad_scores = (product - share_full * row_dot).astype(low)
        total[h] += grad_scores.astype(full)
        queries.append(
            (jnp.dot(grad_scores, key, preferred_element_type=full) * HEAD_DIM ** (-0.5)).astype(
                low
            )
        )
        keys_t.append(
            (
                jnp.dot(queries_t[cols], grad_scores, preferred_element_type=full)
                * HEAD_DIM ** (-0.5)
            ).astype(low)
        )
    key_grads = jnp.concatenate(keys_t, axis=0).astype(full).T.astype(low)
    value_grads = jnp.concatenate(values_t, axis=0).astype(full).T.astype(low)
    back[...] = jnp.concatenate(queries + [key_grads, value_grads], axis=1).reshape(back.shape)

    @pl.when(step == pl.num_programs(0) * pl.num_programs(1) - 1)
    def _():
        for h in range(heads):
            for place, spots in enumerate(sides):
                part = None
                for row, col in spots:
                    block = total[h, row * 64 : row * 64 + 64, :][:, col * 64 : col * 64 + 64]
                    part = block if part is None else part + block
                bias_out[h, place] = part


def spatial_sides():
    sides = [[] for _ in range(9)]
    for row in range(4):
        for col in range(4):
            place = (row // 2 - col // 2 + 1) * 3 + (row % 2 - col % 2 + 1)
            sides[place].append((row, col))
    return sides


def joint_sides():
    sides = [[] for _ in range(2 * FRAMES - 1)]
    for row in range(FRAMES):
        for col in range(FRAMES):
            sides[row - col + FRAMES - 1].append((row, col))
    return sides


def window_specs(is_joint, frames, width):
    if is_joint:
        shape, at = (1, frames, 1, 64, width), lambda i, j, info: (i, 0, j, 0, 0)
    else:
        shape, at = (2, 1, 2, 64, width), lambda i, j, info: (0, j, 0, 0, 0)
    return pl.BlockSpec(shape, at)


def attend(chain, blocks, joined, is_joint):
    frames = joined.shape[1]
    heads = blocks.shape[0]
    width = heads * HEAD_DIM
    grid = (2, 2) if is_joint else (1, frames)
    cells = 64 * frames if is_joint else 256
    number = grid[0] * grid[1]
    sides = joint_sides() if is_joint else spatial_sides()
    fetch = lambda i, j, info: (i * grid[1] + j, 0, 0, 0)
    return chain.run(
        "attend_joint" if is_joint else "attend_spatial",
        lambda *refs: attend_kernel(
            *refs, heads=heads, cells=cells, masked=is_joint, sides=sides
        ),
        [blocks, joined],
        [whole_once(blocks), window_specs(is_joint, frames, 3 * width)],
        [shape_of(joined.shape[:4] + (width,)), shape_of((number, heads, cells, cells))],
        [window_specs(is_joint, frames, width), pl.BlockSpec((1, heads, cells, cells), fetch)],
        grid=grid,
        scratch=[pltpu.VMEM((heads, cells, cells), low)],
    )


def attend_back(chain, joined, grad, probs, is_joint):
    frames = joined.shape[1]
    number, heads, cells, _ = probs.shape
    width = heads * HEAD_DIM
    grid = (2, 2) if is_joint else (1, frames)
    sides = joint_sides() if is_joint else spatial_sides()
    fetch = lambda i, j, info: (i * grid[1] + j, 0, 0, 0)
    sums = shape_of((heads, 9, 64, 64), full)
    return chain.run(
        "attend_back_joint" if is_joint else "attend_back_spatial",
        lambda *refs: attend_back_kernel(*refs, heads=heads, cells=cells, sides=sides),
        [joined, grad, probs],
        [
            window_specs(is_joint, frames, 3 * width),
            window_specs(is_joint, frames, width),
            pl.BlockSpec((1, heads, cells, cells), fetch),
        ],
        [shape_of(joined.shape), sums],
        [window_specs(is_joint, frames, 3 * width), whole(sums)],
        grid=grid,
        scratch=[pltpu.VMEM((heads, cells, cells), full)],
        extra=5,
    )


def offset_hot():
    places = np.arange(WIN_T * WIN_T)
    rows = places[:, None] // WIN_T - places[None, :] // WIN_T + WIN_T - 1
    cols = places[:, None] % WIN_T - places[None, :] % WIN_T + WIN_T - 1
    spots = (rows * (2 * WIN_T - 1) + cols).reshape(-1).astype(np.int32)
    return jnp.arange((2 * WIN_T - 1) ** 2, dtype=jnp.int32)[:, None] == jnp.asarray(spots)[None]


def fast_local(
    latents,
    cotangent,
    frame_counts,
    band_ids,
    class_ids,
    time_table,
    class_table,
    ada_weight,
    ada_bias,
    qkv_weight,
    out_weight,
    up_weight,
    down_weight,
    spatial_bias,
    joint_bias,
):
    frames = latents.shape[1]
    model_width = latents.shape[4]
    heads = spatial_bias.shape[0]
    width = heads * HEAD_DIM
    hidden = up_weight.shape[2]
    col_width = ada_weight.shape[2]
    rows = frames * 128
    z, y, c, x = (lax.axis_index(name) for name in ("z", "y", "c", "x"))
    counts = frame_counts.astype(full)
    count = jnp.where(c == x, counts, flip(counts, "c")).astype(jnp.int32)
    same = (c == x).astype(jnp.int32)
    chain = Chain(
        jnp.concatenate([jnp.stack([z, y, x]).astype(jnp.int32), count, same.reshape(1)])
    )

    def rearranged(values):
        shaped = values.reshape(frames, 8, 2, 8, model_width).transpose(0, 2, 1, 3, 4)
        return shaped.reshape(rows, model_width)

    qkv_rows = qkv_weight.reshape(2, -1, 3 * width)
    out_rows = out_weight.transpose(0, 2, 1)
    down_rows = down_weight.transpose(0, 2, 1)
    first_shard = swap(jnp.concatenate([qkv_rows[0], out_rows[0]], axis=1))
    band_hot = (band_ids[:, None] == jnp.arange(BANDS)[None, :]).astype(low)
    class_hot = (class_ids[:, None] == jnp.arange(CLASSES)[None, :]).astype(low)
    condition = jnp.dot(band_hot, time_table, preferred_element_type=full) + jnp.dot(
        class_hot, class_table, preferred_element_type=full
    )
    activity = jax.nn.silu(condition).astype(low)
    everyone = ("z", "y", "c", "x")
    mod_part = jnp.einsum(
        "cd,bde->cbe", activity, ada_weight, preferred_element_type=full
    ) + ada_bias[None].astype(full)
    mod_part = jnp.broadcast_to(
        mod_part.reshape(8, 1, 2, 2, col_width), (8, 2, 2, 2, col_width)
    ).reshape(32, 2, col_width)
    own_mod = lax.all_to_all(mod_part, everyone, split_axis=0, concat_axis=0, tiled=True)
    own_mod = own_mod.transpose(1, 0, 2).reshape(2, 6, model_width)
    rows_of = lambda *items: jnp.stack([own_mod[k, at] for k, at in items])

    hot = offset_hot()
    wide = 2 * WIN_T - 1
    square = spatial_bias.reshape(heads, 2 * WIN_S - 1, 2 * WIN_S - 1)
    spatial_parts = jnp.stack(
        [
            square[:, 8 * a : 8 * a + wide, 8 * b : 8 * b + wide].reshape(heads, -1)
            for a in range(3)
            for b in range(3)
        ],
        axis=1,
    )
    parts = swap(jnp.concatenate([spatial_parts, joint_bias.reshape(heads, 9, -1)]))
    blocks = jnp.dot(
        parts.reshape(heads * 18, wide * wide), hot.astype(low), preferred_element_type=full
    ).astype(low)
    blocks = blocks.reshape(2, heads, 9, 64, 64)
    near = blocks[0].reshape(heads, 3, 3, 64, 64)
    near = jnp.where(c == 0, near, near[:, ::-1])
    bias_blocks = [near.reshape(heads, 9, 64, 64), blocks[1]]

    windowed = lambda values: values.reshape(2, frames, 2, 64, values.shape[-1])

    chain.wait(own_mod, parts)
    packed = pack_arguments(chain, up_weight, down_rows, qkv_rows, out_rows)
    traded = swap_only(packed)
    gather = Gather(chain, [first_shard] + [None] * 5)
    gather.over_z(0)
    gather.step()
    cuts = [shape_of((64, PIECE))] * 5
    gather.shards[1:] = chain.run(
        "cut_shards",
        cut_kernel,
        [packed, traded],
        [whole(packed)] * 2,
        cuts,
        [whole(a) for a in cuts],
    )
    gather.over_z(1)
    latent_rows = copy_rows(chain, rearranged(latents))
    traded_rows = swap_only(latent_rows)
    gather.step()
    gather.over_z(2)
    chain.wait(*bias_blocks)
    latent_rows, normed_0, inverse_0, moved_0 = first_norm(
        chain, latent_rows, traded_rows, rows_of((0, 0), (0, 1))
    )
    other_0 = flip_rows(moved_0)
    gather.step()
    gather.over_z(3)
    qkv_0, out_0 = gather.place(0, [3 * width, width])
    (joined_0,) = both_times(chain, "plain", moved_0, other_0, qkv_0)
    joined_0 = windowed(joined_0)
    mixed_0, probs_0 = attend(chain, bias_blocks[0], joined_0, False)
    mixed_0 = mixed_0.reshape(2, rows, width)
    away = other_rows(chain, mixed_0, out_0)
    gather.step()
    gather.over_z(4)
    (up_0,) = gather.place(1, [hidden])
    after_0, branch_one_0, normed_1, inverse_1, moved_1 = forward_step(
        chain, mixed_0, out_0, away, latent_rows, rows_of((0, 2), (0, 3), (0, 4)), False
    )
    other_1 = flip_rows(moved_1)
    act_0, slope_0 = both_times(chain, "gelu", moved_1, other_1, up_0)
    gather.step()
    gather.over_z(5)
    (down_0,) = gather.place(2, [hidden])
    away = other_rows(chain, act_0, down_0)
    current_1, branch_two_0, normed_2, inverse_2, moved_2 = forward_step(
        chain, act_0, down_0, away, after_0, rows_of((0, 5), (1, 0), (1, 1)), False
    )
    other_2 = flip_rows(moved_2)

    gather.step()
    qkv_1, out_1 = gather.place(3, [3 * width, width])
    (joined_1,) = both_times(chain, "plain", moved_2, other_2, qkv_1)
    joined_1 = windowed(joined_1)
    mixed_1, probs_1 = attend(chain, bias_blocks[1], joined_1, True)
    mixed_1 = mixed_1.reshape(2, rows, width)
    away = other_rows(chain, mixed_1, out_1)
    gather.step()
    (up_1,) = gather.place(4, [hidden])
    after_1, branch_one_1, normed_3, inverse_3, moved_3 = forward_step(
        chain, mixed_1, out_1, away, current_1, rows_of((1, 2), (1, 3), (1, 4)), False
    )
    other_3 = flip_rows(moved_3)
    act_1, slope_1 = both_times(chain, "gelu", moved_3, other_3, up_1)
    (down_1,) = gather.place(5, [hidden])
    traded_cotangent = swap(copy_rows(chain, rearranged(cotangent)))
    away = other_rows(chain, act_1, down_1)
    final, branch_two_1 = forward_step(
        chain, act_1, down_1, away, after_1, rows_of((1, 5)), True
    )

    def restored(sent):
        shaped = sent.reshape(frames, 2, 8, 8, model_width).transpose(0, 2, 1, 3, 4)
        return shaped.astype(full).reshape(1, frames, 8, 16, model_width)

    traded_final = swap(final)

    exact = lax.Precision.HIGHEST

    state = traded_cotangent
    own_g, sums_a = first_back(chain, state, branch_two_1, rows_of((1, 5)))
    other_g = flip_rows(own_g)
    scatter = Scatter(chain)
    (hidden_g,) = both_times(chain, "slope", own_g, other_g, down_1, slope_1)
    away = other_rows(chain, hidden_g, up_1)
    scatter.weight_grad((own_g, other_g, act_1))
    state, sums_b, own_g = backward_step(
        chain, hidden_g, up_1, away, normed_3, inverse_3, state, rows_of((1, 4), (1, 2)), branch_one_1
    )
    other_g = flip_rows(own_g)
    scatter.weight_grad((moved_3, other_3, hidden_g))
    chain.wait(traded_final)
    scatter.step(6)
    (mixed_g,) = both_times(chain, "plain", own_g, other_g, out_1)
    back, joint_sums = attend_back(chain, joined_1, windowed(mixed_g), probs_1, True)
    back = back.reshape(2, rows, 3 * width)
    away = other_rows(chain, back, qkv_1)
    scatter.weight_grad((moved_2, other_2, back), (own_g, other_g, mixed_1))
    scatter.step(6)
    state, sums_c, own_g = backward_step(
        chain, back, qkv_1, away, normed_2, inverse_2, state, rows_of((1, 1), (0, 5)), branch_two_0
    )
    other_g = flip_rows(own_g)

    (hidden_g,) = both_times(chain, "slope", own_g, other_g, down_0, slope_0)
    away = other_rows(chain, hidden_g, up_0)
    scatter.weight_grad((own_g, other_g, act_0))
    scatter.step(6)
    state, sums_d, own_g = backward_step(
        chain, hidden_g, up_0, away, normed_1, inverse_1, state, rows_of((0, 4), (0, 2)), branch_one_0
    )
    other_g = flip_rows(own_g)
    scatter.weight_grad((moved_1, other_1, hidden_g))
    (mixed_g,) = both_times(chain, "plain", own_g, other_g, out_0)
    scatter.step(6)
    back, spatial_sums = attend_back(chain, joined_0, windowed(mixed_g), probs_0, False)
    back = back.reshape(2, rows, 3 * width)
    away = other_rows(chain, back, qkv_0)
    scatter.weight_grad((moved_0, other_0, back), (own_g, other_g, mixed_0))
    scatter.step(6)
    spatial_tables, joint_tables = bias_tables(chain, [spatial_sums, joint_sums])
    state, sums_e = backward_step(
        chain, back, qkv_0, away, normed_0, inverse_0, state, rows_of((0, 1)), None
    )
    output = restored(traded_final)

    chain.wait(*scatter.held[1:])
    grad_mod = collect_sums(chain, [sums_a, sums_b, sums_c, sums_d, sums_e])
    ordered = grad_mod.reshape(2, 32, col_width).transpose(1, 0, 2)
    cols = lax.all_to_all(ordered, everyone, split_axis=0, concat_axis=0, tiled=True)
    cols = cols.reshape(8, 2, 2, 2, col_width)
    cols = (cols[:, 0] + cols[:, 1]).reshape(16, 2, col_width)
    grad_ada_weight = jnp.einsum("cd,cbe->bde", activity.astype(full), cols, precision=exact)
    grad_ada_bias = jnp.sum(cols, axis=0)
    grad_activity = jnp.einsum("cbe,bde->cd", cols, ada_weight.astype(full), precision=exact)

    near = spatial_tables.reshape(heads, 3, 3, 256)
    near = jnp.where(c == 0, near, near[:, ::-1])
    tables = jnp.concatenate(
        [near.reshape(heads * 9, 256), joint_tables.reshape(heads * 9, 256)]
    )

    shared = jnp.concatenate([grad_activity.reshape(-1, 256), tables])
    chain.wait(cols)
    scatter.step(6)
    scatter.step(6)
    shared, sent = add_all(chain, shared)
    sent = flip(sent, "y")
    traded_state = swap(copy_rows(chain, state))
    (early,) = join_pieces(chain, scatter.done)
    early = swap(early)
    shared, sent = add_all(chain, shared, sent)
    sent = [z_trade(sent, k) for k in (1, 2, 3)]
    chain.wait(traded_state)
    scatter.step(6)
    traded_late = swap_only(scatter.done[5])
    late = jnp.where(c == x, scatter.done[5], traded_late).astype(full)
    chain.wait(early, traded_late)
    shared, sent = add_all(chain, shared, *sent)
    over_x = flip(sent, "x").astype(full)
    over_c = flip(sent, "c").astype(full)
    over_both = lax.ppermute(sent, ("c", "x"), [(0, 3), (1, 2), (2, 1), (3, 0)]).astype(full)
    shared = shared + over_x
    across = over_c + over_both
    grad_activity = (shared + across)[: -heads * 18].reshape(16, model_width)
    tables = jnp.where(c == x, shared[-heads * 18 :], across[-heads * 18 :])
    grad_latents = restored(traded_state)
    done = early.astype(full)
    piece = lambda at: done[:, at * PIECE : (at + 1) * PIECE]
    grad_down = jnp.stack([piece(3).T, piece(0).T])
    grad_up = jnp.stack([piece(4), piece(1)])
    grad_qkv = jnp.stack([late[:, : 3 * width], piece(2)[:, : 3 * width]])
    grad_out = jnp.stack([late[:, 3 * width :].T, piece(2)[:, 3 * width :].T])

    tables = tables.reshape(2, heads, 9, 16, 16)[..., :wide, :wide]
    grad_joint = tables[1].reshape(heads, 9 * wide * wide)
    near = tables[0].reshape(heads, 3, 3, wide, wide)
    long = 2 * WIN_S - 1
    grad_spatial = 0.0
    for a in range(3):
        for b in range(3):
            grad_spatial = grad_spatial + jnp.pad(
                near[:, a, b],
                ((0, 0), (8 * a, long - wide - 8 * a), (8 * b, long - wide - 8 * b)),
            )
    grad_spatial = grad_spatial.reshape(heads, long * long)
    grad_condition = jax.vjp(jax.nn.silu, condition)[1](grad_activity)[0]
    grad_time = jnp.dot(band_hot.astype(full).T, grad_condition, precision=exact)
    grad_class = jnp.dot(class_hot.astype(full).T, grad_condition, precision=exact)

    return (
        output,
        grad_latents,
        grad_time,
        grad_class,
        grad_ada_weight,
        grad_ada_bias,
        grad_qkv.reshape(2, -1, 3, width),
        grad_out,
        grad_up,
        grad_down,
        grad_spatial,
        grad_joint,
    )


def solution(mesh):
    if mesh.shape["dp"] != 16 or mesh.shape["mp"] != 2:
        return solution_any(mesh)
    fine = Mesh(mesh.devices.reshape(4, 2, 2, 2), ("z", "y", "c", "x"))
    dp, mp = ("z", "y", "c"), "x"
    both = dp + (mp,)
    tokens = P(dp, None, mp, None, None)
    weight_specs = (
        P(None, None, both),
        P(None, both),
        P(None, dp, None, mp),
        P(None, mp, dp),
        P(None, dp, mp),
        P(None, mp, dp),
        P(mp, None),
        P(mp, None),
    )
    return jax.shard_map(
        fast_local,
        mesh=fine,
        in_specs=(tokens, tokens, P(dp), P(), P(), P(), P()) + weight_specs,
        out_specs=(tokens, tokens, P(), P()) + weight_specs,
        check_vma=False,
    )
```

```python
import jax
import jax.numpy as jnp
import numpy as np
from jax import lax
from jax.experimental import pallas as pl
from jax.experimental.pallas import tpu as pltpu
from jax.sharding import Mesh
from jax.sharding import PartitionSpec as P

HEAD_DIM = 64
CLASSES = 101
BANDS = 32
FRAMES = 5
WIN_S = 16
WIN_T = 8


epsilon = 1e-06
masked_score = -1e30


def spatial_table():
    places = np.arange(WIN_S * WIN_S)
    row_at = places // WIN_S
    col_at = places % WIN_S
    row_rel = row_at[:, None] - row_at[None, :] + WIN_S - 1
    col_rel = col_at[:, None] - col_at[None, :] + WIN_S - 1
    return (row_rel * (2 * WIN_S - 1) + col_rel).astype(np.int32)


def joint_table():
    places = np.arange(FRAMES * WIN_T * WIN_T)
    time_at = places // (WIN_T * WIN_T)
    row_at = places // WIN_T % WIN_T
    col_at = places % WIN_T
    time_rel = time_at[:, None] - time_at[None, :] + FRAMES - 1
    row_rel = row_at[:, None] - row_at[None, :] + WIN_T - 1
    col_rel = col_at[:, None] - col_at[None, :] + WIN_T - 1
    return ((time_rel * (2 * WIN_T - 1) + row_rel) * (2 * WIN_T - 1) + col_rel).astype(np.int32)


def to_windows(values, window, is_joint):
    clip_count, frames, side_cells, channels = (
        values.shape[0],
        values.shape[1],
        values.shape[2],
        values.shape[4],
    )
    per_side = side_cells // window
    if is_joint:
        shaped = values.reshape(clip_count, frames, per_side, window, per_side, window, channels)
        shaped = shaped.transpose(0, 2, 4, 1, 3, 5, 6)
        return shaped.reshape(clip_count * per_side * per_side, frames * window * window, channels)
    shaped = values.reshape(clip_count, frames, per_side, window, per_side, window, channels)
    shaped = shaped.transpose(0, 1, 2, 4, 3, 5, 6)
    return shaped.reshape(clip_count * frames * per_side * per_side, window * window, channels)


def from_windows(values, clip_count, frames, side_cells, window, is_joint):
    per_side = side_cells // window
    channels = values.shape[-1]
    if is_joint:
        shaped = values.reshape(clip_count, per_side, per_side, frames, window, window, channels)
        shaped = shaped.transpose(0, 3, 1, 4, 2, 5, 6)
    else:
        shaped = values.reshape(clip_count, frames, per_side, per_side, window, window, channels)
        shaped = shaped.transpose(0, 1, 2, 4, 3, 5, 6)
    return shaped.reshape(clip_count, frames, side_cells, side_cells, channels)


def normalize(values):
    center = values - jnp.mean(values, axis=-1, keepdims=True)
    spread = jnp.mean(center * center, axis=-1, keepdims=True)
    inverse = lax.rsqrt(spread + epsilon)
    return (center * inverse, inverse)


def norm_back(grad_normed, normed, inverse):
    first_mean = jnp.mean(grad_normed, axis=-1, keepdims=True)
    second_mean = jnp.mean(grad_normed * normed, axis=-1, keepdims=True)
    return inverse * (grad_normed - first_mean - normed * second_mean)


def exact_gelu(values):
    return jax.nn.gelu(values, approximate=False)


def gather_rows(values):
    return lax.all_gather(values, "mp", axis=2, tiled=True)


def sum_rows(values):
    return lax.psum_scatter(
        values.astype(jnp.bfloat16), "mp", scatter_dimension=2, tiled=True
    ).astype(jnp.float32)


def gather_grads(values):
    return lax.all_gather(values, "mp", axis=2, tiled=True)


def input_sums(values):
    return lax.psum_scatter(
        values.astype(jnp.bfloat16), "mp", scatter_dimension=2, tiled=True
    ).astype(jnp.float32)


def inputs_again(moved):
    return lax.all_gather(moved, "mp", axis=2, tiled=True)


def attention_scores(query_part, key_part, bias_matrix, key_valid):
    scores = (
        jnp.einsum("nqhe,nkhe->nhqk", query_part, key_part, preferred_element_type=jnp.float32)
        * HEAD_DIM ** (-0.5)
        + bias_matrix[None]
    )
    if key_valid is not None:
        scores = jnp.where(key_valid[:, None, None, :] > 0, scores, masked_score)
    return scores


def local(
    latents,
    cotangent,
    frame_counts,
    band_ids,
    class_ids,
    time_table,
    class_table,
    ada_weight,
    ada_bias,
    qkv_weight,
    out_weight,
    up_weight,
    down_weight,
    spatial_bias,
    joint_bias,
):
    clip_count = latents.shape[0]
    frames = latents.shape[1]
    side_cells = latents.shape[3]
    model_width = latents.shape[4]
    heads_local = spatial_bias.shape[0]
    local_width = heads_local * HEAD_DIM
    dp_count = lax.axis_size("dp")
    mp_count = lax.axis_size("mp")
    col_width = ada_weight.shape[2]
    band_hot = (band_ids[:, None] == jnp.arange(BANDS)[None, :]).astype(jnp.bfloat16)
    class_hot = (class_ids[:, None] == jnp.arange(CLASSES)[None, :]).astype(jnp.bfloat16)
    condition = jnp.dot(band_hot, time_table, preferred_element_type=jnp.float32) + jnp.dot(
        class_hot, class_table, preferred_element_type=jnp.float32
    )
    activity_low = jax.nn.silu(condition).astype(jnp.bfloat16)
    ada_cols, ada_bias_cols = (
        lax.all_gather(ada_weight, "mp", axis=2, tiled=True),
        lax.all_gather(ada_bias, "mp", axis=1, tiled=True),
    )
    mod_part = jnp.einsum(
        "cd,bde->bce", activity_low, ada_cols, preferred_element_type=jnp.float32
    ) + ada_bias_cols[:, None, :].astype(jnp.float32)
    modulation = lax.all_gather(mod_part, "dp", axis=2, tiled=True)
    first_clip = lax.axis_index("dp") * clip_count
    own_mod = lax.dynamic_slice_in_dim(modulation, first_clip, clip_count, 1).reshape(
        2, clip_count, 6, model_width
    )
    frame_valid = (jnp.arange(frames)[None, :] < frame_counts[:, None]).astype(jnp.float32)
    frame_mask = frame_valid[:, :, None, None, None]
    key_frames = np.arange(frames * WIN_T * WIN_T) // (WIN_T * WIN_T)
    joint_cells = key_frames.shape[0]
    per_side = side_cells // WIN_T
    key_valid = frame_valid[:, key_frames]
    key_valid = jnp.broadcast_to(
        key_valid[:, None, :], (clip_count, per_side * per_side, joint_cells)
    ).reshape(clip_count * per_side * per_side, joint_cells)
    w_qkv, w_out, w_up, w_down = (
        lax.all_gather(qkv_weight, "dp", axis=1, tiled=True),
        lax.all_gather(out_weight, "dp", axis=2, tiled=True),
        lax.all_gather(up_weight, "dp", axis=1, tiled=True),
        lax.all_gather(down_weight, "dp", axis=2, tiled=True),
    )
    spatial_index = spatial_table()
    joint_index = joint_table()
    spatial_matrix = spatial_bias.astype(jnp.float32)[:, spatial_index]
    joint_matrix = joint_bias.astype(jnp.float32)[:, joint_index]
    current = latents.astype(jnp.float32)
    stored = []
    for which_block in range(2):
        is_joint = which_block == 1
        window = WIN_T if is_joint else WIN_S
        bias_matrix = joint_matrix if is_joint else spatial_matrix
        mask_keys = key_valid if is_joint else None
        block_mod = own_mod[which_block][:, :, None, None, None, :]
        normed_one, inverse_one = normalize(current)
        moved_one = (normed_one * (1.0 + block_mod[:, 1]) + block_mod[:, 0]).astype(jnp.bfloat16)
        gathered_one = gather_rows(moved_one)
        projected = jnp.einsum(
            "cfyxd,dkh->cfyxkh",
            gathered_one,
            w_qkv[which_block],
            preferred_element_type=jnp.float32,
        ).astype(jnp.bfloat16)
        windows = to_windows(
            projected.reshape(clip_count, frames, side_cells, side_cells, 3 * local_width),
            window,
            is_joint,
        )
        windows = windows.reshape(windows.shape[0], windows.shape[1], 3, heads_local, HEAD_DIM)
        scores = attention_scores(windows[:, :, 0], windows[:, :, 1], bias_matrix, mask_keys)
        row_max = jnp.max(scores, axis=-1, keepdims=True)
        log_total = row_max + jnp.log(jnp.sum(jnp.exp(scores - row_max), axis=-1, keepdims=True))
        probs_low = jnp.exp(scores - log_total).astype(jnp.bfloat16)
        mixed_win = jnp.einsum(
            "nhqk,nkhe->nqhe", probs_low, windows[:, :, 2], preferred_element_type=jnp.float32
        ).astype(jnp.bfloat16)
        mixed_rows = from_windows(
            mixed_win.reshape(mixed_win.shape[0], mixed_win.shape[1], local_width),
            clip_count,
            frames,
            side_cells,
            window,
            is_joint,
        )
        branch_one = sum_rows(
            jnp.einsum(
                "cfyxk,kd->cfyxd",
                mixed_rows,
                w_out[which_block],
                preferred_element_type=jnp.float32,
            )
        )
        after_attn = current + frame_mask * block_mod[:, 2] * branch_one
        normed_two, inverse_two = normalize(after_attn)
        moved_two = (normed_two * (1.0 + block_mod[:, 4]) + block_mod[:, 3]).astype(jnp.bfloat16)
        gathered_two = gather_rows(moved_two)
        hidden = jnp.einsum(
            "cfyxd,dk->cfyxk", gathered_two, w_up[which_block], preferred_element_type=jnp.float32
        )
        activated = exact_gelu(hidden).astype(jnp.bfloat16)
        branch_two = sum_rows(
            jnp.einsum(
                "cfyxk,kd->cfyxd",
                activated,
                w_down[which_block],
                preferred_element_type=jnp.float32,
            )
        )
        current = after_attn + frame_mask * block_mod[:, 5] * branch_two
        stored.append(
            (
                normed_one,
                inverse_one,
                moved_one,
                gathered_one,
                windows,
                log_total,
                mixed_rows,
                branch_one,
                normed_two,
                inverse_two,
                moved_two,
                gathered_two,
                hidden,
                activated,
                branch_two,
            )
        )
    grad_state = cotangent.astype(jnp.float32)
    mod_grads = []
    qkv_grads = []
    out_grads = []
    up_grads = []
    down_grads = []
    table_parts = []
    for which_block in (1, 0):
        is_joint = which_block == 1
        window = WIN_T if is_joint else WIN_S
        bias_matrix = joint_matrix if is_joint else spatial_matrix
        mask_keys = key_valid if is_joint else None
        block_mod = own_mod[which_block][:, :, None, None, None, :]
        (
            normed_one,
            inverse_one,
            moved_one,
            gathered_one,
            windows,
            log_total,
            mixed_rows,
            branch_one,
            normed_two,
            inverse_two,
            moved_two,
            gathered_two,
            hidden,
            activated,
            branch_two,
        ) = stored[which_block]
        grad_gate_two = jnp.sum(frame_mask * grad_state * branch_two, axis=(1, 2, 3))
        grad_rows = gather_grads((frame_mask * block_mod[:, 5] * grad_state).astype(jnp.bfloat16))
        down_grads.append(
            jnp.einsum("cfyxk,cfyxd->kd", activated, grad_rows, preferred_element_type=jnp.float32)
        )
        grad_act = jnp.einsum(
            "cfyxd,kd->cfyxk", grad_rows, w_down[which_block], preferred_element_type=jnp.float32
        )
        grad_hidden = jax.vjp(exact_gelu, hidden)[1](grad_act)[0].astype(jnp.bfloat16)
        inputs_two = inputs_again(moved_two)
        up_grads.append(
            jnp.einsum(
                "cfyxd,cfyxk->dk", inputs_two, grad_hidden, preferred_element_type=jnp.float32
            )
        )
        grad_moved = input_sums(
            jnp.einsum(
                "cfyxk,dk->cfyxd",
                grad_hidden,
                w_up[which_block],
                preferred_element_type=jnp.float32,
            )
        )
        grad_shift_two = jnp.sum(grad_moved, axis=(1, 2, 3))
        grad_scale_two = jnp.sum(grad_moved * normed_two, axis=(1, 2, 3))
        grad_state = grad_state + norm_back(
            grad_moved * (1.0 + block_mod[:, 4]), normed_two, inverse_two
        )
        grad_gate_one = jnp.sum(frame_mask * grad_state * branch_one, axis=(1, 2, 3))
        grad_rows = gather_grads((frame_mask * block_mod[:, 2] * grad_state).astype(jnp.bfloat16))
        out_grads.append(
            jnp.einsum("cfyxk,cfyxd->kd", mixed_rows, grad_rows, preferred_element_type=jnp.float32)
        )
        grad_mixed = jnp.einsum(
            "cfyxd,kd->cfyxk", grad_rows, w_out[which_block], preferred_element_type=jnp.float32
        ).astype(jnp.bfloat16)
        grad_win = to_windows(grad_mixed, window, is_joint)
        grad_win = grad_win.reshape(grad_win.shape[0], grad_win.shape[1], heads_local, HEAD_DIM)
        query_part = windows[:, :, 0]
        key_part = windows[:, :, 1]
        value_part = windows[:, :, 2]
        probs_full = jnp.exp(
            attention_scores(query_part, key_part, bias_matrix, mask_keys) - log_total
        )
        grad_value = jnp.einsum(
            "nhqk,nqhe->nkhe",
            probs_full.astype(jnp.bfloat16),
            grad_win,
            preferred_element_type=jnp.float32,
        ).astype(jnp.bfloat16)
        grad_probs = jnp.einsum(
            "nqhe,nkhe->nhqk", grad_win, value_part, preferred_element_type=jnp.float32
        )
        row_dot = jnp.sum(probs_full * grad_probs, axis=-1, keepdims=True)
        grad_scores = (probs_full * (grad_probs - row_dot)).astype(jnp.bfloat16)
        bias_sum = jnp.sum(grad_scores.astype(jnp.float32), axis=0)
        if is_joint:
            table_parts.append(
                jnp.zeros((heads_local, joint_bias.shape[1]), jnp.float32)
                .at[:, joint_index]
                .add(bias_sum)
            )
        else:
            table_parts.append(
                jnp.zeros((heads_local, spatial_bias.shape[1]), jnp.float32)
                .at[:, spatial_index]
                .add(bias_sum)
            )
        grad_query = (
            jnp.einsum("nhqk,nkhe->nqhe", grad_scores, key_part, preferred_element_type=jnp.float32)
            * HEAD_DIM ** (-0.5)
        ).astype(jnp.bfloat16)
        grad_key = (
            jnp.einsum(
                "nhqk,nqhe->nkhe", grad_scores, query_part, preferred_element_type=jnp.float32
            )
            * HEAD_DIM ** (-0.5)
        ).astype(jnp.bfloat16)
        stacked = jnp.stack([grad_query, grad_key, grad_value], axis=2).reshape(
            grad_query.shape[0], grad_query.shape[1], 3 * local_width
        )
        grad_projected = from_windows(
            stacked, clip_count, frames, side_cells, window, is_joint
        ).reshape(clip_count, frames, side_cells, side_cells, 3, local_width)
        inputs_one = inputs_again(moved_one)
        qkv_grads.append(
            jnp.einsum(
                "cfyxd,cfyxkh->dkh", inputs_one, grad_projected, preferred_element_type=jnp.float32
            )
        )
        grad_moved = input_sums(
            jnp.einsum(
                "cfyxkh,dkh->cfyxd",
                grad_projected,
                w_qkv[which_block],
                preferred_element_type=jnp.float32,
            )
        )
        grad_shift_one = jnp.sum(grad_moved, axis=(1, 2, 3))
        grad_scale_one = jnp.sum(grad_moved * normed_one, axis=(1, 2, 3))
        grad_state = grad_state + norm_back(
            grad_moved * (1.0 + block_mod[:, 1]), normed_one, inverse_one
        )
        mod_grads.append(
            jnp.stack(
                [
                    grad_shift_one,
                    grad_scale_one,
                    grad_gate_one,
                    grad_shift_two,
                    grad_scale_two,
                    grad_gate_two,
                ],
                axis=1,
            )
        )
    grad_mod = jnp.stack(mod_grads[::-1], axis=0).reshape(2, clip_count, 6 * model_width)
    ordered = (
        grad_mod.reshape(2, clip_count, dp_count, mp_count, col_width)
        .transpose(0, 1, 3, 2, 4)
        .reshape(2, clip_count, 6 * model_width)
    )
    summed_cols = lax.psum_scatter(ordered, "mp", scatter_dimension=2, tiled=True)
    grad_mod_cols = lax.all_to_all(summed_cols, "dp", split_axis=2, concat_axis=1, tiled=True)
    grad_ada_weight = jnp.einsum(
        "cd,bce->bde",
        activity_low.astype(jnp.float32),
        grad_mod_cols,
        precision=lax.Precision.HIGHEST,
    )
    grad_ada_bias = jnp.sum(grad_mod_cols, axis=1)
    grad_mod_block = lax.all_gather(grad_mod_cols, "mp", axis=2, tiled=True)
    activity_part = jnp.einsum(
        "bce,bde->cd", grad_mod_block, ada_cols.astype(jnp.float32), precision=lax.Precision.HIGHEST
    )
    grad_activity = lax.psum(activity_part, "dp")
    grad_condition = jax.vjp(jax.nn.silu, condition)[1](grad_activity)[0]
    grad_time = jnp.dot(
        band_hot.astype(jnp.float32).T, grad_condition, precision=lax.Precision.HIGHEST
    )
    grad_class = jnp.dot(
        class_hot.astype(jnp.float32).T, grad_condition, precision=lax.Precision.HIGHEST
    )
    grad_spatial, grad_joint = lax.psum((table_parts[1], table_parts[0]), "dp")
    grad_qkv, grad_out, grad_up, grad_down = (
        lax.psum_scatter(jnp.stack(qkv_grads[::-1], axis=0), "dp", scatter_dimension=1, tiled=True),
        lax.psum_scatter(jnp.stack(out_grads[::-1], axis=0), "dp", scatter_dimension=2, tiled=True),
        lax.psum_scatter(jnp.stack(up_grads[::-1], axis=0), "dp", scatter_dimension=1, tiled=True),
        lax.psum_scatter(
            jnp.stack(down_grads[::-1], axis=0), "dp", scatter_dimension=2, tiled=True
        ),
    )
    return (
        current,
        grad_state,
        grad_time,
        grad_class,
        grad_ada_weight,
        grad_ada_bias,
        grad_qkv,
        grad_out,
        grad_up,
        grad_down,
        grad_spatial,
        grad_joint,
    )


def solution_any(mesh):
    placed = (
        P("dp", None, "mp", None, None),
        P("dp", None, "mp", None, None),
        P("dp"),
        P(),
        P(),
        P(),
        P(),
        P(None, None, ("dp", "mp")),
        P(None, ("dp", "mp")),
        P(None, "dp", None, "mp"),
        P(None, "mp", "dp"),
        P(None, "dp", "mp"),
        P(None, "mp", "dp"),
        P("mp", None),
        P("mp", None),
    )
    return jax.shard_map(
        local,
        mesh=mesh,
        in_specs=placed,
        out_specs=(
            P("dp", None, "mp", None, None),
            P("dp", None, "mp", None, None),
            P(),
            P(),
            P(None, None, ("dp", "mp")),
            P(None, ("dp", "mp")),
            P(None, "dp", None, "mp"),
            P(None, "mp", "dp"),
            P(None, "dp", "mp"),
            P(None, "mp", "dp"),
            P("mp", None),
            P("mp", None),
        ),
        check_vma=False,
    )


low = jnp.bfloat16
full = jnp.float32
HALF_ROOT = 0.7071067811865476
PHI_AT_ZERO = 0.3989422804014327
MIB = 1024 * 1024


def flip(values, axis):
    return lax.ppermute(values, axis, [(0, 1), (1, 0)])


def z_trade(values, step):
    return lax.ppermute(values, "z", [(place, place ^ step) for place in range(4)])


def swap_only(values):
    return lax.ppermute(values, ("c", "x"), [(1, 2), (2, 1)])


def swap(values):
    return jnp.where(lax.axis_index("c") == lax.axis_index("x"), values, swap_only(values))


def shape_of(dims, dtype=low):
    return jax.ShapeDtypeStruct(tuple(dims), dtype)


def whole(array):
    zeros = (0,) * len(array.shape)
    return pl.BlockSpec(tuple(array.shape), lambda *at: zeros)


def whole_once(array):
    zeros = (0,) * len(array.shape)
    return pl.BlockSpec(
        tuple(array.shape), lambda *at: zeros, pipeline_mode=pl.Buffered(1)
    )


def space_of(dims, dtype):
    dims = [1] * (2 - len(dims)) + list(dims)
    size = jnp.dtype(dtype).itemsize
    rows = 32 // size
    dims[-1] = -(-dims[-1] // 128) * 128
    dims[-2] = -(-dims[-2] // rows) * rows
    return int(np.prod(dims)) * size


def room_for(specs, arrays, scratch):
    total = 0
    for spec, array in zip(specs, arrays):
        if spec.block_shape is not None:
            once = spec.pipeline_mode is not None
            total += space_of(spec.block_shape, array.dtype) * (1 if once else 2)
    return total + sum(space_of(held.shape, held.dtype) for held in scratch)


class Chain:
    def __init__(self, info):
        self.info = info
        self.last = []
        self.pending = []

    def wait(self, *values):
        self.pending += values

    def run(self, name, kernel, args, in_specs, outs, out_specs, grid=(1,), scratch=(), extra=3, waits=()):
        count = len(args)
        unread = self.last + self.pending + list(waits)
        self.pending = []
        held = len(unread)

        limit = room_for(list(in_specs) + list(out_specs), list(args) + list(outs), scratch)

        def body(*refs):
            kernel(*refs[: 1 + count], *refs[1 + count + held :])

        results = pl.pallas_call(
            body,
            grid_spec=pltpu.PrefetchScalarGridSpec(
                num_scalar_prefetch=1,
                grid=grid,
                in_specs=list(in_specs) + [pl.BlockSpec(memory_space=pl.ANY)] * held,
                out_specs=list(out_specs),
                scratch_shapes=list(scratch),
            ),
            out_shape=list(outs),
            compiler_params=pltpu.CompilerParams(vmem_limit_bytes=limit + extra * MIB),
            cost_estimate=pl.CostEstimate(flops=1, bytes_accessed=1, transcendentals=0),
            name=name,
        )(self.info, *args, *unread)
        self.last = [results[0]]
        return results


def pack_arguments(chain, up, down, qkv, out):
    def kernel(info, up_in, down_in, qkv_in, out_in, packed):
        start = 0
        for part in (up_in[0], down_in[0], qkv_in[1], out_in[1], up_in[1], down_in[1]):
            packed[:, start : start + part.shape[1]] = part
            start += part.shape[1]

    args = [up, down, qkv, out]
    result = shape_of((up.shape[1], 5 * PIECE))
    (packed,) = chain.run(
        "pack_arguments", kernel, args, [whole(v) for v in args], [result], [whole(result)]
    )
    return packed


def copy_rows(chain, values):
    def kernel(info, source, result):
        result[...] = source[...]

    spec = pl.BlockSpec((ROW_TILE, values.shape[1]), lambda i, info: (i, 0))
    (result,) = chain.run(
        "copy_rows", kernel, [values], [spec], [shape_of(values.shape)], [spec], grid=(2,)
    )
    return result


def cut_kernel(info, packed, traded, *outs):
    start = 0
    for out in outs:
        width = out.shape[1]
        cols = slice(start, start + width)

        @pl.when(info[4] == 1)
        def _():
            out[...] = packed[:, cols]

        @pl.when(info[4] == 0)
        def _():
            out[...] = traded[:, cols]

        start += width


PIECE = 2048
PIECE_TILE = 512


def tile_spec(count, rows=64):
    return pl.BlockSpec((count, rows, PIECE_TILE), lambda j, info: (0, 0, j))


def flat_spec(rows=64):
    return pl.BlockSpec((rows, PIECE_TILE), lambda j, info: (0, j))


class Gather:
    def __init__(self, chain, shards):
        self.chain = chain
        self.shards = shards
        self.near = {}
        self.sent = {}
        self.got = {}
        self.step_at = 0

    def over_z(self, at):
        self.near[at] = [z_trade(self.shards[at], k) for k in (1, 2, 3)]

    def step(self):
        at = self.step_at
        self.step_at += 1
        own = at < len(self.shards)
        far = at > 0
        args, specs = [], []
        if own:
            args += [self.shards[at]] + self.near[at]
            specs += [flat_spec()] * 4
        start = 0
        if far:
            got_x, got_y = self.got[at - 1]
            start = (got_x.shape[0] - 4) // 2
            args += [got_x, got_y]
            specs += [
                pl.BlockSpec((2, 64, PIECE_TILE), lambda j, info: (start + 1, 0, j)),
                pl.BlockSpec((2, 64, PIECE_TILE), lambda j, info: (start, 0, j)),
            ]

        def kernel(info, *refs):
            to_x, to_y = refs[-2:]
            if own:
                for k in range(4):
                    to_x[(2 if far else 0) + k] = refs[k][...]
                    to_y[(2 if far else 0) + k] = refs[k][...]
            if far:
                from_x, from_y = refs[-4:-2]
                to_x[0:2] = from_y[...]
                to_y[0:2] = from_x[...]

        count = (2 if far else 0) + (4 if own else 0)
        outs = [shape_of((count, 64, PIECE))] * 2
        to_x, to_y = self.chain.run(
            "gather_step",
            kernel,
            args,
            specs,
            outs,
            [tile_spec(count)] * 2,
            grid=(PIECE // PIECE_TILE,),
        )
        self.sent[at] = to_x
        self.got[at] = (flip(to_x, "x"), flip(to_y, "y"))

    def place(self, at, widths):
        def kernel(info, own, from_x, from_y, far_lo, far_hi, *outs):
            k = pl.program_id(0)
            place = info[1] * 2 + info[2]

            def put(rel, block):
                start = 0
                for out in outs:
                    width = out.shape[3]
                    out[0, place ^ rel] = block[0, :, start : start + width]
                    start += width

            put(0, own)
            put(1, from_x)
            put(2, from_y)

            @pl.when(k < 2)
            def _():
                put(3, far_lo)

            @pl.when(k >= 2)
            def _():
                put(3, far_hi)

        got_x, got_y = self.got[at]
        start = got_x.shape[0] - 4
        block = (1, 64, PIECE)
        quad = pl.BlockSpec(block, lambda k, info: (k + start, 0, 0))
        results = self.chain.run(
            "place_weights",
            kernel,
            [self.sent[at], got_x, got_y, *self.got[at + 1]],
            [
                quad,
                quad,
                quad,
                pl.BlockSpec(block, lambda k, info: (jnp.minimum(k, 1), 0, 0)),
                pl.BlockSpec(block, lambda k, info: (jnp.maximum(k - 2, 0), 0, 0)),
            ],
            [shape_of((4, 4, 64, w)) for w in widths],
            [pl.BlockSpec((1, 4, 64, w), lambda k, info: (info[0] ^ k, 0, 0, 0)) for w in widths],
            grid=(4,),
        )
        return [a.reshape(16 * 64, a.shape[3]) for a in results]


GRAD_TILE = 512


def weight_grad_kernel(info, *refs, pairs, tiles):
    lhs = refs[: 4 * pairs]
    rhs = refs[4 * pairs : 5 * pairs]
    near, to_x, to_y, far_lo, far_hi = refs[5 * pairs : 5 * pairs + 5]
    held = refs[5 * pairs + 5]
    across = refs[5 * pairs + 6 :]
    j = pl.program_id(0)
    place = info[1] * 2 + info[2]
    begin = 0
    for at in range(pairs):

        @pl.when(j == begin)
        def _():
            for part in range(4):
                cols = slice(part * ROW_TILE, (part + 1) * ROW_TILE)
                across[at][:, cols] = lhs[4 * at + part][...].T

        @pl.when((j >= begin) & (j < begin + tiles[at]))
        def _():
            tokens = rhs[at][...].reshape(4 * ROW_TILE, GRAD_TILE)
            for rows in range(0, held.shape[0], 256):
                block = jnp.dot(
                    across[at][rows : rows + 256], tokens, preferred_element_type=full
                )
                held[rows : rows + 256] = block.astype(low)

        begin += tiles[at]

    def part(z, rel):
        return held[pl.ds(pl.multiple_of(z * 256 + (place ^ rel) * 64, 64), 64), :]

    for z in range(4):
        near[z] = part(z, 0)
        to_x[z] = part(z, 1)
        to_y[z] = part(z, 2)
        if z < 2:
            far_lo[z] = part(z, 3)
        else:
            far_hi[z - 2] = part(z, 3)


class Scatter:
    def __init__(self, chain):
        self.chain = chain
        self.parts = []
        self.got = None
        self.held = None
        self.done = []
        self.step_at = 0

    def weight_grad(self, *items):
        pairs = len(items)
        widths = tuple(item[2].shape[2] for item in items)
        rows, features = items[0][0][0].shape
        tiles = [w // GRAD_TILE for w in widths]
        quads = shape_of((4, 64, PIECE))
        twos = shape_of((2, 64, PIECE))

        def rhs_spec(at):
            first, last = sum(tiles[:at]), tiles[at] - 1
            return pl.BlockSpec(
                (2, 2 * rows, GRAD_TILE),
                lambda j, info: (0, 0, jnp.clip(j - first, 0, last)),
            )

        quad_spec = pl.BlockSpec((4, 64, GRAD_TILE), lambda j, info: (0, 0, j))
        two_spec = pl.BlockSpec((2, 64, GRAD_TILE), lambda j, info: (0, 0, j))
        lhs = [part for item in items for pair in item[:2] for part in pair]
        self.parts.append(
            self.chain.run(
                "weight_grad",
                lambda *refs: weight_grad_kernel(*refs, pairs=pairs, tiles=tiles),
                lhs + [item[2] for item in items],
                [whole_once(v) for v in lhs] + [rhs_spec(at) for at in range(pairs)],
                [quads, quads, quads, twos, twos],
                [quad_spec] * 3 + [two_spec] * 2,
                grid=(PIECE // GRAD_TILE,),
                scratch=[pltpu.VMEM((features, GRAD_TILE), low)]
                + [pltpu.VMEM((features, 4 * rows), low)] * pairs,
                extra=3,
            )
        )
        if len(self.parts) == 1:
            self.got = (flip(self.parts[0][3], "x"), flip(self.parts[0][4], "y"))

    def step(self, total):
        at = self.step_at
        self.step_at += 1
        far = at + 1 < total
        mid = at < total
        near = 0 <= at - 1 < total
        last = 0 <= at - 2 < total
        args, specs = [], []

        def put(array, spec):
            args.append(array)
            specs.append(spec)
            return len(args) - 1

        names = {}
        if far:
            names["far_lo"] = put(self.parts[at + 1][3], tile_spec(2))
            names["far_hi"] = put(self.parts[at + 1][4], tile_spec(2))
        if mid:
            names["to_x"] = put(self.parts[at][1], tile_spec(4))
            names["to_y"] = put(self.parts[at][2], tile_spec(4))
        if near:
            names["near"] = put(self.parts[at - 1][0], tile_spec(4))
        if mid or near:
            count = self.got[0].shape[0]
            names["got_x"] = put(self.got[0], tile_spec(count))
            names["got_y"] = put(self.got[1], tile_spec(count))
        if last:
            for k in range(4):
                names["held%d" % k] = put(self.held[k], flat_spec())
        outs, out_specs = [], []
        sent = (2 if far else 0) + (4 if mid else 0)
        if mid:
            outs += [shape_of((sent, 64, PIECE))] * 2
            out_specs += [tile_spec(sent)] * 2
        if near:
            outs += [shape_of((64, PIECE), full)] + [shape_of((64, PIECE))] * 3
            out_specs += [flat_spec()] * 4
        if last:
            outs.append(shape_of((64, PIECE)))
            out_specs.append(flat_spec())
        number = len(args)

        def kernel(info, *refs):
            out = list(refs[number:])
            get = {name: refs[spot] for name, spot in names.items()}
            if mid:
                out_x, out_y = out[:2]
                del out[:2]
                start = 0
                if far:
                    out_x[0:2] = get["far_lo"][...]
                    out_y[0:2] = get["far_hi"][...]
                    start = 2
                for k in range(4):
                    part_x = get["to_x"][k]
                    part_y = get["to_y"][k]
                    if k < 2:
                        part_y = (part_y.astype(full) + get["got_x"][k].astype(full)).astype(low)
                    else:
                        part_x = (
                            part_x.astype(full) + get["got_y"][k - 2].astype(full)
                        ).astype(low)
                    out_x[start + k] = part_x
                    out_y[start + k] = part_y
            if near:
                start = get["got_x"].shape[0] - 4
                for k in range(4):
                    spot = info[0] ^ k
                    value = get["near"][spot].astype(full)
                    value = value + get["got_x"][start + spot].astype(full)
                    value = value + get["got_y"][start + spot].astype(full)
                    out[k][...] = value.astype(out[k].dtype)
                del out[:4]
            if last:
                value = get["held0"][...]
                for k in (1, 2, 3):
                    value = value + get["held%d" % k][...].astype(full)
                out[0][...] = value.astype(low)

        results = list(
            self.chain.run(
                "scatter_step", kernel, args, specs, outs, out_specs, grid=(PIECE // PIECE_TILE,)
            )
        )
        if mid:
            self.got = (flip(results[0], "x"), flip(results[1], "y"))
            del results[:2]
        if near:
            self.held = [results[0]] + [z_trade(results[k], k) for k in (1, 2, 3)]
            del results[:4]
        if last:
            self.done.append(results[0])


def offset_columns():
    cells = np.arange(WIN_T * WIN_T)
    spots = 119 - (cells // WIN_T * 16 + cells % WIN_T)
    hot = (spots[:, None] == np.arange(256)[None, :]).astype(np.float32)
    return jnp.asarray(np.concatenate([hot] * 3), low)


def bias_tables(chain, sums):
    heads, sides = sums[0].shape[:2]

    def kernel(info, *refs):
        hot = refs[len(sums)][...]
        for at, out in enumerate(refs[len(sums) + 1 :]):
            for h in range(heads):
                values = refs[at][h].reshape(sides * 64, 64)
                first = values.astype(low)
                rest = values - first.astype(full)
                second = rest.astype(low)
                third = (rest - second.astype(full)).astype(low)
                parts = jnp.concatenate([first, second, third], axis=1)
                spread = jnp.dot(parts, hot, preferred_element_type=full)
                spread = spread.reshape(sides, 8, 8, 256)
                by_row = spread[:, 0]
                for row in range(1, 8):
                    by_row = by_row + pltpu.roll(spread[:, row], 16 * row, 2)
                total = by_row[:, 0]
                for col in range(1, 8):
                    total = total + pltpu.roll(by_row[:, col], col, 1)
                out[h] = total

    hot = offset_columns()
    args = list(sums) + [hot]
    outs = [shape_of((heads, sides, 256), full)] * len(sums)
    return chain.run(
        "bias_tables", kernel, args, [whole(v) for v in args], outs, [whole(v) for v in outs], extra=8
    )


def collect_sums(chain, sums):
    spots = [(4, 0), (4, 1), (3, 2), (3, 0), (3, 1), (2, 2), (2, 0), (2, 1), (1, 2), (1, 0), (1, 1), (0, 0)]

    def kernel(info, *refs):
        for row, (at, spot) in enumerate(spots):
            refs[-1][row : row + 1] = refs[at][spot : spot + 1]

    out = shape_of((len(spots), sums[0].shape[1]), full)
    (result,) = chain.run(
        "collect_sums", kernel, list(sums), [whole(v) for v in sums], [out], [whole(out)]
    )
    return result


def add_all(chain, *values):
    def kernel(info, *refs):
        total = refs[0][...]
        for other in refs[1:-2]:
            total = total + other[...].astype(full)
        refs[-2][...] = total
        refs[-1][...] = total.astype(low)

    outs = [shape_of(values[0].shape, full), shape_of(values[0].shape)]
    return chain.run(
        "add_all",
        kernel,
        list(values),
        [whole(v) for v in values],
        outs,
        [whole(v) for v in outs],
    )


def join_pieces(chain, pieces, *copied):
    count = len(pieces)

    def kernel(info, *refs):
        out = refs[count + len(copied)]
        for at in range(count):
            out[:, at * PIECE : (at + 1) * PIECE] = refs[at][...]
        for at in range(len(copied)):
            refs[count + len(copied) + 1 + at][...] = refs[count + at][...]

    args = list(pieces) + list(copied)
    outs = [shape_of((64, PIECE * count))] + [shape_of(v.shape) for v in copied]
    return chain.run(
        "join_pieces", kernel, args, [whole(v) for v in args], outs, [whole(v) for v in outs]
    )


def gelu_and_slope(values):
    bell = jnp.exp(-0.5 * values * values)
    t = 1.0 / (1.0 + (0.3275911 * HALF_ROOT) * jnp.abs(values))
    poly = t * (
        0.254829592
        + t * (-0.284496736 + t * (1.421413741 + t * (-1.453152027 + t * 1.061405429)))
    )
    tail = 0.5 * poly * bell
    phi = jnp.where(values >= 0, 1.0 - tail, tail)
    return values * phi, phi + (PHI_AT_ZERO * values) * bell


ROW_TILE = 320


def flip_rows(pair):
    return tuple(flip(part, "c") for part in pair)


def both_kernel(info, *refs, kind):
    weight = refs[4][...]
    for part in range(4):
        half = part // 2
        rows = slice(part % 2 * ROW_TILE, (part % 2 + 1) * ROW_TILE)
        product = jnp.dot(refs[part][...], weight, preferred_element_type=full)
        if kind == "gelu":
            act, slope = gelu_and_slope(product)
            refs[5][half, rows] = act.astype(low)
            refs[6][half, rows] = slope.astype(low)
        elif kind == "slope":
            refs[6][half, rows] = (product * refs[5][half, rows].astype(full)).astype(low)
        else:
            refs[5][half, rows] = product.astype(low)


def both_times(chain, kind, own, other, weight, slope=None, waits=()):
    depth = weight.shape[0]
    rows = 2 * ROW_TILE
    width = weight.shape[1]
    tile = 512
    out_spec = pl.BlockSpec((2, rows, tile), lambda j, info: (0, 0, j))
    extra = [] if slope is None else [slope]
    count = 2 if kind == "gelu" else 1
    return chain.run(
        "both_" + kind,
        lambda *refs: both_kernel(*refs, kind=kind),
        [*own, *other, weight] + extra,
        [whole_once(part) for part in (*own, *other)]
        + [pl.BlockSpec((depth, tile), lambda j, info: (0, j))]
        + [out_spec] * len(extra),
        [shape_of((2, rows, width))] * count,
        [out_spec] * count,
        grid=(width // tile,),
        waits=waits,
    )


def times_back(values, weight):
    return lax.dot_general(
        values, weight, (((1,), (1,)), ((), ())), preferred_element_type=full
    ).astype(low)


def other_rows(chain, values, weight):
    rows, depth = values.shape[1:]
    width = weight.shape[0]
    tile = 512

    def kernel(info, rows_in, weight_in, first, second):
        result = times_back(rows_in[0], weight_in[...])
        first[...] = result[:ROW_TILE]
        second[...] = result[ROW_TILE:]

    half = pl.BlockSpec((ROW_TILE, tile), lambda j, info: (0, j))
    results = chain.run(
        "other_rows",
        kernel,
        [values, weight],
        [
            pl.BlockSpec(
                (1, rows, depth), lambda j, info: (1, 0, 0), pipeline_mode=pl.Buffered(1)
            ),
            pl.BlockSpec((tile, depth), lambda j, info: (j, 0)),
        ],
        [shape_of((ROW_TILE, width))] * 2,
        [half] * 2,
        grid=(width // tile,),
    )
    return flip_rows(results)


def put_half(pair, values):
    @pl.when(pl.program_id(0) == 0)
    def _():
        pair[0][...] = values

    @pl.when(pl.program_id(0) == 1)
    def _():
        pair[1][...] = values


def get_half(pair):
    return jnp.where(pl.program_id(0) == 0, pair[0][...].astype(full), pair[1][...].astype(full))


def shown_rows(info):
    first = pl.program_id(0) * ROW_TILE
    row = first + lax.broadcasted_iota(jnp.int32, (ROW_TILE, 1), 0)
    return (row < info[3] * 128).astype(full)


def norm_and_move(values, shift, scale):
    center = values - jnp.mean(values, axis=-1, keepdims=True)
    spread = jnp.mean(center * center, axis=-1, keepdims=True)
    inverse = lax.rsqrt(spread + epsilon)
    normed = center * inverse
    return normed.astype(low), inverse, (normed * (1.0 + scale) + shift).astype(low)


def row_specs(model_width):
    tall = pl.BlockSpec((ROW_TILE, model_width), lambda i, info: (i, 0))
    thin = pl.BlockSpec((ROW_TILE, 1), lambda i, info: (i, 0))
    return tall, thin


def first_norm(chain, current, traded, rows_of):
    rows, model_width = current.shape
    tall, thin = row_specs(model_width)

    def kernel(info, ours, theirs, given, kept, normed, inverse, *moved):
        values = jnp.where(info[4] == 1, ours[...].astype(full), theirs[...].astype(full))
        kept[...] = values.astype(low)
        normed[...], inverse[...], result = norm_and_move(values, given[0:1], given[1:2])
        put_half(moved, result)

    half = shape_of((ROW_TILE, model_width))
    kept, normed, inverse, *moved = chain.run(
        "first_norm",
        kernel,
        [current, traded, rows_of],
        [tall, tall, whole_once(rows_of)],
        [shape_of(current.shape)] * 2 + [shape_of((rows, 1), full), half, half],
        [tall, tall, thin, whole(half), whole(half)],
        grid=(rows // ROW_TILE,),
    )
    return kept, normed, inverse, moved


def forward_step(chain, values, weight, away, current, rows_of, last, waits=()):
    rows, model_width = current.shape
    depth = values.shape[2]
    tall, thin = row_specs(model_width)

    def kernel(info, own, weight_in, first, second, current_in, given, after, branch_out, *rest):
        branch = times_back(own[0], weight_in[...]).astype(full) + get_half((first, second))
        total = current_in[...].astype(full) + shown_rows(info) * given[0:1] * branch
        after[...] = total.astype(after.dtype)
        branch_out[...] = branch.astype(low)
        if not last:
            normed, inverse, *moved = rest
            normed[...], inverse[...], result = norm_and_move(total, given[1:2], given[2:3])
            put_half(moved, result)

    outs = [shape_of(current.shape, low if last else full), shape_of(current.shape)]
    specs = [tall, tall]
    if not last:
        half = shape_of((ROW_TILE, model_width))
        outs += [shape_of(current.shape), shape_of((rows, 1), full), half, half]
        specs += [tall, thin, whole(half), whole(half)]
    results = chain.run(
        "forward_step",
        kernel,
        [values, weight, *away, current, rows_of],
        [
            pl.BlockSpec((1, ROW_TILE, depth), lambda i, info: (0, i, 0)),
            whole_once(weight),
            whole_once(away[0]),
            whole_once(away[1]),
            tall,
            whole_once(rows_of),
        ],
        outs,
        specs,
        grid=(rows // ROW_TILE,),
        waits=waits,
    )
    return results if last else (*results[:4], results[4:])


def add_rows(out, at, values):
    total = jnp.sum(values, axis=0, keepdims=True)

    @pl.when(pl.program_id(0) == 0)
    def _():
        out[at : at + 1] = total

    @pl.when(pl.program_id(0) > 0)
    def _():
        out[at : at + 1] += total


def first_back(chain, state, branch, gate):
    rows, model_width = state.shape
    tall, _ = row_specs(model_width)

    def kernel(info, state_in, branch_in, gate_in, first, second, sums):
        values = state_in[...].astype(full) * shown_rows(info)
        put_half((first, second), (values * gate_in[...]).astype(low))
        add_rows(sums, 0, values * branch_in[...].astype(full))

    sums = shape_of((8, model_width), full)
    half = shape_of((ROW_TILE, model_width))
    first, second, sums = chain.run(
        "first_back",
        kernel,
        [state, branch, gate],
        [tall, tall, whole_once(gate)],
        [half, half, sums],
        [whole(half), whole(half), whole(sums)],
        grid=(rows // ROW_TILE,),
    )
    return (first, second), sums


def backward_step(chain, values, weight, away, normed, inverse, state, rows_of, branch):
    rows, model_width = state.shape
    depth = values.shape[2]
    tall, thin = row_specs(model_width)
    last = branch is None

    def kernel(
        info, own, weight_in, first, second, normed_in, inverse_in, state_in, given, *rest
    ):
        grad = times_back(own[0], weight_in[...]).astype(full) + get_half((first, second))
        normal = normed_in[...].astype(full)
        moved = grad * (1.0 + given[0:1])
        first_mean = jnp.mean(moved, axis=-1, keepdims=True)
        second_mean = jnp.mean(moved * normal, axis=-1, keepdims=True)
        total = state_in[...].astype(full) + inverse_in[...] * (
            moved - first_mean - normal * second_mean
        )
        if last:
            state_out, sums = rest
        else:
            branch_in, state_out, sums, *sent = rest
        state_out[...] = total.astype(state_out.dtype)
        add_rows(sums, 0, grad)
        add_rows(sums, 1, grad * normal)
        if not last:
            shown = total * shown_rows(info)
            put_half(sent, (shown * given[1:2]).astype(low))
            add_rows(sums, 2, shown * branch_in[...].astype(full))

    sums = shape_of((8, model_width), full)
    outs = [shape_of(state.shape, low if last else full), sums]
    specs = [tall, whole(sums)]
    if not last:
        half = shape_of((ROW_TILE, model_width))
        outs += [half, half]
        specs += [whole(half)] * 2
    extra = [] if last else [branch]
    results = chain.run(
        "backward_step",
        kernel,
        [values, weight, *away, normed, inverse, state, rows_of] + extra,
        [
            pl.BlockSpec((1, ROW_TILE, depth), lambda i, info: (0, i, 0)),
            whole_once(weight),
            whole_once(away[0]),
            whole_once(away[1]),
            tall,
            thin,
            tall,
            whole_once(rows_of),
        ]
        + [tall] * len(extra),
        outs,
        specs,
        grid=(rows // ROW_TILE,),
    )
    return results if last else (*results[:2], results[2:])


def attend_kernel(info, blocks, joined, mixed, probs, bias, *, heads, cells, masked, sides):
    width = heads * HEAD_DIM

    @pl.when((pl.program_id(0) == 0) & (pl.program_id(1) == 0))
    def _():
        for h in range(heads):
            for place, spots in enumerate(sides):
                block = blocks[h, place]
                for row, col in spots:
                    bias[h, row * 64 : row * 64 + 64, col * 64 : col * 64 + 64] = block

    values = joined[...].reshape(cells, 3 * width)
    lead = mixed.shape
    if masked:
        column = lax.broadcasted_iota(jnp.int32, (1, cells), 1)
        shown = column < info[3] * (WIN_T * WIN_T)
    outs = []
    for h in range(heads):
        cols = slice(h * HEAD_DIM, (h + 1) * HEAD_DIM)
        query = values[:, cols]
        key = values[:, width + h * HEAD_DIM : width + (h + 1) * HEAD_DIM]
        value = values[:, 2 * width + h * HEAD_DIM : 2 * width + (h + 1) * HEAD_DIM]
        scores = lax.dot_general(
            query, key, (((1,), (1,)), ((), ())), preferred_element_type=full
        ) * HEAD_DIM ** (-0.5) + bias[h].astype(full)
        if masked:
            scores = jnp.where(shown, scores, masked_score)
        weights = jnp.exp(scores - jnp.max(scores, axis=-1, keepdims=True))
        share = (weights * (1.0 / jnp.sum(weights, axis=-1, keepdims=True))).astype(low)
        probs[0, h] = share
        outs.append(jnp.dot(share, value, preferred_element_type=full).astype(low))
    mixed[...] = jnp.concatenate(outs, axis=1).reshape(lead)


def attend_back_kernel(info, joined, grad, probs, back, bias_out, total, *, heads, cells, sides):
    step = pl.program_id(0) * pl.num_programs(1) + pl.program_id(1)
    width = heads * HEAD_DIM
    values = joined[...].reshape(cells, 3 * width)
    grads = grad[...].reshape(cells, width)
    grads_t = grads.astype(full).T.astype(low)
    queries_t = values[:, :width].astype(full).T.astype(low)
    queries, keys_t, values_t = [], [], []

    @pl.when(step == 0)
    def _():
        total[...] = jnp.zeros(total.shape, full)

    for h in range(heads):
        cols = slice(h * HEAD_DIM, (h + 1) * HEAD_DIM)
        key = values[:, width + h * HEAD_DIM : width + (h + 1) * HEAD_DIM]
        value = values[:, 2 * width + h * HEAD_DIM : 2 * width + (h + 1) * HEAD_DIM]
        share = probs[0, h]
        values_t.append(jnp.dot(grads_t[cols], share, preferred_element_type=full).astype(low))
        grad_share = lax.dot_general(
            grads[:, cols], value, (((1,), (1,)), ((), ())), preferred_element_type=full
        )
        share_full = share.astype(full)
        product = share_full * grad_share
        row_dot = jnp.sum(product, axis=-1, keepdims=True)
        grad_scores = (product - share_full * row_dot).astype(low)
        total[h] += grad_scores.astype(full)
        queries.append(
            (jnp.dot(grad_scores, key, preferred_element_type=full) * HEAD_DIM ** (-0.5)).astype(
                low
            )
        )
        keys_t.append(
            (
                jnp.dot(queries_t[cols], grad_scores, preferred_element_type=full)
                * HEAD_DIM ** (-0.5)
            ).astype(low)
        )
    key_grads = jnp.concatenate(keys_t, axis=0).astype(full).T.astype(low)
    value_grads = jnp.concatenate(values_t, axis=0).astype(full).T.astype(low)
    back[...] = jnp.concatenate(queries + [key_grads, value_grads], axis=1).reshape(back.shape)

    @pl.when(step == pl.num_programs(0) * pl.num_programs(1) - 1)
    def _():
        for h in range(heads):
            for place, spots in enumerate(sides):
                part = None
                for row, col in spots:
                    block = total[h, row * 64 : row * 64 + 64, :][:, col * 64 : col * 64 + 64]
                    part = block if part is None else part + block
                bias_out[h, place] = part


def spatial_sides():
    sides = [[] for _ in range(9)]
    for row in range(4):
        for col in range(4):
            place = (row // 2 - col // 2 + 1) * 3 + (row % 2 - col % 2 + 1)
            sides[place].append((row, col))
    return sides


def joint_sides():
    sides = [[] for _ in range(2 * FRAMES - 1)]
    for row in range(FRAMES):
        for col in range(FRAMES):
            sides[row - col + FRAMES - 1].append((row, col))
    return sides


def window_specs(is_joint, frames, width):
    if is_joint:
        shape, at = (1, frames, 1, 64, width), lambda i, j, info: (i, 0, j, 0, 0)
    else:
        shape, at = (2, 1, 2, 64, width), lambda i, j, info: (0, j, 0, 0, 0)
    return pl.BlockSpec(shape, at)


def attend(chain, blocks, joined, is_joint):
    frames = joined.shape[1]
    heads = blocks.shape[0]
    width = heads * HEAD_DIM
    grid = (2, 2) if is_joint else (1, frames)
    cells = 64 * frames if is_joint else 256
    number = grid[0] * grid[1]
    sides = joint_sides() if is_joint else spatial_sides()
    fetch = lambda i, j, info: (i * grid[1] + j, 0, 0, 0)
    return chain.run(
        "attend_joint" if is_joint else "attend_spatial",
        lambda *refs: attend_kernel(
            *refs, heads=heads, cells=cells, masked=is_joint, sides=sides
        ),
        [blocks, joined],
        [whole_once(blocks), window_specs(is_joint, frames, 3 * width)],
        [shape_of(joined.shape[:4] + (width,)), shape_of((number, heads, cells, cells))],
        [window_specs(is_joint, frames, width), pl.BlockSpec((1, heads, cells, cells), fetch)],
        grid=grid,
        scratch=[pltpu.VMEM((heads, cells, cells), low)],
    )


def attend_back(chain, joined, grad, probs, is_joint):
    frames = joined.shape[1]
    number, heads, cells, _ = probs.shape
    width = heads * HEAD_DIM
    grid = (2, 2) if is_joint else (1, frames)
    sides = joint_sides() if is_joint else spatial_sides()
    fetch = lambda i, j, info: (i * grid[1] + j, 0, 0, 0)
    sums = shape_of((heads, 9, 64, 64), full)
    return chain.run(
        "attend_back_joint" if is_joint else "attend_back_spatial",
        lambda *refs: attend_back_kernel(*refs, heads=heads, cells=cells, sides=sides),
        [joined, grad, probs],
        [
            window_specs(is_joint, frames, 3 * width),
            window_specs(is_joint, frames, width),
            pl.BlockSpec((1, heads, cells, cells), fetch),
        ],
        [shape_of(joined.shape), sums],
        [window_specs(is_joint, frames, 3 * width), whole(sums)],
        grid=grid,
        scratch=[pltpu.VMEM((heads, cells, cells), full)],
        extra=5,
    )


def offset_hot():
    places = np.arange(WIN_T * WIN_T)
    rows = places[:, None] // WIN_T - places[None, :] // WIN_T + WIN_T - 1
    cols = places[:, None] % WIN_T - places[None, :] % WIN_T + WIN_T - 1
    spots = (rows * (2 * WIN_T - 1) + cols).reshape(-1).astype(np.int32)
    return jnp.arange((2 * WIN_T - 1) ** 2, dtype=jnp.int32)[:, None] == jnp.asarray(spots)[None]


def fast_local(
    latents,
    cotangent,
    frame_counts,
    band_ids,
    class_ids,
    time_table,
    class_table,
    ada_weight,
    ada_bias,
    qkv_weight,
    out_weight,
    up_weight,
    down_weight,
    spatial_bias,
    joint_bias,
):
    frames = latents.shape[1]
    model_width = latents.shape[4]
    heads = spatial_bias.shape[0]
    width = heads * HEAD_DIM
    hidden = up_weight.shape[2]
    col_width = ada_weight.shape[2]
    rows = frames * 128
    z, y, c, x = (lax.axis_index(name) for name in ("z", "y", "c", "x"))
    counts = frame_counts.astype(full)
    count = jnp.where(c == x, counts, flip(counts, "c")).astype(jnp.int32)
    same = (c == x).astype(jnp.int32)
    chain = Chain(
        jnp.concatenate([jnp.stack([z, y, x]).astype(jnp.int32), count, same.reshape(1)])
    )

    def rearranged(values):
        shaped = values.reshape(frames, 8, 2, 8, model_width).transpose(0, 2, 1, 3, 4)
        return shaped.reshape(rows, model_width)

    qkv_rows = qkv_weight.reshape(2, -1, 3 * width)
    out_rows = out_weight.transpose(0, 2, 1)
    down_rows = down_weight.transpose(0, 2, 1)
    first_shard = swap(jnp.concatenate([qkv_rows[0], out_rows[0]], axis=1))
    band_hot = (band_ids[:, None] == jnp.arange(BANDS)[None, :]).astype(low)
    class_hot = (class_ids[:, None] == jnp.arange(CLASSES)[None, :]).astype(low)
    condition = jnp.dot(band_hot, time_table, preferred_element_type=full) + jnp.dot(
        class_hot, class_table, preferred_element_type=full
    )
    activity = jax.nn.silu(condition).astype(low)
    everyone = ("z", "y", "c", "x")
    mod_part = jnp.einsum(
        "cd,bde->cbe", activity, ada_weight, preferred_element_type=full
    ) + ada_bias[None].astype(full)
    mod_part = jnp.broadcast_to(
        mod_part.reshape(8, 1, 2, 2, col_width), (8, 2, 2, 2, col_width)
    ).reshape(32, 2, col_width)
    own_mod = lax.all_to_all(mod_part, everyone, split_axis=0, concat_axis=0, tiled=True)
    own_mod = own_mod.transpose(1, 0, 2).reshape(2, 6, model_width)
    rows_of = lambda *items: jnp.stack([own_mod[k, at] for k, at in items])

    hot = offset_hot()
    wide = 2 * WIN_T - 1
    square = spatial_bias.reshape(heads, 2 * WIN_S - 1, 2 * WIN_S - 1)
    spatial_parts = jnp.stack(
        [
            square[:, 8 * a : 8 * a + wide, 8 * b : 8 * b + wide].reshape(heads, -1)
            for a in range(3)
            for b in range(3)
        ],
        axis=1,
    )
    parts = swap(jnp.concatenate([spatial_parts, joint_bias.reshape(heads, 9, -1)]))
    blocks = jnp.dot(
        parts.reshape(heads * 18, wide * wide), hot.astype(low), preferred_element_type=full
    ).astype(low)
    blocks = blocks.reshape(2, heads, 9, 64, 64)
    near = blocks[0].reshape(heads, 3, 3, 64, 64)
    near = jnp.where(c == 0, near, near[:, ::-1])
    bias_blocks = [near.reshape(heads, 9, 64, 64), blocks[1]]

    windowed = lambda values: values.reshape(2, frames, 2, 64, values.shape[-1])

    chain.wait(own_mod, parts)
    packed = pack_arguments(chain, up_weight, down_rows, qkv_rows, out_rows)
    traded = swap_only(packed)
    gather = Gather(chain, [first_shard] + [None] * 5)
    gather.over_z(0)
    gather.step()
    cuts = [shape_of((64, PIECE))] * 5
    gather.shards[1:] = chain.run(
        "cut_shards",
        cut_kernel,
        [packed, traded],
        [whole(packed)] * 2,
        cuts,
        [whole(a) for a in cuts],
    )
    gather.over_z(1)
    latent_rows = copy_rows(chain, rearranged(latents))
    traded_rows = swap_only(latent_rows)
    gather.step()
    gather.over_z(2)
    chain.wait(*bias_blocks)
    latent_rows, normed_0, inverse_0, moved_0 = first_norm(
        chain, latent_rows, traded_rows, rows_of((0, 0), (0, 1))
    )
    other_0 = flip_rows(moved_0)
    gather.step()
    gather.over_z(3)
    qkv_0, out_0 = gather.place(0, [3 * width, width])
    (joined_0,) = both_times(chain, "plain", moved_0, other_0, qkv_0)
    joined_0 = windowed(joined_0)
    mixed_0, probs_0 = attend(chain, bias_blocks[0], joined_0, False)
    mixed_0 = mixed_0.reshape(2, rows, width)
    away = other_rows(chain, mixed_0, out_0)
    gather.step()
    gather.over_z(4)
    (up_0,) = gather.place(1, [hidden])
    after_0, branch_one_0, normed_1, inverse_1, moved_1 = forward_step(
        chain, mixed_0, out_0, away, latent_rows, rows_of((0, 2), (0, 3), (0, 4)), False
    )
    other_1 = flip_rows(moved_1)
    act_0, slope_0 = both_times(chain, "gelu", moved_1, other_1, up_0)
    gather.step()
    gather.over_z(5)
    (down_0,) = gather.place(2, [hidden])
    away = other_rows(chain, act_0, down_0)
    current_1, branch_two_0, normed_2, inverse_2, moved_2 = forward_step(
        chain, act_0, down_0, away, after_0, rows_of((0, 5), (1, 0), (1, 1)), False
    )
    other_2 = flip_rows(moved_2)

    gather.step()
    qkv_1, out_1 = gather.place(3, [3 * width, width])
    (joined_1,) = both_times(chain, "plain", moved_2, other_2, qkv_1)
    joined_1 = windowed(joined_1)
    mixed_1, probs_1 = attend(chain, bias_blocks[1], joined_1, True)
    mixed_1 = mixed_1.reshape(2, rows, width)
    away = other_rows(chain, mixed_1, out_1)
    gather.step()
    (up_1,) = gather.place(4, [hidden])
    after_1, branch_one_1, normed_3, inverse_3, moved_3 = forward_step(
        chain, mixed_1, out_1, away, current_1, rows_of((1, 2), (1, 3), (1, 4)), False
    )
    other_3 = flip_rows(moved_3)
    act_1, slope_1 = both_times(chain, "gelu", moved_3, other_3, up_1)
    (down_1,) = gather.place(5, [hidden])
    traded_cotangent = swap(copy_rows(chain, rearranged(cotangent)))
    away = other_rows(chain, act_1, down_1)
    final, branch_two_1 = forward_step(
        chain, act_1, down_1, away, after_1, rows_of((1, 5)), True
    )

    def restored(sent):
        shaped = sent.reshape(frames, 2, 8, 8, model_width).transpose(0, 2, 1, 3, 4)
        return shaped.astype(full).reshape(1, frames, 8, 16, model_width)

    traded_final = swap(final)

    exact = lax.Precision.HIGHEST

    state = traded_cotangent
    own_g, sums_a = first_back(chain, state, branch_two_1, rows_of((1, 5)))
    other_g = flip_rows(own_g)
    scatter = Scatter(chain)
    (hidden_g,) = both_times(chain, "slope", own_g, other_g, down_1, slope_1)
    away = other_rows(chain, hidden_g, up_1)
    scatter.weight_grad((own_g, other_g, act_1))
    state, sums_b, own_g = backward_step(
        chain, hidden_g, up_1, away, normed_3, inverse_3, state, rows_of((1, 4), (1, 2)), branch_one_1
    )
    other_g = flip_rows(own_g)
    scatter.weight_grad((moved_3, other_3, hidden_g))
    chain.wait(traded_final)
    scatter.step(6)
    (mixed_g,) = both_times(chain, "plain", own_g, other_g, out_1)
    back, joint_sums = attend_back(chain, joined_1, windowed(mixed_g), probs_1, True)
    back = back.reshape(2, rows, 3 * width)
    away = other_rows(chain, back, qkv_1)
    scatter.weight_grad((moved_2, other_2, back), (own_g, other_g, mixed_1))
    scatter.step(6)
    state, sums_c, own_g = backward_step(
        chain, back, qkv_1, away, normed_2, inverse_2, state, rows_of((1, 1), (0, 5)), branch_two_0
    )
    other_g = flip_rows(own_g)

    (hidden_g,) = both_times(chain, "slope", own_g, other_g, down_0, slope_0)
    away = other_rows(chain, hidden_g, up_0)
    scatter.weight_grad((own_g, other_g, act_0))
    scatter.step(6)
    state, sums_d, own_g = backward_step(
        chain, hidden_g, up_0, away, normed_1, inverse_1, state, rows_of((0, 4), (0, 2)), branch_one_0
    )
    other_g = flip_rows(own_g)
    scatter.weight_grad((moved_1, other_1, hidden_g))
    (mixed_g,) = both_times(chain, "plain", own_g, other_g, out_0)
    scatter.step(6)
    back, spatial_sums = attend_back(chain, joined_0, windowed(mixed_g), probs_0, False)
    back = back.reshape(2, rows, 3 * width)
    away = other_rows(chain, back, qkv_0)
    scatter.weight_grad((moved_0, other_0, back), (own_g, other_g, mixed_0))
    scatter.step(6)
    spatial_tables, joint_tables = bias_tables(chain, [spatial_sums, joint_sums])
    state, sums_e = backward_step(
        chain, back, qkv_0, away, normed_0, inverse_0, state, rows_of((0, 1)), None
    )
    output = restored(traded_final)

    chain.wait(*scatter.held[1:])
    grad_mod = collect_sums(chain, [sums_a, sums_b, sums_c, sums_d, sums_e])
    ordered = grad_mod.reshape(2, 32, col_width).transpose(1, 0, 2)
    cols = lax.all_to_all(ordered, everyone, split_axis=0, concat_axis=0, tiled=True)
    cols = cols.reshape(8, 2, 2, 2, col_width)
    cols = (cols[:, 0] + cols[:, 1]).reshape(16, 2, col_width)
    grad_ada_weight = jnp.einsum("cd,cbe->bde", activity.astype(full), cols, precision=exact)
    grad_ada_bias = jnp.sum(cols, axis=0)
    grad_activity = jnp.einsum("cbe,bde->cd", cols, ada_weight.astype(full), precision=exact)

    near = spatial_tables.reshape(heads, 3, 3, 256)
    near = jnp.where(c == 0, near, near[:, ::-1])
    tables = jnp.concatenate(
        [near.reshape(heads * 9, 256), joint_tables.reshape(heads * 9, 256)]
    )

    shared = jnp.concatenate([grad_activity.reshape(-1, 256), tables])
    chain.wait(cols)
    scatter.step(6)
    scatter.step(6)
    shared, sent = add_all(chain, shared)
    sent = flip(sent, "y")
    traded_state = swap(copy_rows(chain, state))
    (early,) = join_pieces(chain, scatter.done)
    early = swap(early)
    shared, sent = add_all(chain, shared, sent)
    sent = [z_trade(sent, k) for k in (1, 2, 3)]
    chain.wait(traded_state)
    scatter.step(6)
    traded_late = swap_only(scatter.done[5])
    late = jnp.where(c == x, scatter.done[5], traded_late).astype(full)
    chain.wait(early, traded_late)
    shared, sent = add_all(chain, shared, *sent)
    over_x = flip(sent, "x").astype(full)
    over_c = flip(sent, "c").astype(full)
    over_both = lax.ppermute(sent, ("c", "x"), [(0, 3), (1, 2), (2, 1), (3, 0)]).astype(full)
    shared = shared + over_x
    across = over_c + over_both
    grad_activity = (shared + across)[: -heads * 18].reshape(16, model_width)
    tables = jnp.where(c == x, shared[-heads * 18 :], across[-heads * 18 :])
    grad_latents = restored(traded_state)
    done = early.astype(full)
    piece = lambda at: done[:, at * PIECE : (at + 1) * PIECE]
    grad_down = jnp.stack([piece(3).T, piece(0).T])
    grad_up = jnp.stack([piece(4), piece(1)])
    grad_qkv = jnp.stack([late[:, : 3 * width], piece(2)[:, : 3 * width]])
    grad_out = jnp.stack([late[:, 3 * width :].T, piece(2)[:, 3 * width :].T])

    tables = tables.reshape(2, heads, 9, 16, 16)[..., :wide, :wide]
    grad_joint = tables[1].reshape(heads, 9 * wide * wide)
    near = tables[0].reshape(heads, 3, 3, wide, wide)
    long = 2 * WIN_S - 1
    grad_spatial = 0.0
    for a in range(3):
        for b in range(3):
            grad_spatial = grad_spatial + jnp.pad(
                near[:, a, b],
                ((0, 0), (8 * a, long - wide - 8 * a), (8 * b, long - wide - 8 * b)),
            )
    grad_spatial = grad_spatial.reshape(heads, long * long)
    grad_condition = jax.vjp(jax.nn.silu, condition)[1](grad_activity)[0]
    grad_time = jnp.dot(band_hot.astype(full).T, grad_condition, precision=exact)
    grad_class = jnp.dot(class_hot.astype(full).T, grad_condition, precision=exact)

    return (
        output,
        grad_latents,
        grad_time,
        grad_class,
        grad_ada_weight,
        grad_ada_bias,
        grad_qkv.reshape(2, -1, 3, width),
        grad_out,
        grad_up,
        grad_down,
        grad_spatial,
        grad_joint,
    )


def solution(mesh):
    if mesh.shape["dp"] != 16 or mesh.shape["mp"] != 2:
        return solution_any(mesh)
    fine = Mesh(mesh.devices.reshape(4, 2, 2, 2), ("z", "y", "c", "x"))
    dp, mp = ("z", "y", "c"), "x"
    both = dp + (mp,)
    tokens = P(dp, None, mp, None, None)
    weight_specs = (
        P(None, None, both),
        P(None, both),
        P(None, dp, None, mp),
        P(None, mp, dp),
        P(None, dp, mp),
        P(None, mp, dp),
        P(mp, None),
        P(mp, None),
    )
    return jax.shard_map(
        fast_local,
        mesh=fine,
        in_specs=(tokens, tokens, P(dp), P(), P(), P(), P()) + weight_specs,
        out_specs=(tokens, tokens, P(), P()) + weight_specs,
        check_vma=False,
    )
```
